32 devices in a mesh: rows: 16 (over z, y, core), cols: 2 (over x).
Axes of the slice: x: 2, y: 2, z: 4, core: 2. Of those that a mesh axis runs over, the one named last changes fastest.
Arguments:
- sens_base: bfloat16 [131072, 1024], P('rows', 'cols'), may hold values from -0.09564563 to 0.09564563
- design_field: float32 [128, 1024], P('rows'), may hold values from -3 to 3
- gradient: bfloat16 [128, 1024], P('rows'), may hold values from -6 to 6
- tile_index: int32 [1024], P('cols'), may hold values from 0 to 7
- type_codes: int32 [1024], P('cols'), may hold values from 0 to 2
Outputs:
- r_panels: float32 [512, 1024], P(None, 'cols')
- multipliers: float32 [512], replicated
The draws below stay inside these ranges and needn't reach their ends.
Inputs may be any that keep to these rules, and one draw needn't show every extreme that they name: `tile_index`: each constraint names one support tile.
All inputs are finite; a program needn't handle non-finite values.
Results may differ from the reference program's by a relative error of at most 0.0003.
The reference program's roundings to bfloat16 on the way (of `jacobian_t`) count: a program that leaves them out, or rounds other values in their place, can miss the bound.
Values may be sent and summed in bfloat16 or wider, within the bound.
No kernel may reach another device: no remote copies, remote signals or barrier semaphores. Data moves between devices by JAX's collectives and lax.ppermute only.
A program may use at most 64 MiB of HBM per device.

```python
import math
import jax
import jax.numpy as jnp
from jax import lax

GX = 1024
TILE = 128
NC = 1024
KF = 512
GY = 128
NV = 131072
NT = 8
N_ROWS = 16
N_COLS = 2


def draw_sens_base(key, part):
    keys = jax.random.split(jax.random.fold_in(key, 7), 6)
    devices_all = N_ROWS * N_COLS
    block_cells = NV // devices_all
    noise = jnp.clip(jax.random.normal(keys[0], (NV, NC), jnp.float32), -4.0, 4.0)
    owner = jax.random.randint(keys[1], (NC,), 0, devices_all)
    cell_ids = jnp.arange(NV, dtype=jnp.int32)
    block_of = cell_ids // block_cells
    boost = jnp.where(block_of[:, None] == owner[None, :], float(devices_all) ** 0.5, 1.0)
    reach = (NC / 8.0) ** 0.5
    freq_rows = jax.random.uniform(keys[2], (NC,), jnp.float32, 0.0, reach)
    freq_cols = jax.random.uniform(keys[3], (NC,), jnp.float32, -reach, reach)
    shift = jax.random.uniform(keys[4], (NC,), jnp.float32, -math.pi, math.pi)
    low_scale = 0.25
    high_scale = 4.0
    cell_scale = jnp.exp(jax.random.uniform(keys[5], (NV,), jnp.float32, math.log(low_scale), math.log(high_scale)))
    mean_square = (high_scale ** 2 - low_scale ** 2) / (2.0 * math.log(high_scale / low_scale))
    amp_norm = (2.0 / (NV * mean_square)) ** 0.5
    rows_at = (cell_ids // GX).astype(jnp.float32)
    cols_at = (cell_ids % GX).astype(jnp.float32)
    column_amp = jnp.ones((NC,), jnp.float32)
    phase = 2.0 * math.pi * (rows_at[:, None] * (freq_rows[None, :] / GY) + cols_at[:, None] * (freq_cols[None, :] / GX)) + shift[None, :]
    wave = (amp_norm * cell_scale)[:, None] * column_amp[None, :] * jnp.cos(phase)
    return (noise * boost / NV ** 0.5 + wave).astype(jnp.bfloat16)


def set_ends(result, key, smallest, largest):
    spot = [jax.random.randint(jax.random.fold_in(key, axis), (), 0, length) for axis, length in enumerate(result.shape)]
    widest = result.shape.index(max(result.shape))
    beside = spot[:widest] + [(spot[widest] + 1) % result.shape[widest]] + spot[widest + 1:]
    return result.at[tuple(spot)].set(smallest).at[tuple(beside)].set(largest)


def level_of(stream_key, extent, cuts, least, high):
    loudness, own = 1.0, jax.random.fold_in(stream_key, 6)
    for position, blocks in cuts:
        heights = jnp.exp(jax.random.uniform(jax.random.fold_in(own, position), (blocks,), jnp.float32, least / len(cuts), high / len(cuts)))
        loudness = loudness * jnp.repeat(heights, extent[position] // blocks).reshape([-1 if axis == position else 1 for axis in range(len(extent))])
    return loudness


def scatter_about(own_key, shape, width, bound, cuts=(), kind=jnp.bfloat16):
    drawn = width * jax.random.normal(own_key, shape, jnp.float32)
    if cuts:
        drawn = drawn * level_of(own_key, shape, cuts, -0.22, 0.18)
    return jnp.clip(drawn, -bound, bound).astype(kind)


def setup_inputs(seed: int = 0) -> dict:
    arg_keys = jax.random.split(jax.random.key(seed), 6)
    return {
        "sens_base": draw_sens_base(jax.random.fold_in(arg_keys[5], 71), 0),
        "design_field": scatter_about(arg_keys[1], (GY, GX), 0.5, 3.0, ((0, 16),), jnp.float32),
        "gradient": scatter_about(arg_keys[2], (GY, GX), 1.0, 6.0, ((0, 16),)),
        "tile_index": set_ends(jax.random.randint(arg_keys[3], (NC,), 0, NT), jax.random.fold_in(arg_keys[3], 1), 0, NT - 1).astype(jnp.int32),
        "type_codes": set_ends(jax.random.randint(arg_keys[4], (NC,), 0, 3), jax.random.fold_in(arg_keys[4], 1), 0, 2).astype(jnp.int32),
    }


def stencil_fields(design_field):
    padded = jnp.pad(design_field, 1)
    north_cells = padded[:-2, 1:-1]
    south_cells = padded[2:, 1:-1]
    west_cells = padded[1:-1, :-2]
    east_cells = padded[1:-1, 2:]
    laplace = 4.0 * design_field - (north_cells + south_cells + west_cells + east_cells)
    slope_x = 0.5 * (east_cells - west_cells)
    slope_y = 0.5 * (south_cells - north_cells)
    return jnp.stack([laplace, slope_x, slope_y]).reshape(3, -1)

def assemble(base_cols, tile_cols, type_cols, stencils, cell_tile):
    kinds_all = jnp.arange(3, dtype=jnp.int32)
    chooser = (type_cols[None, :] == kinds_all[:, None]).astype(jnp.float32)
    picked = lax.dot_general(stencils.astype(jnp.float32), chooser.astype(jnp.float32), (((0,), (0,)), ((), ())), precision=lax.Precision.HIGHEST, preferred_element_type=jnp.float32)
    inside = cell_tile[:, None] == tile_cols[None, :]
    total = base_cols.astype(jnp.float32) + jnp.where(inside, picked / TILE, 0.0)
    return total.astype(jnp.bfloat16)

def reference(sens_base, design_field, gradient, tile_index, type_codes):
    stencils = stencil_fields(design_field)
    row_ids = jnp.arange(GY, dtype=jnp.int32) // TILE
    col_ids = jnp.arange(GX, dtype=jnp.int32) // TILE
    cell_tile = (row_ids[:, None] * (GX // TILE) + col_ids[None, :]).reshape(-1).astype(jnp.int32)
    col_block = min(128, NC)
    pieces = []
    for index_block in range(NC // col_block):
        start = index_block * col_block
        pieces.append(assemble(sens_base[:, start:start + col_block], tile_index[start:start + col_block], type_codes[start:start + col_block], stencils, cell_tile))
    jacobian_t = jnp.concatenate(pieces, axis=1)
    leading = jacobian_t[:, :KF]
    gram_block = lax.dot_general(leading.astype(jnp.float32), jacobian_t.astype(jnp.float32), (((0,), (0,)), ((), ())), preferred_element_type=jnp.float32)
    projected = jnp.dot(gradient.reshape(-1).astype(jnp.float32), leading.astype(jnp.float32), preferred_element_type=jnp.float32)
    lower_chol = jnp.linalg.cholesky(gram_block[:, :KF])
    r_panels = jax.scipy.linalg.solve_triangular(lower_chol, gram_block, lower=True)
    half_solved = jax.scipy.linalg.solve_triangular(lower_chol, projected, lower=True)
    multipliers = jax.scipy.linalg.solve_triangular(lower_chol.T, half_solved, lower=False)
    return (r_panels, multipliers)
```

```python
import jax
import jax.numpy as jnp
from jax import lax
from jax.experimental import pallas as pl
from jax.experimental.pallas import tpu as pltpu
from jax.sharding import PartitionSpec as P

TILE = 128
PW = 256
BLOCK = 128
HIGHEST = lax.Precision.HIGHEST


def padded_2(cells, sides, width):
    for axis, dim in sides:
        count = lax.axis_size(axis)
        ends = count - 1
        head = lax.slice_in_dim(cells, 0, width, axis=dim)
        tail = lax.slice_in_dim(cells, cells.shape[dim] - width, cells.shape[dim], axis=dim)
        cells = jnp.concatenate(
            [
                lax.ppermute(tail, axis, [(i, (i + 1) % count) for i in range(ends)]),
                cells,
                lax.ppermute(head, axis, [((i + 1) % count, i) for i in range(ends)]),
            ],
            axis=dim,
        )
    return cells


def assemble(base_cols, tile_cols, type_cols, stencils, cell_tile):
    kinds_all = jnp.arange(3, dtype=jnp.int32)
    chooser = (type_cols[None, :] == kinds_all[:, None]).astype(jnp.float32)
    picked = lax.dot_general(
        stencils,
        chooser,
        (((0,), (0,)), ((), ())),
        precision=lax.Precision.HIGHEST,
        preferred_element_type=jnp.float32,
    )
    inside = cell_tile[:, None] == tile_cols[None, :]
    total = base_cols.astype(jnp.float32) + jnp.where(inside, picked / TILE, 0.0)
    return total.astype(jnp.bfloat16)


def matmul(left, right):
    return jnp.dot(left, right, precision=HIGHEST, preferred_element_type=jnp.float32)


def inverse_root(value):
    guess = lax.rsqrt(value)
    return guess * (1.5 - 0.5 * value * guess * guess)


def diagonal_inverse(block):
    groups = BLOCK // 8
    lanes = lax.broadcasted_iota(jnp.int32, (8, BLOCK), 1)
    subs = lax.broadcasted_iota(jnp.int32, (8, BLOCK), 0)
    parts = [block[8 * g : 8 * g + 8, :] for g in range(groups)]
    for j in range(BLOCK):
        own, sub = j // 8, j % 8
        here = lanes == j
        column = jnp.broadcast_to(parts[own][:, j : j + 1], (8, BLOCK))
        pivot = jnp.broadcast_to(column[sub : sub + 1, :], (8, BLOCK))
        row = jnp.broadcast_to(parts[own][sub : sub + 1, :], (8, BLOCK))
        row = jnp.where(here, 1.0, row) / pivot
        if sub < 7:
            below = subs > sub
            changed = jnp.where(here, 0.0, parts[own]) - column * row
            parts[own] = jnp.where(below, changed, parts[own])
        for g in range(own + 1, groups):
            column = jnp.broadcast_to(parts[g][:, j : j + 1], (8, BLOCK))
            parts[g] = jnp.where(here, 0.0, parts[g]) - column * row
    whole = []
    for g in range(groups):
        rows = subs + 8 * g
        pivots = jnp.sum(jnp.where(lanes == rows, parts[g], 0.0), axis=1, keepdims=True)
        unit = jnp.where(lanes == rows, 1.0, jnp.where(lanes < rows, parts[g], 0.0))
        whole.append(unit * inverse_root(pivots))
    return jnp.concatenate(whole, axis=0)


def factor_kernel(gram_ref, projected_ref, upper_ref, inverse_ref, multipliers_ref):
    order = gram_ref.shape[0]
    upper_ref[...] = gram_ref[...]
    rows = lax.broadcasted_iota(jnp.int32, (order, order), 0)
    cols = lax.broadcasted_iota(jnp.int32, (order, order), 1)
    inverse_ref[...] = jnp.where(rows == cols, 1.0, 0.0)

    @pl.loop(0, order // BLOCK)
    def _(step):
        start = pl.multiple_of(step * BLOCK, BLOCK)
        mine = pl.ds(start, BLOCK)
        small = diagonal_inverse(upper_ref[mine, mine])
        upper_ref[mine, :] = matmul(small, upper_ref[mine, :])
        inverse_ref[mine, :] = matmul(small, inverse_ref[mine, :])

        @pl.loop(step + 1, order // BLOCK)
        def _(later):
            theirs = pl.ds(pl.multiple_of(later * BLOCK, BLOCK), BLOCK)
            factor = upper_ref[mine, theirs]

            def minus(target):
                target[theirs, :] -= lax.dot_general(
                    factor,
                    target[mine, :],
                    (((0,), (0,)), ((), ())),
                    precision=HIGHEST,
                    preferred_element_type=jnp.float32,
                )

            minus(upper_ref)
            minus(inverse_ref)

    upper_ref[...] = jnp.where(rows <= cols, upper_ref[...], 0.0)
    half = jnp.sum(inverse_ref[...] * projected_ref[...], axis=1, keepdims=True)
    multipliers_ref[...] = jnp.sum(inverse_ref[...] * half, axis=0, keepdims=True)


def factor(gram, projected):
    order = gram.shape[0]
    return pl.pallas_call(
        factor_kernel,
        out_shape=(
            jax.ShapeDtypeStruct((order, order), jnp.float32),
            jax.ShapeDtypeStruct((order, order), jnp.float32),
            jax.ShapeDtypeStruct((1, order), jnp.float32),
        ),
        in_specs=[pl.BlockSpec(memory_space=pltpu.VMEM)] * 2,
        out_specs=[pl.BlockSpec(memory_space=pltpu.VMEM)] * 3,
        compiler_params=pltpu.CompilerParams(vmem_limit_bytes=32 * 2**20),
        cost_estimate=pl.CostEstimate(
            flops=6 * order**3, bytes_accessed=12 * order**2, transcendentals=0
        ),
    )(gram, projected)


def shards(sens_base, design_field, gradient, tile_index, type_codes):
    rows_here = design_field.shape[0]
    grid_width = design_field.shape[1]
    cols_here = sens_base.shape[1]
    factored = 2 * PW
    padded = padded_2(design_field, (("rows", 0),), 1)
    padded = jnp.pad(padded, ((0, 0), (1, 1)))
    north_cells = padded[:-2, 1:-1]
    south_cells = padded[2:, 1:-1]
    west_cells = padded[1:-1, :-2]
    east_cells = padded[1:-1, 2:]
    laplace = 4.0 * design_field - (north_cells + south_cells + west_cells + east_cells)
    slope_x = 0.5 * (east_cells - west_cells)
    slope_y = 0.5 * (south_cells - north_cells)
    stencils = jnp.stack([laplace, slope_x, slope_y]).reshape(3, -1)
    row_glob = lax.axis_index("rows") * rows_here + jnp.arange(rows_here, dtype=jnp.int32)
    col_ids = jnp.arange(grid_width, dtype=jnp.int32) // TILE
    cell_tile = ((row_glob // TILE)[:, None] * (grid_width // TILE) + col_ids[None, :]).reshape(-1)
    local_jac = assemble(sens_base, tile_index, type_codes, stencils, cell_tile)
    grad_flat = gradient.reshape(-1)
    row_major = lax.all_to_all(local_jac, "cols", split_axis=0, concat_axis=1, tiled=True)
    row_piece = row_major.shape[0]
    grad_part = lax.dynamic_slice_in_dim(
        grad_flat, lax.axis_index("cols") * row_piece, row_piece, 0
    )
    leading = row_major[:, :factored]
    gram_block = lax.dot_general(
        leading, row_major, (((0,), (0,)), ((), ())), preferred_element_type=jnp.float32
    )
    projected = jnp.dot(grad_part, leading, preferred_element_type=jnp.float32)
    gram_block, projected = lax.psum((gram_block, projected), ("rows", "cols"))
    gram_head = gram_block[:, :factored]
    gram_own = lax.dynamic_slice_in_dim(
        gram_block, lax.axis_index("cols") * cols_here, cols_here, 1
    )
    _, inverse, multipliers = factor(gram_head, projected[None, :])
    r_panels = matmul(inverse, gram_own)
    return (r_panels, multipliers[0])


def solution(mesh):
    placed = (P("rows", "cols"), P("rows", None), P("rows", None), P("cols"), P("cols"))
    return jax.shard_map(
        shards, mesh=mesh, in_specs=placed, out_specs=(P(None, "cols"), P()), check_vma=False
    )
```

```python
import jax
import jax.numpy as jnp
from jax import lax
from jax.experimental import pallas as pl
from jax.experimental.pallas import tpu as pltpu
from jax.sharding import PartitionSpec as P

TILE = 128
PW = 256
BLOCK = 128
FEATURES = 80
GROUP = 4
HIGHEST = lax.Precision.HIGHEST
VMEM = pl.BlockSpec(memory_space=pltpu.VMEM)
SMEM = pl.BlockSpec(memory_space=pltpu.SMEM)
LIMIT = 40 * 2**20
ANY = pl.BlockSpec(memory_space=pl.ANY)
STAGES = (2, 2)
BRIEF = pl.CostEstimate(flops=1000, bytes_accessed=1000, transcendentals=0)


def padded_2(cells, sides, width):
    for axis, dim in sides:
        count = lax.axis_size(axis)
        ends = count - 1
        head = lax.slice_in_dim(cells, 0, width, axis=dim)
        tail = lax.slice_in_dim(cells, cells.shape[dim] - width, cells.shape[dim], axis=dim)
        cells = jnp.concatenate(
            [
                lax.ppermute(tail, axis, [(i, (i + 1) % count) for i in range(ends)]),
                cells,
                lax.ppermute(head, axis, [((i + 1) % count, i) for i in range(ends)]),
            ],
            axis=dim,
        )
    return cells


def assemble(base_cols, tile_cols, type_cols, stencils, cell_tile):
    kinds_all = jnp.arange(3, dtype=jnp.int32)
    chooser = (type_cols[None, :] == kinds_all[:, None]).astype(jnp.float32)
    picked = lax.dot_general(
        stencils,
        chooser,
        (((0,), (0,)), ((), ())),
        precision=lax.Precision.HIGHEST,
        preferred_element_type=jnp.float32,
    )
    inside = cell_tile[:, None] == tile_cols[None, :]
    total = base_cols.astype(jnp.float32) + jnp.where(inside, picked / TILE, 0.0)
    return total.astype(jnp.bfloat16)


def matmul(left, right):
    return jnp.dot(left, right, precision=HIGHEST, preferred_element_type=jnp.float32)


def inverse_root(value):
    guess = lax.rsqrt(value)
    return guess * (1.5 - 0.5 * value * guess * guess)


def reciprocal(value):
    guess = pl.reciprocal(value, approx=True)
    guess = guess * (2.0 - value * guess)
    return guess * (2.0 - value * guess)


def lane(part, index):
    return jnp.broadcast_to(part[:, index : index + 1], part.shape)


def sublane(part, index):
    return jnp.broadcast_to(part[index : index + 1, :], part.shape)


def diagonal_inverse(block):
    groups = BLOCK // 8
    shape = (8, BLOCK)
    lanes = lax.broadcasted_iota(jnp.int32, shape, 1)
    subs = lax.broadcasted_iota(jnp.int32, shape, 0)
    parts = [block[8 * g : 8 * g + 8, :] for g in range(groups)]
    whole = []
    for p in range(groups):
        part, first = parts[p], 8 * p
        cols = [lane(part, first + k) for k in range(8)]
        inv = [None] * 8
        low = [jnp.zeros(shape, jnp.float32) for _ in range(8)]
        pivots = jnp.ones(shape, jnp.float32)
        for j in range(8):
            here = subs == j
            pivot = sublane(cols[j], j)
            ratio = reciprocal(pivot)
            pivots = jnp.where(here, pivot, pivots)
            for k in range(j):
                low[k] = jnp.where(here, inv[k], low[k])
            low[j] = jnp.where(here, 1.0, low[j])
            column = cols[j]
            for k in range(j + 1, 8):
                row = sublane(cols[k], j) * ratio
                cols[k] = jnp.where(here, row, cols[k] - column * row)
            for k in range(j):
                row = sublane(inv[k], j) * ratio
                inv[k] = jnp.where(here, row, inv[k] - column * row)
            inv[j] = jnp.where(here, ratio, -column * ratio)
        scale = inverse_root(pivots)
        inside = (lanes >= first) & (lanes < first + 8)
        unit = jnp.where(lanes - first == subs, 1.0, 0.0)
        rows = jnp.where(inside, unit, part)
        spread = [sublane(rows, k) for k in range(8)]
        solved = sum(low[k] * spread[k] for k in range(8)) * scale
        whole.append(jnp.where(lanes < first + 8, solved, 0.0))
        if p + 1 < groups:
            step = sum(inv[k] * spread[k] for k in range(8))
            step = [sublane(step, k) for k in range(8)]
            for g in range(p + 1, groups):
                taken = sum(lane(parts[g], first + k) * step[k] for k in range(8))
                parts[g] = jnp.where(inside, 0.0, parts[g]) - taken
    return jnp.concatenate(whole, axis=0)


def factor_kernel(gram_ref, projected_ref, upper_ref, inverse_ref, multipliers_ref):
    order = gram_ref.shape[0]
    upper_ref[...] = gram_ref[...]
    rows = lax.broadcasted_iota(jnp.int32, (order, order), 0)
    cols = lax.broadcasted_iota(jnp.int32, (order, order), 1)
    inverse_ref[...] = jnp.where(rows == cols, 1.0, 0.0)

    @pl.loop(0, order // BLOCK)
    def _(step):
        start = pl.multiple_of(step * BLOCK, BLOCK)
        mine = pl.ds(start, BLOCK)
        small = diagonal_inverse(upper_ref[mine, mine])
        upper_ref[mine, :] = matmul(small, upper_ref[mine, :])
        inverse_ref[mine, :] = matmul(small, inverse_ref[mine, :])

        @pl.loop(step + 1, order // BLOCK)
        def _(later):
            theirs = pl.ds(pl.multiple_of(later * BLOCK, BLOCK), BLOCK)
            factor = upper_ref[mine, theirs]

            def minus(target):
                target[theirs, :] -= lax.dot_general(
                    factor,
                    target[mine, :],
                    (((0,), (0,)), ((), ())),
                    precision=HIGHEST,
                    preferred_element_type=jnp.float32,
                )

            minus(upper_ref)
            minus(inverse_ref)

    upper_ref[...] = jnp.where(rows <= cols, upper_ref[...], 0.0)
    half = jnp.sum(inverse_ref[...] * projected_ref[...], axis=1, keepdims=True)
    multipliers_ref[...] = jnp.sum(inverse_ref[...] * half, axis=0, keepdims=True)


def factor(gram, projected):
    order = gram.shape[0]
    return pl.pallas_call(
        factor_kernel,
        out_shape=(
            jax.ShapeDtypeStruct((order, order), jnp.float32),
            jax.ShapeDtypeStruct((order, order), jnp.float32),
            jax.ShapeDtypeStruct((1, order), jnp.float32),
        ),
        in_specs=[pl.BlockSpec(memory_space=pltpu.VMEM)] * 2,
        out_specs=[pl.BlockSpec(memory_space=pltpu.VMEM)] * 3,
        compiler_params=pltpu.CompilerParams(vmem_limit_bytes=32 * 2**20),
        cost_estimate=pl.CostEstimate(
            flops=6 * order**3, bytes_accessed=12 * order**2, transcendentals=0
        ),
    )(gram, projected)


def features_kernel(field_ref, north_ref, south_ref, out_ref):
    field = field_ref[...]
    rows, width = field.shape
    lanes = lax.broadcasted_iota(jnp.int32, field.shape, 1)
    north = jnp.concatenate([north_ref[...], field[:-1]], axis=0)
    south = jnp.concatenate([field[1:], south_ref[...]], axis=0)
    west = jnp.where(lanes == 0, 0.0, pltpu.roll(field, 1, 1))
    east = jnp.where(lanes == width - 1, 0.0, pltpu.roll(field, width - 1, 1))
    laplace = 4.0 * field - (north + south + west + east)
    slope_x = 0.5 * (east - west)
    slope_y = 0.5 * (south - north)
    parts = []
    for stencil in (laplace, slope_x, slope_y):
        rest = stencil / TILE
        for _ in range(3):
            part = rest.astype(jnp.bfloat16).astype(jnp.float32)
            parts.append(part)
            rest = rest - part
    tiles = width // TILE
    shape = (FEATURES, width)
    owner = lax.broadcasted_iota(jnp.int32, shape, 0) // len(parts)
    tile = lax.broadcasted_iota(jnp.int32, shape, 1) // TILE
    blank = jnp.zeros((FEATURES - tiles * len(parts), width), jnp.float32)
    for row in range(rows):
        block = jnp.concatenate([part[row : row + 1] for part in parts], axis=0)
        whole = jnp.concatenate([block] * tiles + [blank], axis=0)
        out_ref[row] = jnp.where(owner == tile, whole, 0.0).astype(jnp.bfloat16)


def features(field, north, south):
    rows, width = field.shape
    return pl.pallas_call(
        features_kernel,
        out_shape=jax.ShapeDtypeStruct((rows, FEATURES, width), jnp.bfloat16),
        in_specs=[VMEM] * 3,
        out_specs=VMEM,
        compiler_params=pltpu.CompilerParams(vmem_limit_bytes=LIMIT),
        cost_estimate=BRIEF,
    )(field, north, south)


def assembled(base, feature, key):
    rows = lax.broadcasted_iota(jnp.int32, (FEATURES, key.shape[1]), 0) // 3
    chooser = jnp.where(rows == key, 1.0, 0.0).astype(jnp.bfloat16)
    added = lax.dot_general(
        feature, chooser, (((0,), (0,)), ((), ())), preferred_element_type=jnp.float32
    )
    return (base.astype(jnp.float32) + added).astype(jnp.bfloat16)


def transposed_dot(left, right):
    return lax.dot_general(
        left, right, (((0,), (0,)), ((), ())), preferred_element_type=jnp.float32
    )


def upper_blocks(order):
    count = order // BLOCK
    return [(a, b) for a in range(count) for b in range(a, count)]


def packed_rows(order):
    used = len(upper_blocks(order)) * BLOCK + order // BLOCK
    return -(-used // (8 * GROUP)) * 8 * GROUP


def own_kernel(base_ref, feature_ref, key_ref, grad_ref, jac_ref, packed_ref, gram, projected):
    step = pl.program_id(0)
    order = base_ref.shape[1]
    jac = assembled(base_ref[...], feature_ref[0], key_ref[...])
    jac_ref[...] = jac

    @pl.when(step == 0)
    def _():
        gram[...] = jnp.zeros_like(gram)
        projected[...] = jnp.zeros_like(projected)

    gram[...] += transposed_dot(jac, jac)
    projected[...] += jnp.dot(grad_ref[0], jac, preferred_element_type=jnp.float32)

    @pl.when(step == pl.num_programs(0) - 1)
    def _():
        packed_ref[...] = jnp.zeros_like(packed_ref)
        blocks = upper_blocks(order)
        for index, (a, b) in enumerate(blocks):
            packed_ref[pl.ds(index * BLOCK, BLOCK), :] = gram[
                pl.ds(a * BLOCK, BLOCK), pl.ds(b * BLOCK, BLOCK)
            ]
        for c in range(order // BLOCK):
            packed_ref[pl.ds(len(blocks) * BLOCK + c, 1), :] = projected[
                :, pl.ds(c * BLOCK, BLOCK)
            ]


def own_part(base, feature, key, gradient):
    cells, order = base.shape
    rows, width = gradient.shape
    return pl.pallas_call(
        own_kernel,
        grid=(rows,),
        out_shape=(
            jax.ShapeDtypeStruct((cells, order), jnp.bfloat16),
            jax.ShapeDtypeStruct((packed_rows(order), BLOCK), jnp.float32),
        ),
        in_specs=[
            pl.BlockSpec((width, order), lambda i: (i, 0)),
            pl.BlockSpec((1, FEATURES, width), lambda i: (i, 0, 0)),
            pl.BlockSpec((1, order), lambda i: (0, 0)),
            pl.BlockSpec((1, 1, width), lambda i: (i, 0, 0)),
        ],
        out_specs=(
            pl.BlockSpec((width, order), lambda i: (i, 0)),
            pl.BlockSpec((packed_rows(order), BLOCK), lambda i: (0, 0)),
        ),
        scratch_shapes=[
            pltpu.VMEM((order, order), jnp.float32),
            pltpu.VMEM((1, order), jnp.float32),
        ],
        compiler_params=pltpu.CompilerParams(vmem_limit_bytes=LIMIT),
        cost_estimate=BRIEF,
    )(base, feature, key, gradient.reshape(rows, 1, width))


def cross_kernel(side_ref, recv_ref, jac_ref, feature_ref, key_ref, _, out_ref, total):
    step = pl.program_id(0)
    other = assembled(recv_ref[...], feature_ref[0], key_ref[...])

    @pl.when(step == 0)
    def _():
        total[...] = jnp.zeros_like(total)

    total[...] += transposed_dot(other, jac_ref[...])
    count = total.shape[1] // BLOCK
    part = BLOCK // GROUP
    last = step == pl.num_programs(0) - 1

    blocks = total.shape[0] // BLOCK

    @pl.when(last & (side_ref[0] == 0))
    def _():
        for k in range(blocks):
            for q in range(GROUP):
                for c in range(count):
                    out_ref[q, pl.ds(BLOCK * k + part * c, part), :] = total[
                        pl.ds(BLOCK * k + part * q, part), pl.ds(BLOCK * c, BLOCK)
                    ]

    @pl.when(last & (side_ref[0] != 0))
    def _():
        for k in range(blocks):
            for c in range(count):
                block = total[pl.ds(BLOCK * k, BLOCK), pl.ds(BLOCK * c, BLOCK)].T
                for q in range(GROUP):
                    out_ref[q, pl.ds(BLOCK * k + part * c, part), :] = block[
                        part * q : part * q + part
                    ]


def cross_part(side, recv, jac, feature, key, after):
    cells, width_recv = recv.shape
    order = jac.shape[1]
    rows, _, width = feature.shape
    steps = rows // 2
    return pl.pallas_call(
        cross_kernel,
        grid_spec=pltpu.PrefetchScalarGridSpec(
            num_scalar_prefetch=1,
            grid=(steps,),
            in_specs=[
                pl.BlockSpec((width, width_recv), lambda i, s: (i, 0)),
                pl.BlockSpec((width, order), lambda i, s: (s[0] * steps + i, 0)),
                pl.BlockSpec((1, FEATURES, width), lambda i, s: (s[0] * steps + i, 0, 0)),
                pl.BlockSpec((1, width_recv), lambda i, s: (0, 0)),
                ANY,
            ],
            out_specs=pl.BlockSpec((GROUP, width_recv, BLOCK), lambda i, s: (0, 0, 0)),
            scratch_shapes=[pltpu.VMEM((width_recv, order), jnp.float32)],
        ),
        out_shape=jax.ShapeDtypeStruct((GROUP, width_recv, BLOCK), jnp.float32),
        compiler_params=pltpu.CompilerParams(vmem_limit_bytes=LIMIT),
        cost_estimate=BRIEF,
    )(side, recv, jac, feature, key, after)


def swap(value, axis, mask):
    count = lax.axis_size(axis)
    return lax.ppermute(value, axis, [(i, i ^ mask) for i in range(count)])


def group_sum(parts):
    own = lax.axis_index("rows") % GROUP
    held = lax.dynamic_index_in_dim(parts, own, 0, keepdims=False)
    got = [
        swap(lax.dynamic_index_in_dim(parts, own ^ mask, 0, keepdims=False), "rows", mask)
        for mask in range(1, GROUP)
    ]
    return held + got[0] + got[1] + got[2]


def groups_sum(held):
    masks = range(GROUP, lax.axis_size("rows"), GROUP)
    return held + sum(swap(held, "rows", mask) for mask in masks)


def rows_gather(own):
    return [own] + [swap(own, "rows", mask) for mask in range(1, GROUP)]


def unpack_factor_kernel(quarter_ref, *refs):
    pieces = refs[:GROUP]
    upper_ref, inverse_ref, multipliers_ref, whole, gram, projected = refs[GROUP + 1 :]
    size = pieces[0].shape[0]
    for mask in range(GROUP):
        start = pl.multiple_of((quarter_ref[0] ^ mask) * size, 8)
        whole[pl.ds(start, size), :] = pieces[mask][...]
    order = gram.shape[0]
    blocks = upper_blocks(order)
    for index, (a, b) in enumerate(blocks):
        gram[pl.ds(a * BLOCK, BLOCK), pl.ds(b * BLOCK, BLOCK)] = whole[
            pl.ds(index * BLOCK, BLOCK), :
        ]
        if a < b:
            gram[pl.ds(b * BLOCK, BLOCK), pl.ds(a * BLOCK, BLOCK)] = jnp.zeros(
                (BLOCK, BLOCK), jnp.float32
            )
    for c in range(order // BLOCK):
        projected[:, pl.ds(c * BLOCK, BLOCK)] = whole[pl.ds(len(blocks) * BLOCK + c, 1), :]
    factor_kernel(gram, projected, upper_ref, inverse_ref, multipliers_ref)


def unpack_factor(quarter, pieces, order, after):
    return pl.pallas_call(
        unpack_factor_kernel,
        out_shape=(
            jax.ShapeDtypeStruct((order, order), jnp.float32),
            jax.ShapeDtypeStruct((order, order), jnp.float32),
            jax.ShapeDtypeStruct((1, order), jnp.float32),
        ),
        in_specs=[SMEM] + [VMEM] * GROUP + [ANY],
        out_specs=[VMEM] * 3,
        scratch_shapes=[
            pltpu.VMEM((packed_rows(order), BLOCK), jnp.float32),
            pltpu.VMEM((order, order), jnp.float32),
            pltpu.VMEM((1, order), jnp.float32),
        ],
        compiler_params=pltpu.CompilerParams(vmem_limit_bytes=LIMIT),
        cost_estimate=pl.CostEstimate(
            flops=40 * 10**9, bytes_accessed=12 * order**2, transcendentals=0
        ),
    )(quarter, *pieces, after)


def finish_kernel(where_ref, upper_ref, inverse_ref, *refs):
    pieces = refs[:GROUP]
    out_ref, cross = refs[GROUP:]
    order = upper_ref.shape[0]
    part = BLOCK // GROUP

    @pl.when(where_ref[0] == 0)
    def _():
        out_ref[...] = upper_ref[...]

    @pl.when(where_ref[0] != 0)
    def _():
        for mask in range(GROUP):
            quarter = where_ref[1] ^ mask
            for b in range(order // BLOCK):
                start = pl.multiple_of(BLOCK * b + part * quarter, part)
                cross[pl.ds(start, part), :] = pieces[mask][pl.ds(part * b, part), :]
        for a in range(order // BLOCK):
            rows, depth = pl.ds(a * BLOCK, BLOCK), (a + 1) * BLOCK
            out_ref[rows, :] = lax.dot_general(
                inverse_ref[rows, pl.ds(0, depth)],
                cross[:, pl.ds(0, depth)],
                (((1,), (1,)), ((), ())),
                precision=HIGHEST,
                preferred_element_type=jnp.float32,
            )


def finish(where, upper, inverse, pieces):
    order = upper.shape[0]
    return pl.pallas_call(
        finish_kernel,
        out_shape=jax.ShapeDtypeStruct((order, order), jnp.float32),
        in_specs=[SMEM] + [VMEM] * (2 + GROUP),
        out_specs=VMEM,
        scratch_shapes=[pltpu.VMEM((order, order), jnp.float32)],
        compiler_params=pltpu.CompilerParams(vmem_limit_bytes=LIMIT),
        cost_estimate=pl.CostEstimate(
            flops=12 * order**3, bytes_accessed=16 * order**2, transcendentals=0
        ),
    )(where, upper, inverse, *pieces)


def shards(sens_base, design_field, gradient, tile_index, type_codes):
    cells, order = sens_base.shape
    rows_here, width = design_field.shape
    half = cells // 2
    side = lax.axis_index("cols")
    quarter = lax.axis_index("rows") % GROUP
    side_here = side[None].astype(jnp.int32)

    cuts = [BLOCK * sum(STAGES[:s]) for s in range(len(STAGES) + 1)]
    received = []
    for start, end in zip(cuts, cuts[1:]):
        sent = lax.dynamic_slice(sens_base, ((1 - side) * half, start), (half, end - start))
        received.append(swap(sent, "cols", 1))

    tiles = width // TILE
    first_tile = lax.axis_index("rows") * rows_here // TILE * tiles
    key = ((tile_index - first_tile) * 3 + type_codes)[None, :]
    key_other = swap(key, "cols", 1)

    count = lax.axis_size("rows")
    north = lax.ppermute(design_field[-1:], "rows", [(i, i + 1) for i in range(count - 1)])
    south = lax.ppermute(design_field[:1], "rows", [(i + 1, i) for i in range(count - 1)])
    feature = features(design_field, north, south)
    jac, packed = own_part(sens_base, feature, key, gradient)

    packed = groups_sum(group_sum(packed.reshape(GROUP, -1, BLOCK)))
    other = lax.ppermute(packed, "cols", [(0, 1)])
    packed = jnp.where(side == 0, packed, other)
    pieces = rows_gather(packed)

    def stage(index, after):
        start, end = cuts[index], cuts[index + 1]
        products = cross_part(
            side_here, received[index], jac, feature, key_other[:, start:end], after
        )
        return group_sum(products)

    held = stage(0, jac)
    upper, inverse, multipliers = unpack_factor(
        quarter[None].astype(jnp.int32), pieces, order, held
    )
    sums = [groups_sum(held)]
    for index in range(1, len(STAGES)):
        sums.append(groups_sum(stage(index, multipliers)))
    others = [lax.ppermute(value, "cols", [(0, 1)]) for value in sums]

    part = BLOCK // GROUP
    blocks = order // BLOCK

    def cut(values, block, c):
        index = max(s for s in range(len(STAGES)) if cuts[s] <= block * BLOCK)
        start = block * BLOCK - cuts[index] + c * part
        return values[index][start : start + part]

    cross = jnp.concatenate(
        [
            jnp.concatenate(
                [cut(sums, a, b) + cut(others, b, a) for a in range(blocks)], axis=1
            )
            for b in range(blocks)
        ],
        axis=0,
    )
    r_panels = finish(
        jnp.stack([side, quarter]).astype(jnp.int32), upper, inverse, rows_gather(cross)
    )
    return (r_panels, multipliers[0])


def shards_general(sens_base, design_field, gradient, tile_index, type_codes):
    rows_here = design_field.shape[0]
    grid_width = design_field.shape[1]
    cols_here = sens_base.shape[1]
    factored = 2 * PW
    padded = padded_2(design_field, (("rows", 0),), 1)
    padded = jnp.pad(padded, ((0, 0), (1, 1)))
    north_cells = padded[:-2, 1:-1]
    south_cells = padded[2:, 1:-1]
    west_cells = padded[1:-1, :-2]
    east_cells = padded[1:-1, 2:]
    laplace = 4.0 * design_field - (north_cells + south_cells + west_cells + east_cells)
    slope_x = 0.5 * (east_cells - west_cells)
    slope_y = 0.5 * (south_cells - north_cells)
    stencils = jnp.stack([laplace, slope_x, slope_y]).reshape(3, -1)
    row_glob = lax.axis_index("rows") * rows_here + jnp.arange(rows_here, dtype=jnp.int32)
    col_ids = jnp.arange(grid_width, dtype=jnp.int32) // TILE
    cell_tile = ((row_glob // TILE)[:, None] * (grid_width // TILE) + col_ids[None, :]).reshape(-1)
    local_jac = assemble(sens_base, tile_index, type_codes, stencils, cell_tile)
    grad_flat = gradient.reshape(-1)
    row_major = lax.all_to_all(local_jac, "cols", split_axis=0, concat_axis=1, tiled=True)
    row_piece = row_major.shape[0]
    grad_part = lax.dynamic_slice_in_dim(
        grad_flat, lax.axis_index("cols") * row_piece, row_piece, 0
    )
    leading = row_major[:, :factored]
    gram_block = lax.dot_general(
        leading, row_major, (((0,), (0,)), ((), ())), preferred_element_type=jnp.float32
    )
    projected = jnp.dot(grad_part, leading, preferred_element_type=jnp.float32)
    gram_block, projected = lax.psum((gram_block, projected), ("rows", "cols"))
    gram_head = gram_block[:, :factored]
    gram_own = lax.dynamic_slice_in_dim(
        gram_block, lax.axis_index("cols") * cols_here, cols_here, 1
    )
    _, inverse, multipliers = factor(gram_head, projected[None, :])
    r_panels = matmul(inverse, gram_own)
    return (r_panels, multipliers[0])


def solution(mesh):
    placed = (P("rows", "cols"), P("rows", None), P("rows", None), P("cols"), P("cols"))
    pairs = mesh.shape["cols"] == 2 and mesh.shape["rows"] in (4, 8, 16, 32, 64)
    return jax.shard_map(
        shards if pairs else shards_general,
        mesh=mesh,
        in_specs=placed,
        out_specs=(P(None, "cols"), P()),
        check_vma=False,
    )
```

```python
import functools

import jax
import jax.numpy as jnp
from jax import lax
from jax.experimental import pallas as pl
from jax.experimental.pallas import tpu as pltpu
from jax.sharding import PartitionSpec as P

TILE = 128
PW = 256
BLOCK = 128
FEATURES = 80
GROUP = 4
HIGHEST = lax.Precision.HIGHEST
VMEM = pl.BlockSpec(memory_space=pltpu.VMEM)
SMEM = pl.BlockSpec(memory_space=pltpu.SMEM)
LIMIT = 16 * 2**20
WIDE_LIMIT = 48 * 2**20
ANY = pl.BlockSpec(memory_space=pl.ANY)
STAGES = (3, 1)
LONG = pl.CostEstimate(flops=8 * 10**9, bytes_accessed=1000, transcendentals=0)
BRIEF = pl.CostEstimate(flops=1000, bytes_accessed=1000, transcendentals=0)


def padded_2(cells, sides, width):
    for axis, dim in sides:
        count = lax.axis_size(axis)
        ends = count - 1
        head = lax.slice_in_dim(cells, 0, width, axis=dim)
        tail = lax.slice_in_dim(cells, cells.shape[dim] - width, cells.shape[dim], axis=dim)
        cells = jnp.concatenate(
            [
                lax.ppermute(tail, axis, [(i, (i + 1) % count) for i in range(ends)]),
                cells,
                lax.ppermute(head, axis, [((i + 1) % count, i) for i in range(ends)]),
            ],
            axis=dim,
        )
    return cells


def assemble(base_cols, tile_cols, type_cols, stencils, cell_tile):
    kinds_all = jnp.arange(3, dtype=jnp.int32)
    chooser = (type_cols[None, :] == kinds_all[:, None]).astype(jnp.float32)
    picked = lax.dot_general(
        stencils,
        chooser,
        (((0,), (0,)), ((), ())),
        precision=lax.Precision.HIGHEST,
        preferred_element_type=jnp.float32,
    )
    inside = cell_tile[:, None] == tile_cols[None, :]
    total = base_cols.astype(jnp.float32) + jnp.where(inside, picked / TILE, 0.0)
    return total.astype(jnp.bfloat16)


def matmul(left, right):
    return jnp.dot(left, right, precision=HIGHEST, preferred_element_type=jnp.float32)


def inverse_root(value):
    guess = lax.rsqrt(value)
    return guess * (1.5 - 0.5 * value * guess * guess)


def reciprocal(value):
    guess = pl.reciprocal(value, approx=True)
    guess = guess * (2.0 - value * guess)
    return guess * (2.0 - value * guess)


def lane(part, index):
    return jnp.broadcast_to(part[:, index : index + 1], part.shape)


def sublane(part, index):
    return jnp.broadcast_to(part[index : index + 1, :], part.shape)


def diagonal_inverse(block):
    groups = BLOCK // 8
    shape = (8, BLOCK)
    lanes = lax.broadcasted_iota(jnp.int32, shape, 1)
    subs = lax.broadcasted_iota(jnp.int32, shape, 0)
    parts = [block[8 * g : 8 * g + 8, :] for g in range(groups)]
    whole = []
    for p in range(groups):
        part, first = parts[p], 8 * p
        cols = [lane(part, first + k) for k in range(8)]
        inv = [None] * 8
        low = [jnp.zeros(shape, jnp.float32) for _ in range(8)]
        pivots = jnp.ones(shape, jnp.float32)
        for j in range(8):
            here = subs == j
            pivot = sublane(cols[j], j)
            ratio = reciprocal(pivot)
            pivots = jnp.where(here, pivot, pivots)
            for k in range(j):
                low[k] = jnp.where(here, inv[k], low[k])
            low[j] = jnp.where(here, 1.0, low[j])
            column = cols[j]
            for k in range(j + 1, 8):
                row = sublane(cols[k], j) * ratio
                cols[k] = jnp.where(here, row, cols[k] - column * row)
            for k in range(j):
                row = sublane(inv[k], j) * ratio
                inv[k] = jnp.where(here, row, inv[k] - column * row)
            inv[j] = jnp.where(here, ratio, -column * ratio)
        scale = inverse_root(pivots)
        inside = (lanes >= first) & (lanes < first + 8)
        unit = jnp.where(lanes - first == subs, 1.0, 0.0)
        rows = jnp.where(inside, unit, part)
        spread = [sublane(rows, k) for k in range(8)]
        solved = sum(low[k] * spread[k] for k in range(8)) * scale
        whole.append(jnp.where(lanes < first + 8, solved, 0.0))
        if p + 1 < groups:
            step = sum(inv[k] * spread[k] for k in range(8))
            step = [sublane(step, k) for k in range(8)]
            for g in range(p + 1, groups):
                taken = sum(lane(parts[g], first + k) * step[k] for k in range(8))
                parts[g] = jnp.where(inside, 0.0, parts[g]) - taken
    return jnp.concatenate(whole, axis=0)


def factor_steps(upper_ref, inverse_ref, first, last):
    blocks = upper_ref.shape[0] // BLOCK

    @pl.loop(first, last)
    def _(step):
        mine = pl.ds(pl.multiple_of(step * BLOCK, BLOCK), BLOCK)
        small = diagonal_inverse(upper_ref[mine, mine])
        upper_ref[mine, :] = matmul(small, upper_ref[mine, :])
        inverse_ref[mine, :] = matmul(small, inverse_ref[mine, :])

        @pl.loop(step + 1, blocks)
        def _(later):
            theirs = pl.ds(pl.multiple_of(later * BLOCK, BLOCK), BLOCK)
            factor = upper_ref[mine, theirs]

            def minus(target):
                target[theirs, :] -= lax.dot_general(
                    factor,
                    target[mine, :],
                    (((0,), (0,)), ((), ())),
                    precision=HIGHEST,
                    preferred_element_type=jnp.float32,
                )

            minus(upper_ref)
            minus(inverse_ref)


def start_inverse(inverse_ref):
    rows = lax.broadcasted_iota(jnp.int32, inverse_ref.shape, 0)
    cols = lax.broadcasted_iota(jnp.int32, inverse_ref.shape, 1)
    inverse_ref[...] = jnp.where(rows == cols, 1.0, 0.0)


def keep_upper(upper_ref):
    rows = lax.broadcasted_iota(jnp.int32, upper_ref.shape, 0)
    cols = lax.broadcasted_iota(jnp.int32, upper_ref.shape, 1)
    upper_ref[...] = jnp.where(rows <= cols, upper_ref[...], 0.0)


def solve_twice(inverse_ref, projected_ref):
    half = jnp.sum(inverse_ref[...] * projected_ref[...], axis=1, keepdims=True)
    return jnp.sum(inverse_ref[...] * half, axis=0, keepdims=True)


def factor_kernel(gram_ref, projected_ref, upper_ref, inverse_ref, multipliers_ref):
    upper_ref[...] = gram_ref[...]
    start_inverse(inverse_ref)
    factor_steps(upper_ref, inverse_ref, 0, upper_ref.shape[0] // BLOCK)
    keep_upper(upper_ref)
    multipliers_ref[...] = solve_twice(inverse_ref, projected_ref)


def factor(gram, projected):
    order = gram.shape[0]
    return pl.pallas_call(
        factor_kernel,
        out_shape=(
            jax.ShapeDtypeStruct((order, order), jnp.float32),
            jax.ShapeDtypeStruct((order, order), jnp.float32),
            jax.ShapeDtypeStruct((1, order), jnp.float32),
        ),
        in_specs=[pl.BlockSpec(memory_space=pltpu.VMEM)] * 2,
        out_specs=[pl.BlockSpec(memory_space=pltpu.VMEM)] * 3,
        compiler_params=pltpu.CompilerParams(vmem_limit_bytes=LIMIT),
        cost_estimate=pl.CostEstimate(
            flops=6 * order**3, bytes_accessed=12 * order**2, transcendentals=0
        ),
    )(gram, projected)


def features_kernel(field_ref, north_ref, south_ref, out_ref):
    field = field_ref[...]
    rows, width = field.shape
    lanes = lax.broadcasted_iota(jnp.int32, field.shape, 1)
    north = jnp.concatenate([north_ref[...], field[:-1]], axis=0)
    south = jnp.concatenate([field[1:], south_ref[...]], axis=0)
    west = jnp.where(lanes == 0, 0.0, pltpu.roll(field, 1, 1))
    east = jnp.where(lanes == width - 1, 0.0, pltpu.roll(field, width - 1, 1))
    laplace = 4.0 * field - (north + south + west + east)
    slope_x = 0.5 * (east - west)
    slope_y = 0.5 * (south - north)
    parts = []
    for stencil in (laplace, slope_x, slope_y):
        rest = stencil / TILE
        for _ in range(3):
            part = rest.astype(jnp.bfloat16).astype(jnp.float32)
            parts.append(part)
            rest = rest - part
    tiles = width // TILE
    shape = (FEATURES, width)
    owner = lax.broadcasted_iota(jnp.int32, shape, 0) // len(parts)
    tile = lax.broadcasted_iota(jnp.int32, shape, 1) // TILE
    blank = jnp.zeros((FEATURES - tiles * len(parts), width), jnp.float32)
    for row in range(rows):
        block = jnp.concatenate([part[row : row + 1] for part in parts], axis=0)
        whole = jnp.concatenate([block] * tiles + [blank], axis=0)
        out_ref[row] = jnp.where(owner == tile, whole, 0.0).astype(jnp.bfloat16)


def features(field, north, south):
    rows, width = field.shape
    return pl.pallas_call(
        features_kernel,
        out_shape=jax.ShapeDtypeStruct((rows, FEATURES, width), jnp.bfloat16),
        in_specs=[VMEM] * 3,
        out_specs=VMEM,
        compiler_params=pltpu.CompilerParams(vmem_limit_bytes=LIMIT),
        cost_estimate=BRIEF,
    )(field, north, south)


def assembled(base, feature, key):
    rows = lax.broadcasted_iota(jnp.int32, (FEATURES, key.shape[1]), 0) // 3
    chooser = jnp.where(rows == key, 1.0, 0.0).astype(jnp.bfloat16)
    added = lax.dot_general(
        feature, chooser, (((0,), (0,)), ((), ())), preferred_element_type=jnp.float32
    )
    return (base.astype(jnp.float32) + added).astype(jnp.bfloat16)


def transposed_dot(left, right):
    return lax.dot_general(
        left, right, (((0,), (0,)), ((), ())), preferred_element_type=jnp.float32
    )


def upper_blocks(order):
    count = order // BLOCK
    return [(a, b) for a in range(count) for b in range(a, count)]


def packed_rows(order):
    used = len(upper_blocks(order)) * BLOCK + order // BLOCK
    return -(-used // (8 * GROUP)) * 8 * GROUP


def own_kernel(
    place_ref, base_ref, feature_ref, key_ref, grad_ref, _, jac_ref, *refs
):
    outs = refs[:GROUP]
    gram, projected, packed = refs[GROUP:]
    step = pl.program_id(0)
    half = pl.num_programs(0) // 2
    order = base_ref.shape[1]
    jac = assembled(base_ref[...], feature_ref[0], key_ref[...])

    @pl.when(step // half == place_ref[0])
    def _():
        jac_ref[...] = jac

    @pl.when(step == 0)
    def _():
        gram[...] = jnp.zeros_like(gram)
        projected[...] = jnp.zeros_like(projected)

    gram[...] += transposed_dot(jac, jac)
    projected[...] += jnp.dot(grad_ref[0], jac, preferred_element_type=jnp.float32)

    @pl.when(step == pl.num_programs(0) - 1)
    def _():
        packed[...] = jnp.zeros_like(packed)
        blocks = upper_blocks(order)
        for index, (a, b) in enumerate(blocks):
            packed[pl.ds(index * BLOCK, BLOCK), :] = gram[
                pl.ds(a * BLOCK, BLOCK), pl.ds(b * BLOCK, BLOCK)
            ]
        for c in range(order // BLOCK):
            packed[pl.ds(len(blocks) * BLOCK + c, 1), :] = projected[:, pl.ds(c * BLOCK, BLOCK)]
        size = outs[0].shape[0]
        for mask in range(GROUP):
            start = pl.multiple_of((place_ref[1] ^ mask) * size, 8)
            outs[mask][...] = packed[pl.ds(start, size), :]


def own_part(place, base, feature, key, gradient, after):
    cells, order = base.shape
    rows, width = gradient.shape
    half = rows // 2
    size = packed_rows(order) // GROUP
    return pl.pallas_call(
        own_kernel,
        grid_spec=pltpu.PrefetchScalarGridSpec(
            num_scalar_prefetch=1,
            grid=(rows,),
            in_specs=[
                pl.BlockSpec((width, order), lambda i, s: (i, 0)),
                pl.BlockSpec((1, FEATURES, width), lambda i, s: (i, 0, 0)),
                pl.BlockSpec((1, order), lambda i, s: (0, 0)),
                pl.BlockSpec((1, 1, width), lambda i, s: (i, 0, 0)),
                ANY,
            ],
            out_specs=[
                pl.BlockSpec(
                    (width, order), lambda i, s: (jnp.clip(i - s[0] * half, 0, half - 1), 0)
                )
            ]
            + [pl.BlockSpec((size, BLOCK), lambda i, s: (0, 0))] * GROUP,
            scratch_shapes=[
                pltpu.VMEM((order, order), jnp.float32),
                pltpu.VMEM((1, order), jnp.float32),
                pltpu.VMEM((GROUP * size, BLOCK), jnp.float32),
            ],
        ),
        out_shape=[jax.ShapeDtypeStruct((cells // 2, order), jnp.bfloat16)]
        + [jax.ShapeDtypeStruct((size, BLOCK), jnp.float32)] * GROUP,
        compiler_params=pltpu.CompilerParams(vmem_limit_bytes=WIDE_LIMIT),
        cost_estimate=BRIEF,
    )(place, base, feature, key, gradient.reshape(rows, 1, width), after)


def send_kernel(place_ref, base_ref, out_ref):
    out_ref[...] = base_ref[...]


def send_part(place, base, rows, start, end):
    cells = base.shape[0]
    height, width = cells // rows, end - start
    half = rows // 2
    return pl.pallas_call(
        send_kernel,
        grid_spec=pltpu.PrefetchScalarGridSpec(
            num_scalar_prefetch=1,
            grid=(half, width // BLOCK),
            in_specs=[
                pl.BlockSpec(
                    (height, BLOCK), lambda i, j, s: ((1 - s[0]) * half + i, start // BLOCK + j)
                )
            ],
            out_specs=pl.BlockSpec((height, BLOCK), lambda i, j, s: (i, j)),
        ),
        out_shape=jax.ShapeDtypeStruct((cells // 2, width), base.dtype),
        compiler_params=pltpu.CompilerParams(vmem_limit_bytes=WIDE_LIMIT + 2**23),
        cost_estimate=BRIEF,
    )(place, base)


def cross_kernel(place_ref, recv_ref, jac_ref, feature_ref, key_ref, *refs):
    outs = refs[-2 - GROUP : -2]
    total, out_ref = refs[-2:]
    step = pl.program_id(0)
    other = assembled(recv_ref[...], feature_ref[0], key_ref[...])

    @pl.when(step == 0)
    def _():
        total[...] = jnp.zeros_like(total)

    total[...] += transposed_dot(other, jac_ref[...])
    count = total.shape[1] // BLOCK
    part = BLOCK // GROUP
    last = step == pl.num_programs(0) - 1

    blocks = total.shape[0] // BLOCK

    @pl.when(last & (place_ref[0] == 0))
    def _():
        for k in range(blocks):
            for q in range(GROUP):
                for c in range(count):
                    out_ref[q, pl.ds(BLOCK * k + part * c, part), :] = total[
                        pl.ds(BLOCK * k + part * q, part), pl.ds(BLOCK * c, BLOCK)
                    ]

    @pl.when(last & (place_ref[0] != 0))
    def _():
        for k in range(blocks):
            for c in range(count):
                block = total[pl.ds(BLOCK * k, BLOCK), pl.ds(BLOCK * c, BLOCK)].T
                for q in range(GROUP):
                    out_ref[q, pl.ds(BLOCK * k + part * c, part), :] = block[
                        part * q : part * q + part
                    ]

    @pl.when(last)
    def _():
        for mask in range(GROUP):
            outs[mask][...] = out_ref[place_ref[1] ^ mask]


def cross_part(place, recv, jac, feature, key, *after):
    cells, width_recv = recv.shape
    order = jac.shape[1]
    rows, _, width = feature.shape
    steps = rows // 2
    return pl.pallas_call(
        cross_kernel,
        grid_spec=pltpu.PrefetchScalarGridSpec(
            num_scalar_prefetch=1,
            grid=(steps,),
            in_specs=[
                pl.BlockSpec((width, width_recv), lambda i, s: (i, 0)),
                pl.BlockSpec((width, order), lambda i, s: (i, 0)),
                pl.BlockSpec((1, FEATURES, width), lambda i, s: (s[0] * steps + i, 0, 0)),
                pl.BlockSpec((1, width_recv), lambda i, s: (0, 0)),
            ]
            + [ANY] * len(after),
            out_specs=[pl.BlockSpec((width_recv, BLOCK), lambda i, s: (0, 0))] * GROUP,
            scratch_shapes=[
                pltpu.VMEM((width_recv, order), jnp.float32),
                pltpu.VMEM((GROUP, width_recv, BLOCK), jnp.float32),
            ],
        ),
        out_shape=[jax.ShapeDtypeStruct((width_recv, BLOCK), jnp.float32)] * GROUP,
        compiler_params=pltpu.CompilerParams(vmem_limit_bytes=LIMIT),
        cost_estimate=BRIEF,
    )(place, recv, jac, feature, key, *after)


def swap(value, axis, mask):
    count = lax.axis_size(axis)
    return lax.ppermute(value, axis, [(i, i ^ mask) for i in range(count)])


def add_kernel(count, *refs):
    refs[-1][...] = sum(ref[...] for ref in refs[1:count]) + refs[0][...]


def add(values, *after):
    return pl.pallas_call(
        functools.partial(add_kernel, len(values)),
        out_shape=jax.ShapeDtypeStruct(values[0].shape, values[0].dtype),
        in_specs=[VMEM] * len(values) + [ANY] * len(after),
        out_specs=VMEM,
        compiler_params=pltpu.CompilerParams(vmem_limit_bytes=LIMIT),
        cost_estimate=BRIEF,
    )(*values, *after)


def group_swaps(parts):
    return [parts[0]] + [swap(parts[mask], "rows", mask) for mask in range(1, GROUP)]


def group_sum(parts):
    got = group_swaps(parts)
    return got[0] + got[1] + got[2] + got[3]


def groups_sum(held):
    masks = range(GROUP, lax.axis_size("rows"), GROUP)
    return held + sum(swap(held, "rows", mask) for mask in masks)


def doubled(held, masks):
    for mask in masks:
        held = held + swap(held, "rows", mask)
    return held


def rows_gather(own):
    return [own] + [swap(own, "rows", mask) for mask in range(1, GROUP)]


def first_factor_kernel(last, place_ref, *refs):
    pieces = refs[:GROUP]
    upper_ref, inverse_ref, projected_ref, whole = refs[GROUP + 1 :]
    size = pieces[0].shape[0]
    for mask in range(GROUP):
        start = pl.multiple_of((place_ref[1] ^ mask) * size, 8)
        whole[pl.ds(start, size), :] = pieces[mask][...]
    order = upper_ref.shape[0]
    blocks = upper_blocks(order)
    upper_ref[...] = jnp.zeros_like(upper_ref)
    for index, (a, b) in enumerate(blocks):
        upper_ref[pl.ds(a * BLOCK, BLOCK), pl.ds(b * BLOCK, BLOCK)] = whole[
            pl.ds(index * BLOCK, BLOCK), :
        ]
    for c in range(order // BLOCK):
        projected_ref[:, pl.ds(c * BLOCK, BLOCK)] = whole[pl.ds(len(blocks) * BLOCK + c, 1), :]
    start_inverse(inverse_ref)
    factor_steps(upper_ref, inverse_ref, 0, last)


def square(order):
    return jax.ShapeDtypeStruct((order, order), jnp.float32)


def row(order):
    return jax.ShapeDtypeStruct((1, order), jnp.float32)


def first_factor(place, pieces, order, last, after):
    return pl.pallas_call(
        functools.partial(first_factor_kernel, last),
        out_shape=(square(order), square(order), row(order)),
        in_specs=[SMEM] + [VMEM] * GROUP + [ANY],
        out_specs=[VMEM] * 3,
        scratch_shapes=[pltpu.VMEM((packed_rows(order), BLOCK), jnp.float32)],
        compiler_params=pltpu.CompilerParams(vmem_limit_bytes=LIMIT),
        cost_estimate=BRIEF,
    )(place, *pieces, after)


def more_factor_kernel(first, last, upper_in, inverse_in, _, upper_ref, inverse_ref):
    upper_ref[...] = upper_in[...]
    inverse_ref[...] = inverse_in[...]
    factor_steps(upper_ref, inverse_ref, first, last)


def more_factor(upper, inverse, first, last, after, cost):
    order = upper.shape[0]
    return pl.pallas_call(
        functools.partial(more_factor_kernel, first, last),
        out_shape=(square(order), square(order)),
        in_specs=[VMEM] * 2 + [ANY],
        out_specs=[VMEM] * 2,
        compiler_params=pltpu.CompilerParams(vmem_limit_bytes=LIMIT),
        cost_estimate=cost,
    )(upper, inverse, after)


def lower_rows(order):
    return len(upper_blocks(order)) * BLOCK


def last_factor_kernel(first, upper_in, inverse_in, projected, _, upper_ref, inverse_ref, out_ref):
    upper_ref[...] = upper_in[...]
    inverse_ref[...] = inverse_in[...]
    factor_steps(upper_ref, inverse_ref, first, upper_ref.shape[0] // BLOCK)
    keep_upper(upper_ref)
    out_ref[...] = solve_twice(inverse_ref, projected)


def last_factor(upper, inverse, projected, first, after, cost):
    order = upper.shape[0]
    return pl.pallas_call(
        functools.partial(last_factor_kernel, first),
        out_shape=(square(order), square(order), row(order)),
        in_specs=[VMEM] * 3 + [ANY],
        out_specs=[VMEM] * 3,
        compiler_params=pltpu.CompilerParams(vmem_limit_bytes=LIMIT),
        cost_estimate=cost,
    )(upper, inverse, projected, after)


def pack_kernel(inverse_ref, solved_ref, _, packed_ref):
    order = inverse_ref.shape[0]
    for index, (b, a) in enumerate(upper_blocks(order)):
        packed_ref[pl.ds(index * BLOCK, BLOCK), :] = inverse_ref[
            pl.ds(a * BLOCK, BLOCK), pl.ds(b * BLOCK, BLOCK)
        ]
    packed_ref[pl.ds(lower_rows(order), 8), :] = jnp.zeros((8, BLOCK), jnp.float32)
    for c in range(order // BLOCK):
        packed_ref[pl.ds(lower_rows(order) + c, 1), :] = solved_ref[:, pl.ds(c * BLOCK, BLOCK)]


def pack(inverse, solved, after):
    order = inverse.shape[0]
    return pl.pallas_call(
        pack_kernel,
        out_shape=jax.ShapeDtypeStruct((lower_rows(order) + 8, BLOCK), jnp.float32),
        in_specs=[VMEM] * 2 + [ANY],
        out_specs=VMEM,
        compiler_params=pltpu.CompilerParams(vmem_limit_bytes=LIMIT),
        cost_estimate=BRIEF,
    )(inverse, solved, after)


def finish_kernel(place_ref, upper_ref, packed_ref, *refs):
    pieces = refs[:GROUP]
    out_ref, cross, inverse = refs[GROUP:]
    order = upper_ref.shape[0]
    part = BLOCK // GROUP

    @pl.when(place_ref[0] == 0)
    def _():
        out_ref[...] = upper_ref[...]

    @pl.when(place_ref[0] != 0)
    def _():
        for mask in range(GROUP):
            quarter = place_ref[1] ^ mask
            for b in range(order // BLOCK):
                start = pl.multiple_of(BLOCK * b + part * quarter, part)
                cross[pl.ds(start, part), :] = pieces[mask][pl.ds(part * b, part), :]
        for index, (b, a) in enumerate(upper_blocks(order)):
            inverse[pl.ds(a * BLOCK, BLOCK), pl.ds(b * BLOCK, BLOCK)] = packed_ref[
                pl.ds(index * BLOCK, BLOCK), :
            ]
        for a in range(order // BLOCK):
            rows, depth = pl.ds(a * BLOCK, BLOCK), (a + 1) * BLOCK
            out_ref[rows, :] = lax.dot_general(
                inverse[rows, pl.ds(0, depth)],
                cross[:, pl.ds(0, depth)],
                (((1,), (1,)), ((), ())),
                precision=HIGHEST,
                preferred_element_type=jnp.float32,
            )


def finish(place, upper, packed, pieces):
    order = upper.shape[0]
    return pl.pallas_call(
        finish_kernel,
        out_shape=square(order),
        in_specs=[SMEM] + [VMEM] * (2 + GROUP),
        out_specs=VMEM,
        scratch_shapes=[pltpu.VMEM((order, order), jnp.float32)] * 2,
        compiler_params=pltpu.CompilerParams(vmem_limit_bytes=LIMIT),
        cost_estimate=BRIEF,
    )(place, upper, packed, *pieces)


def shards(sens_base, design_field, gradient, tile_index, type_codes):
    cells, order = sens_base.shape
    rows_here, width = design_field.shape
    side = lax.axis_index("cols")
    quarter = lax.axis_index("rows") % GROUP
    place = jnp.stack([side, quarter]).astype(jnp.int32)

    cuts = [BLOCK * sum(STAGES[:s]) for s in range(len(STAGES) + 1)]
    received = [
        swap(send_part(place, sens_base, rows_here, start, end), "cols", 1)
        for start, end in zip(cuts, cuts[1:])
    ]

    tiles = width // TILE
    first_tile = lax.axis_index("rows") * rows_here // TILE * tiles
    key = ((tile_index - first_tile) * 3 + type_codes)[None, :]
    key_other = swap(key, "cols", 1)

    count = lax.axis_size("rows")
    north = lax.ppermute(design_field[-1:], "rows", [(i, i + 1) for i in range(count - 1)])
    south = lax.ppermute(design_field[:1], "rows", [(i + 1, i) for i in range(count - 1)])
    feature = features(design_field, north, south)
    jac, *packed = own_part(place, sens_base, feature, key, gradient, key_other)
    pieces = rows_gather(groups_sum(group_sum(packed)))

    def stage(index, *after):
        start, end = cuts[index], cuts[index + 1]
        return cross_part(place, received[index], jac, feature, key_other[:, start:end], *after)

    first = stage(0, *pieces[1:])
    shares = group_swaps(first)
    upper, inverse, projected = first_factor(place, pieces, order, 1, first[0])
    held = add(shares, inverse)
    upper, inverse = more_factor(upper, inverse, 1, 2, held, BRIEF)
    middle = doubled(held, [GROUP])
    last = stage(1, inverse, middle)
    shares = group_swaps(last)
    upper, inverse = more_factor(upper, inverse, 2, 3, last[0], LONG)
    held_last = add(shares, inverse)
    masks = range(GROUP, count, GROUP)
    shares = [held_last] + [swap(held_last, "rows", mask) for mask in masks]
    upper, inverse, solved = last_factor(upper, inverse, projected, 3, held_last, LONG)
    far = range(2 * GROUP, count, 2 * GROUP)
    sums = [
        middle + sum(swap(middle, "rows", mask) for mask in far),
        add(shares, solved),
    ]
    others = [lax.ppermute(value, "cols", [(0, 1)]) for value in sums]
    packed = pack(inverse, solved, others[1])
    packed_other = lax.ppermute(packed, "cols", [(0, 1)])

    part = BLOCK // GROUP
    blocks = order // BLOCK

    def cut(values, block, c):
        index = max(s for s in range(len(STAGES)) if cuts[s] <= block * BLOCK)
        start = block * BLOCK - cuts[index] + c * part
        return values[index][start : start + part]

    cross = jnp.concatenate(
        [
            jnp.concatenate(
                [cut(sums, a, b) + cut(others, b, a) for a in range(blocks)], axis=1
            )
            for b in range(blocks)
        ],
        axis=0,
    )
    r_panels = finish(place, upper, packed_other, rows_gather(cross))
    begin = lower_rows(order)
    multipliers = jnp.where(side == 0, packed[begin:], packed_other[begin:])
    return (r_panels, multipliers[:blocks].reshape(-1))


def shards_general(sens_base, design_field, gradient, tile_index, type_codes):
    rows_here = design_field.shape[0]
    grid_width = design_field.shape[1]
    cols_here = sens_base.shape[1]
    factored = 2 * PW
    padded = padded_2(design_field, (("rows", 0),), 1)
    padded = jnp.pad(padded, ((0, 0), (1, 1)))
    north_cells = padded[:-2, 1:-1]
    south_cells = padded[2:, 1:-1]
    west_cells = padded[1:-1, :-2]
    east_cells = padded[1:-1, 2:]
    laplace = 4.0 * design_field - (north_cells + south_cells + west_cells + east_cells)
    slope_x = 0.5 * (east_cells - west_cells)
    slope_y = 0.5 * (south_cells - north_cells)
    stencils = jnp.stack([laplace, slope_x, slope_y]).reshape(3, -1)
    row_glob = lax.axis_index("rows") * rows_here + jnp.arange(rows_here, dtype=jnp.int32)
    col_ids = jnp.arange(grid_width, dtype=jnp.int32) // TILE
    cell_tile = ((row_glob // TILE)[:, None] * (grid_width // TILE) + col_ids[None, :]).reshape(-1)
    local_jac = assemble(sens_base, tile_index, type_codes, stencils, cell_tile)
    grad_flat = gradient.reshape(-1)
    row_major = lax.all_to_all(local_jac, "cols", split_axis=0, concat_axis=1, tiled=True)
    row_piece = row_major.shape[0]
    grad_part = lax.dynamic_slice_in_dim(
        grad_flat, lax.axis_index("cols") * row_piece, row_piece, 0
    )
    leading = row_major[:, :factored]
    gram_block = lax.dot_general(
        leading, row_major, (((0,), (0,)), ((), ())), preferred_element_type=jnp.float32
    )
    projected = jnp.dot(grad_part, leading, preferred_element_type=jnp.float32)
    gram_block, projected = lax.psum((gram_block, projected), ("rows", "cols"))
    gram_head = gram_block[:, :factored]
    gram_own = lax.dynamic_slice_in_dim(
        gram_block, lax.axis_index("cols") * cols_here, cols_here, 1
    )
    _, inverse, multipliers = factor(gram_head, projected[None, :])
    r_panels = matmul(inverse, gram_own)
    return (r_panels, multipliers[0])


def solution(mesh):
    placed = (P("rows", "cols"), P("rows", None), P("rows", None), P("cols"), P("cols"))
    pairs = mesh.shape["cols"] == 2 and mesh.shape["rows"] in (8, 16, 32, 64)
    return jax.shard_map(
        shards if pairs else shards_general,
        mesh=mesh,
        in_specs=placed,
        out_specs=(P(None, "cols"), P()),
        check_vma=False,
    )
```

```python
import functools

import jax
import jax.numpy as jnp
from jax import lax
from jax.experimental import pallas as pl
from jax.experimental.pallas import tpu as pltpu
from jax.sharding import PartitionSpec as P

TILE = 128
PW = 256
BLOCK = 128
FEATURES = 80
KEY_ROWS = 16
GROUP = 4
HIGHEST = lax.Precision.HIGHEST
VMEM = pl.BlockSpec(memory_space=pltpu.VMEM)
SMEM = pl.BlockSpec(memory_space=pltpu.SMEM)
LIMIT = 16 * 2**20
WIDE_LIMIT = 48 * 2**20
ANY = pl.BlockSpec(memory_space=pl.ANY)
STAGES = (3, 1)
LONG = pl.CostEstimate(flops=8 * 10**9, bytes_accessed=1000, transcendentals=0)
BRIEF = pl.CostEstimate(flops=1000, bytes_accessed=1000, transcendentals=0)


def padded_2(cells, sides, width):
    for axis, dim in sides:
        count = lax.axis_size(axis)
        ends = count - 1
        head = lax.slice_in_dim(cells, 0, width, axis=dim)
        tail = lax.slice_in_dim(cells, cells.shape[dim] - width, cells.shape[dim], axis=dim)
        cells = jnp.concatenate(
            [
                lax.ppermute(tail, axis, [(i, (i + 1) % count) for i in range(ends)]),
                cells,
                lax.ppermute(head, axis, [((i + 1) % count, i) for i in range(ends)]),
            ],
            axis=dim,
        )
    return cells


def assemble(base_cols, tile_cols, type_cols, stencils, cell_tile):
    kinds_all = jnp.arange(3, dtype=jnp.int32)
    chooser = (type_cols[None, :] == kinds_all[:, None]).astype(jnp.float32)
    picked = lax.dot_general(
        stencils,
        chooser,
        (((0,), (0,)), ((), ())),
        precision=lax.Precision.HIGHEST,
        preferred_element_type=jnp.float32,
    )
    inside = cell_tile[:, None] == tile_cols[None, :]
    total = base_cols.astype(jnp.float32) + jnp.where(inside, picked / TILE, 0.0)
    return total.astype(jnp.bfloat16)


def matmul(left, right):
    return jnp.dot(left, right, precision=HIGHEST, preferred_element_type=jnp.float32)


def inverse_root(value):
    guess = lax.rsqrt(value)
    return guess * (1.5 - 0.5 * value * guess * guess)


def reciprocal(value):
    guess = pl.reciprocal(value, approx=True)
    guess = guess * (2.0 - value * guess)
    return guess * (2.0 - value * guess)


def lane(part, index):
    return jnp.broadcast_to(part[:, index : index + 1], part.shape)


def sublane(part, index):
    return jnp.broadcast_to(part[index : index + 1, :], part.shape)


def diagonal_inverse(block):
    groups = BLOCK // 8
    shape = (8, BLOCK)
    lanes = lax.broadcasted_iota(jnp.int32, shape, 1)
    subs = lax.broadcasted_iota(jnp.int32, shape, 0)
    parts = [block[8 * g : 8 * g + 8, :] for g in range(groups)]
    whole = []
    for p in range(groups):
        part, first = parts[p], 8 * p
        cols = [lane(part, first + k) for k in range(8)]
        inv = [None] * 8
        low = [jnp.zeros(shape, jnp.float32) for _ in range(8)]
        pivots = jnp.ones(shape, jnp.float32)
        for j in range(8):
            here = subs == j
            pivot = sublane(cols[j], j)
            ratio = reciprocal(pivot)
            pivots = jnp.where(here, pivot, pivots)
            for k in range(j):
                low[k] = jnp.where(here, inv[k], low[k])
            low[j] = jnp.where(here, 1.0, low[j])
            column = cols[j]
            for k in range(j + 1, 8):
                row = sublane(cols[k], j) * ratio
                cols[k] = jnp.where(here, row, cols[k] - column * row)
            for k in range(j):
                row = sublane(inv[k], j) * ratio
                inv[k] = jnp.where(here, row, inv[k] - column * row)
            inv[j] = jnp.where(here, ratio, -column * ratio)
        scale = inverse_root(pivots)
        inside = (lanes >= first) & (lanes < first + 8)
        unit = jnp.where(lanes - first == subs, 1.0, 0.0)
        rows = jnp.where(inside, unit, part)
        spread = [sublane(rows, k) for k in range(8)]
        solved = sum(low[k] * spread[k] for k in range(8)) * scale
        whole.append(jnp.where(lanes < first + 8, solved, 0.0))
        if p + 1 < groups:
            step = sum(inv[k] * spread[k] for k in range(8))
            step = [sublane(step, k) for k in range(8)]
            for g in range(p + 1, groups):
                taken = sum(lane(parts[g], first + k) * step[k] for k in range(8))
                parts[g] = jnp.where(inside, 0.0, parts[g]) - taken
    return jnp.concatenate(whole, axis=0)


def factor_steps(upper_ref, inverse_ref, first, last):
    blocks = upper_ref.shape[0] // BLOCK

    @pl.loop(first, last)
    def _(step):
        mine = pl.ds(pl.multiple_of(step * BLOCK, BLOCK), BLOCK)
        small = diagonal_inverse(upper_ref[mine, mine])
        upper_ref[mine, :] = matmul(small, upper_ref[mine, :])
        inverse_ref[mine, :] = matmul(small, inverse_ref[mine, :])

        @pl.loop(step + 1, blocks)
        def _(later):
            theirs = pl.ds(pl.multiple_of(later * BLOCK, BLOCK), BLOCK)
            factor = upper_ref[mine, theirs]

            def minus(target):
                target[theirs, :] -= lax.dot_general(
                    factor,
                    target[mine, :],
                    (((0,), (0,)), ((), ())),
                    precision=HIGHEST,
                    preferred_element_type=jnp.float32,
                )

            minus(upper_ref)
            minus(inverse_ref)


def start_inverse(inverse_ref):
    rows = lax.broadcasted_iota(jnp.int32, inverse_ref.shape, 0)
    cols = lax.broadcasted_iota(jnp.int32, inverse_ref.shape, 1)
    inverse_ref[...] = jnp.where(rows == cols, 1.0, 0.0)


def keep_upper(upper_ref):
    rows = lax.broadcasted_iota(jnp.int32, upper_ref.shape, 0)
    cols = lax.broadcasted_iota(jnp.int32, upper_ref.shape, 1)
    upper_ref[...] = jnp.where(rows <= cols, upper_ref[...], 0.0)


def solve_twice(inverse_ref, projected_ref):
    half = jnp.sum(inverse_ref[...] * projected_ref[...], axis=1, keepdims=True)
    return jnp.sum(inverse_ref[...] * half, axis=0, keepdims=True)


def factor_kernel(gram_ref, projected_ref, upper_ref, inverse_ref, multipliers_ref):
    upper_ref[...] = gram_ref[...]
    start_inverse(inverse_ref)
    factor_steps(upper_ref, inverse_ref, 0, upper_ref.shape[0] // BLOCK)
    keep_upper(upper_ref)
    multipliers_ref[...] = solve_twice(inverse_ref, projected_ref)


def factor(gram, projected):
    order = gram.shape[0]
    return pl.pallas_call(
        factor_kernel,
        out_shape=(
            jax.ShapeDtypeStruct((order, order), jnp.float32),
            jax.ShapeDtypeStruct((order, order), jnp.float32),
            jax.ShapeDtypeStruct((1, order), jnp.float32),
        ),
        in_specs=[pl.BlockSpec(memory_space=pltpu.VMEM)] * 2,
        out_specs=[pl.BlockSpec(memory_space=pltpu.VMEM)] * 3,
        compiler_params=pltpu.CompilerParams(vmem_limit_bytes=LIMIT),
        cost_estimate=pl.CostEstimate(
            flops=6 * order**3, bytes_accessed=12 * order**2, transcendentals=0
        ),
    )(gram, projected)


def features_kernel(field_ref, north_ref, south_ref, out_ref):
    field = field_ref[...]
    rows, width = field.shape
    lanes = lax.broadcasted_iota(jnp.int32, field.shape, 1)
    north = jnp.concatenate([north_ref[...], field[:-1]], axis=0)
    south = jnp.concatenate([field[1:], south_ref[...]], axis=0)
    west = jnp.where(lanes == 0, 0.0, pltpu.roll(field, 1, 1))
    east = jnp.where(lanes == width - 1, 0.0, pltpu.roll(field, width - 1, 1))
    laplace = 4.0 * field - (north + south + west + east)
    slope_x = 0.5 * (east - west)
    slope_y = 0.5 * (south - north)
    parts = []
    for stencil in (laplace, slope_x, slope_y):
        rest = stencil / TILE
        for _ in range(3):
            part = rest.astype(jnp.bfloat16).astype(jnp.float32)
            parts.append(part)
            rest = rest - part
    tiles = width // TILE
    shape = (FEATURES, width)
    owner = lax.broadcasted_iota(jnp.int32, shape, 0) // len(parts)
    tile = lax.broadcasted_iota(jnp.int32, shape, 1) // TILE
    blank = jnp.zeros((FEATURES - tiles * len(parts), width), jnp.float32)
    for row in range(rows):
        block = jnp.concatenate([part[row : row + 1] for part in parts], axis=0)
        whole = jnp.concatenate([block] * tiles + [blank], axis=0)
        out_ref[row] = jnp.where(owner == tile, whole, 0.0).astype(jnp.bfloat16)


def features(field, north, south):
    rows, width = field.shape
    return pl.pallas_call(
        features_kernel,
        out_shape=jax.ShapeDtypeStruct((rows, FEATURES, width), jnp.bfloat16),
        in_specs=[VMEM] * 3,
        out_specs=VMEM,
        compiler_params=pltpu.CompilerParams(vmem_limit_bytes=LIMIT),
        cost_estimate=BRIEF,
    )(field, north, south)


def assembled(base, feature, key, first):
    rows = lax.broadcasted_iota(jnp.int32, (FEATURES, key.shape[1]), 0) // 3 + first
    chooser = jnp.where(rows.astype(jnp.float32) == key, 1.0, 0.0).astype(jnp.bfloat16)
    added = lax.dot_general(
        feature, chooser, (((0,), (0,)), ((), ())), preferred_element_type=jnp.float32
    )
    return (base.astype(jnp.float32) + added).astype(jnp.bfloat16)


def transposed_dot(left, right):
    return lax.dot_general(
        left, right, (((0,), (0,)), ((), ())), preferred_element_type=jnp.float32
    )


def upper_blocks(order):
    count = order // BLOCK
    return [(a, b) for a in range(count) for b in range(a, count)]


def packed_rows(order):
    used = len(upper_blocks(order)) * BLOCK + order // BLOCK
    return -(-used // (8 * GROUP)) * 8 * GROUP


def own_kernel(
    place_ref, base_ref, feature_ref, key_ref, grad_ref, jac_ref, *refs
):
    outs = refs[:GROUP]
    gram, projected, packed = refs[GROUP:]
    step = pl.program_id(0)
    half = pl.num_programs(0) // 2
    order = base_ref.shape[1]
    jac = assembled(base_ref[...], feature_ref[0], key_ref[...], place_ref[2])

    @pl.when(step // half == place_ref[0])
    def _():
        jac_ref[...] = jac

    @pl.when(step == 0)
    def _():
        gram[...] = jnp.zeros_like(gram)
        projected[...] = jnp.zeros_like(projected)

    gram[...] += transposed_dot(jac, jac)
    projected[...] += jnp.dot(grad_ref[0], jac, preferred_element_type=jnp.float32)

    @pl.when(step == pl.num_programs(0) - 1)
    def _():
        packed[...] = jnp.zeros_like(packed)
        blocks = upper_blocks(order)
        for index, (a, b) in enumerate(blocks):
            packed[pl.ds(index * BLOCK, BLOCK), :] = gram[
                pl.ds(a * BLOCK, BLOCK), pl.ds(b * BLOCK, BLOCK)
            ]
        for c in range(order // BLOCK):
            packed[pl.ds(len(blocks) * BLOCK + c, 1), :] = projected[:, pl.ds(c * BLOCK, BLOCK)]
        size = outs[0].shape[0]
        for mask in range(GROUP):
            start = pl.multiple_of((place_ref[1] ^ mask) * size, 8)
            outs[mask][...] = packed[pl.ds(start, size), :]


def own_part(place, base, feature, key, gradient):
    cells, order = base.shape
    rows, width = gradient.shape
    half = rows // 2
    size = packed_rows(order) // GROUP
    return pl.pallas_call(
        own_kernel,
        grid_spec=pltpu.PrefetchScalarGridSpec(
            num_scalar_prefetch=1,
            grid=(rows,),
            in_specs=[
                pl.BlockSpec((width, order), lambda i, s: (i, 0)),
                pl.BlockSpec((1, FEATURES, width), lambda i, s: (i, 0, 0)),
                pl.BlockSpec((1, order), lambda i, s: (0, 0)),
                pl.BlockSpec((1, 1, width), lambda i, s: (i, 0, 0)),
            ],
            out_specs=[
                pl.BlockSpec(
                    (width, order), lambda i, s: (jnp.clip(i - s[0] * half, 0, half - 1), 0)
                )
            ]
            + [pl.BlockSpec((size, BLOCK), lambda i, s: (0, 0))] * GROUP,
            scratch_shapes=[
                pltpu.VMEM((order, order), jnp.float32),
                pltpu.VMEM((1, order), jnp.float32),
                pltpu.VMEM((GROUP * size, BLOCK), jnp.float32),
            ],
        ),
        out_shape=[jax.ShapeDtypeStruct((cells // 2, order), jnp.bfloat16)]
        + [jax.ShapeDtypeStruct((size, BLOCK), jnp.float32)] * GROUP,
        compiler_params=pltpu.CompilerParams(vmem_limit_bytes=WIDE_LIMIT),
        cost_estimate=BRIEF,
    )(place, base, feature, key, gradient.reshape(rows, 1, width))


def send_kernel(place_ref, base_ref, key_ref, out_ref):
    step = pl.program_id(0)
    height = base_ref.shape[0]
    out_ref[pl.ds(pl.multiple_of(step * height, height), height), :] = base_ref[...]

    @pl.when(step == 0)
    def _():
        key = jnp.broadcast_to(key_ref[...], (KEY_ROWS, key_ref.shape[1]))
        out_ref[pl.ds(pl.num_programs(0) * height, KEY_ROWS), :] = key.astype(jnp.bfloat16)


def send_part(place, base, key, rows, start, end):
    cells = base.shape[0]
    height, width = cells // rows, end - start
    half = rows // 2
    return pl.pallas_call(
        send_kernel,
        grid_spec=pltpu.PrefetchScalarGridSpec(
            num_scalar_prefetch=1,
            grid=(half,),
            in_specs=[
                pl.BlockSpec(
                    (height, width), lambda i, s: ((1 - s[0]) * half + i, start // width)
                ),
                pl.BlockSpec((1, width), lambda i, s: (0, start // width)),
            ],
            out_specs=VMEM,
        ),
        out_shape=jax.ShapeDtypeStruct((cells // 2 + KEY_ROWS, width), base.dtype),
        compiler_params=pltpu.CompilerParams(vmem_limit_bytes=WIDE_LIMIT + 2**23),
        cost_estimate=BRIEF,
    )(place, base, key)


def cross_kernel(place_ref, recv_ref, jac_ref, feature_ref, key_ref, *refs):
    outs = refs[-2 - GROUP : -2]
    total, out_ref = refs[-2:]
    step = pl.program_id(0)
    key = key_ref[0:1, :].astype(jnp.float32)
    other = assembled(recv_ref[...], feature_ref[0], key, place_ref[2])

    @pl.when(step == 0)
    def _():
        total[...] = jnp.zeros_like(total)

    total[...] += transposed_dot(other, jac_ref[...])
    count = total.shape[1] // BLOCK
    part = BLOCK // GROUP
    last = step == pl.num_programs(0) - 1

    blocks = total.shape[0] // BLOCK

    @pl.when(last & (place_ref[0] == 0))
    def _():
        for k in range(blocks):
            for q in range(GROUP):
                for c in range(count):
                    out_ref[q, pl.ds(BLOCK * k + part * c, part), :] = total[
                        pl.ds(BLOCK * k + part * q, part), pl.ds(BLOCK * c, BLOCK)
                    ]

    @pl.when(last & (place_ref[0] != 0))
    def _():
        for k in range(blocks):
            for c in range(count):
                block = total[pl.ds(BLOCK * k, BLOCK), pl.ds(BLOCK * c, BLOCK)].T
                for q in range(GROUP):
                    out_ref[q, pl.ds(BLOCK * k + part * c, part), :] = block[
                        part * q : part * q + part
                    ]

    @pl.when(last)
    def _():
        for mask in range(GROUP):
            outs[mask][...] = out_ref[place_ref[1] ^ mask]


def cross_part(place, recv, jac, feature, *after):
    cells, width_recv = jac.shape[0], recv.shape[1]
    order = jac.shape[1]
    rows, _, width = feature.shape
    steps = rows // 2
    return pl.pallas_call(
        cross_kernel,
        grid_spec=pltpu.PrefetchScalarGridSpec(
            num_scalar_prefetch=1,
            grid=(steps,),
            in_specs=[
                pl.BlockSpec((width, width_recv), lambda i, s: (i, 0)),
                pl.BlockSpec((width, order), lambda i, s: (i, 0)),
                pl.BlockSpec((1, FEATURES, width), lambda i, s: (s[0] * steps + i, 0, 0)),
                pl.BlockSpec((KEY_ROWS, width_recv), lambda i, s: (cells // KEY_ROWS, 0)),
            ]
            + [ANY] * len(after),
            out_specs=[pl.BlockSpec((width_recv, BLOCK), lambda i, s: (0, 0))] * GROUP,
            scratch_shapes=[
                pltpu.VMEM((width_recv, order), jnp.float32),
                pltpu.VMEM((GROUP, width_recv, BLOCK), jnp.float32),
            ],
        ),
        out_shape=[jax.ShapeDtypeStruct((width_recv, BLOCK), jnp.float32)] * GROUP,
        compiler_params=pltpu.CompilerParams(vmem_limit_bytes=LIMIT),
        cost_estimate=BRIEF,
    )(place, recv, jac, feature, recv, *after)


def swap(value, axis, mask):
    count = lax.axis_size(axis)
    return lax.ppermute(value, axis, [(i, i ^ mask) for i in range(count)])


def add_kernel(count, *refs):
    refs[-1][...] = sum(ref[...] for ref in refs[1:count]) + refs[0][...]


def add(values, *after):
    return pl.pallas_call(
        functools.partial(add_kernel, len(values)),
        out_shape=jax.ShapeDtypeStruct(values[0].shape, values[0].dtype),
        in_specs=[VMEM] * len(values) + [ANY] * len(after),
        out_specs=VMEM,
        compiler_params=pltpu.CompilerParams(vmem_limit_bytes=LIMIT),
        cost_estimate=BRIEF,
    )(*values, *after)


def group_swaps(parts):
    return [parts[0]] + [swap(parts[mask], "rows", mask) for mask in range(1, GROUP)]


def group_sum(parts):
    got = group_swaps(parts)
    return got[0] + got[1] + got[2] + got[3]


def groups_sum(held):
    masks = range(GROUP, lax.axis_size("rows"), GROUP)
    return held + sum(swap(held, "rows", mask) for mask in masks)


def doubled(held, masks):
    for mask in masks:
        held = held + swap(held, "rows", mask)
    return held


def rows_gather(own):
    return [own] + [swap(own, "rows", mask) for mask in range(1, GROUP)]


def first_factor_kernel(last, place_ref, *refs):
    pieces = refs[:GROUP]
    upper_ref, inverse_ref, projected_ref, whole = refs[GROUP + 1 :]
    size = pieces[0].shape[0]
    for mask in range(GROUP):
        start = pl.multiple_of((place_ref[1] ^ mask) * size, 8)
        whole[pl.ds(start, size), :] = pieces[mask][...]
    order = upper_ref.shape[0]
    blocks = upper_blocks(order)
    upper_ref[...] = jnp.zeros_like(upper_ref)
    for index, (a, b) in enumerate(blocks):
        upper_ref[pl.ds(a * BLOCK, BLOCK), pl.ds(b * BLOCK, BLOCK)] = whole[
            pl.ds(index * BLOCK, BLOCK), :
        ]
    for c in range(order // BLOCK):
        projected_ref[:, pl.ds(c * BLOCK, BLOCK)] = whole[pl.ds(len(blocks) * BLOCK + c, 1), :]
    start_inverse(inverse_ref)
    factor_steps(upper_ref, inverse_ref, 0, last)


def square(order):
    return jax.ShapeDtypeStruct((order, order), jnp.float32)


def row(order):
    return jax.ShapeDtypeStruct((1, order), jnp.float32)


def first_factor(place, pieces, order, last, after):
    return pl.pallas_call(
        functools.partial(first_factor_kernel, last),
        out_shape=(square(order), square(order), row(order)),
        in_specs=[SMEM] + [VMEM] * GROUP + [ANY],
        out_specs=[VMEM] * 3,
        scratch_shapes=[pltpu.VMEM((packed_rows(order), BLOCK), jnp.float32)],
        compiler_params=pltpu.CompilerParams(vmem_limit_bytes=LIMIT),
        cost_estimate=BRIEF,
    )(place, *pieces, after)


def more_factor_kernel(first, last, upper_in, inverse_in, _, upper_ref, inverse_ref, *packed):
    upper_ref[...] = upper_in[...]
    inverse_ref[...] = inverse_in[...]
    factor_steps(upper_ref, inverse_ref, first, last)
    for ref in packed:
        pack_rows(ref, inverse_ref, lower_blocks(upper_ref.shape[0])[: early(last)])


def more_factor(upper, inverse, first, last, after, cost, packed=False):
    order = upper.shape[0]
    extra = [jax.ShapeDtypeStruct((early(last) * BLOCK, BLOCK), jnp.float32)] if packed else []
    return pl.pallas_call(
        functools.partial(more_factor_kernel, first, last),
        out_shape=[square(order), square(order)] + extra,
        in_specs=[VMEM] * 2 + [ANY],
        out_specs=[VMEM] * (2 + len(extra)),
        compiler_params=pltpu.CompilerParams(vmem_limit_bytes=LIMIT),
        cost_estimate=cost,
    )(upper, inverse, after)


def last_factor_kernel(first, upper_in, inverse_in, projected, _, upper_ref, inverse_ref, out_ref):
    upper_ref[...] = upper_in[...]
    inverse_ref[...] = inverse_in[...]
    factor_steps(upper_ref, inverse_ref, first, upper_ref.shape[0] // BLOCK)
    keep_upper(upper_ref)
    out_ref[...] = solve_twice(inverse_ref, projected)


def last_factor(upper, inverse, projected, first, after, cost):
    order = upper.shape[0]
    return pl.pallas_call(
        functools.partial(last_factor_kernel, first),
        out_shape=(square(order), square(order), row(order)),
        in_specs=[VMEM] * 3 + [ANY],
        out_specs=[VMEM] * 3,
        compiler_params=pltpu.CompilerParams(vmem_limit_bytes=LIMIT),
        cost_estimate=cost,
    )(upper, inverse, projected, after)


def lower_blocks(order):
    return [(a, b) for a in range(order // BLOCK) for b in range(a + 1)]


def early(step):
    return step * (step + 1) // 2


def pack_rows(packed_ref, inverse_ref, blocks):
    for index, (a, b) in enumerate(blocks):
        packed_ref[pl.ds(index * BLOCK, BLOCK), :] = inverse_ref[
            pl.ds(a * BLOCK, BLOCK), pl.ds(b * BLOCK, BLOCK)
        ]


def pack_kernel(step, inverse_ref, solved_ref, _, packed_ref):
    order = inverse_ref.shape[0]
    blocks = lower_blocks(order)[early(step) :]
    pack_rows(packed_ref, inverse_ref, blocks)
    start = len(blocks) * BLOCK
    packed_ref[pl.ds(start, 8), :] = jnp.zeros((8, BLOCK), jnp.float32)
    for c in range(order // BLOCK):
        packed_ref[pl.ds(start + c, 1), :] = solved_ref[:, pl.ds(c * BLOCK, BLOCK)]


def pack(inverse, solved, step, after):
    order = inverse.shape[0]
    blocks = len(lower_blocks(order)) - early(step)
    return pl.pallas_call(
        functools.partial(pack_kernel, step),
        out_shape=jax.ShapeDtypeStruct((blocks * BLOCK + 8, BLOCK), jnp.float32),
        in_specs=[VMEM] * 2 + [ANY],
        out_specs=VMEM,
        compiler_params=pltpu.CompilerParams(vmem_limit_bytes=LIMIT),
        cost_estimate=BRIEF,
    )(inverse, solved, after)


def finish_kernel(place_ref, upper_ref, packed_first, packed_last, *refs):
    pieces = refs[:GROUP]
    out_ref, cross, inverse = refs[GROUP:]
    order = upper_ref.shape[0]
    part = BLOCK // GROUP

    @pl.when(place_ref[0] == 0)
    def _():
        out_ref[...] = upper_ref[...]

    @pl.when(place_ref[0] != 0)
    def _():
        for mask in range(GROUP):
            quarter = place_ref[1] ^ mask
            for b in range(order // BLOCK):
                start = pl.multiple_of(BLOCK * b + part * quarter, part)
                cross[pl.ds(start, part), :] = pieces[mask][pl.ds(part * b, part), :]
        done = packed_first.shape[0] // BLOCK
        for index, (a, b) in enumerate(lower_blocks(order)):
            source = packed_first if index < done else packed_last
            inverse[pl.ds(a * BLOCK, BLOCK), pl.ds(b * BLOCK, BLOCK)] = source[
                pl.ds(index % done * BLOCK, BLOCK), :
            ]
        for a in range(order // BLOCK):
            rows, depth = pl.ds(a * BLOCK, BLOCK), (a + 1) * BLOCK
            out_ref[rows, :] = lax.dot_general(
                inverse[rows, pl.ds(0, depth)],
                cross[:, pl.ds(0, depth)],
                (((1,), (1,)), ((), ())),
                precision=HIGHEST,
                preferred_element_type=jnp.float32,
            )


def finish(place, upper, packed_first, packed_last, pieces):
    order = upper.shape[0]
    return pl.pallas_call(
        finish_kernel,
        out_shape=square(order),
        in_specs=[SMEM] + [VMEM] * (3 + GROUP),
        out_specs=VMEM,
        scratch_shapes=[pltpu.VMEM((order, order), jnp.float32)] * 2,
        compiler_params=pltpu.CompilerParams(vmem_limit_bytes=LIMIT),
        cost_estimate=BRIEF,
    )(place, upper, packed_first, packed_last, *pieces)


def shards(sens_base, design_field, gradient, tile_index, type_codes):
    cells, order = sens_base.shape
    rows_here, width = design_field.shape
    side = lax.axis_index("cols")
    quarter = lax.axis_index("rows") % GROUP
    tiles = width // TILE
    first_tile = lax.axis_index("rows") * rows_here // TILE * tiles
    place = jnp.stack([side, quarter, 3 * first_tile]).astype(jnp.int32)
    key = (tile_index * 3 + type_codes)[None, :].astype(jnp.float32)

    cuts = [BLOCK * sum(STAGES[:s]) for s in range(len(STAGES) + 1)]
    received = [
        swap(send_part(place, sens_base, key, rows_here, start, end), "cols", 1)
        for start, end in zip(cuts, cuts[1:])
    ]

    count = lax.axis_size("rows")
    north = lax.ppermute(design_field[-1:], "rows", [(i, i + 1) for i in range(count - 1)])
    south = lax.ppermute(design_field[:1], "rows", [(i + 1, i) for i in range(count - 1)])
    feature = features(design_field, north, south)
    jac, *packed = own_part(place, sens_base, feature, key, gradient)
    pieces = rows_gather(groups_sum(group_sum(packed)))

    def stage(index, *after):
        return cross_part(place, received[index], jac, feature, *after)

    first = stage(0, *pieces[1:])
    shares = group_swaps(first)
    upper, inverse, projected = first_factor(place, pieces, order, 1, first[0])
    held = add(shares, inverse)
    upper, inverse = more_factor(upper, inverse, 1, 2, held, BRIEF)
    middle = doubled(held, [GROUP])
    last = stage(1, inverse, middle)
    shares = group_swaps(last)
    upper, inverse, packed = more_factor(upper, inverse, 2, 3, last[0], LONG, True)
    packed_first = lax.ppermute(packed, "cols", [(0, 1)])
    held_last = add(shares, inverse)
    masks = range(GROUP, count, GROUP)
    shares = [held_last] + [swap(held_last, "rows", mask) for mask in masks]
    upper, inverse, solved = last_factor(upper, inverse, projected, 3, held_last, LONG)
    far = range(2 * GROUP, count, 2 * GROUP)
    sums = [
        middle + sum(swap(middle, "rows", mask) for mask in far),
        add(shares, solved, packed_first),
    ]
    others = [lax.ppermute(value, "cols", [(0, 1)]) for value in sums]
    packed = pack(inverse, solved, 3, others[1])
    packed_last = lax.ppermute(packed, "cols", [(0, 1)])

    part = BLOCK // GROUP
    blocks = order // BLOCK

    def cut(values, block, c):
        index = max(s for s in range(len(STAGES)) if cuts[s] <= block * BLOCK)
        start = block * BLOCK - cuts[index] + c * part
        return values[index][start : start + part]

    cross = jnp.concatenate(
        [
            jnp.concatenate(
                [cut(sums, a, b) + cut(others, b, a) for a in range(blocks)], axis=1
            )
            for b in range(blocks)
        ],
        axis=0,
    )
    r_panels = finish(place, upper, packed_first, packed_last, rows_gather(cross))
    multipliers = jnp.where(side == 0, packed[-8:], packed_last[-8:])
    return (r_panels, multipliers[:blocks].reshape(-1))


def shards_general(sens_base, design_field, gradient, tile_index, type_codes):
    rows_here = design_field.shape[0]
    grid_width = design_field.shape[1]
    cols_here = sens_base.shape[1]
    factored = 2 * PW
    padded = padded_2(design_field, (("rows", 0),), 1)
    padded = jnp.pad(padded, ((0, 0), (1, 1)))
    north_cells = padded[:-2, 1:-1]
    south_cells = padded[2:, 1:-1]
    west_cells = padded[1:-1, :-2]
    east_cells = padded[1:-1, 2:]
    laplace = 4.0 * design_field - (north_cells + south_cells + west_cells + east_cells)
    slope_x = 0.5 * (east_cells - west_cells)
    slope_y = 0.5 * (south_cells - north_cells)
    stencils = jnp.stack([laplace, slope_x, slope_y]).reshape(3, -1)
    row_glob = lax.axis_index("rows") * rows_here + jnp.arange(rows_here, dtype=jnp.int32)
    col_ids = jnp.arange(grid_width, dtype=jnp.int32) // TILE
    cell_tile = ((row_glob // TILE)[:, None] * (grid_width // TILE) + col_ids[None, :]).reshape(-1)
    local_jac = assemble(sens_base, tile_index, type_codes, stencils, cell_tile)
    grad_flat = gradient.reshape(-1)
    row_major = lax.all_to_all(local_jac, "cols", split_axis=0, concat_axis=1, tiled=True)
    row_piece = row_major.shape[0]
    grad_part = lax.dynamic_slice_in_dim(
        grad_flat, lax.axis_index("cols") * row_piece, row_piece, 0
    )
    leading = row_major[:, :factored]
    gram_block = lax.dot_general(
        leading, row_major, (((0,), (0,)), ((), ())), preferred_element_type=jnp.float32
    )
    projected = jnp.dot(grad_part, leading, preferred_element_type=jnp.float32)
    gram_block, projected = lax.psum((gram_block, projected), ("rows", "cols"))
    gram_head = gram_block[:, :factored]
    gram_own = lax.dynamic_slice_in_dim(
        gram_block, lax.axis_index("cols") * cols_here, cols_here, 1
    )
    _, inverse, multipliers = factor(gram_head, projected[None, :])
    r_panels = matmul(inverse, gram_own)
    return (r_panels, multipliers[0])


def solution(mesh):
    placed = (P("rows", "cols"), P("rows", None), P("rows", None), P("cols"), P("cols"))
    pairs = mesh.shape["cols"] == 2 and mesh.shape["rows"] in (8, 16, 32, 64)
    return jax.shard_map(
        shards if pairs else shards_general,
        mesh=mesh,
        in_specs=placed,
        out_specs=(P(None, "cols"), P()),
        check_vma=False,
    )
```

```python
import functools

import jax
import jax.numpy as jnp
from jax import lax
from jax.experimental import pallas as pl
from jax.experimental.pallas import tpu as pltpu
from jax.sharding import PartitionSpec as P

TILE = 128
PW = 256
BLOCK = 128
FEATURES = 80
KEY_ROWS = 16
SEND_CUTS = 4
GROUP = 4
HIGHEST = lax.Precision.HIGHEST
VMEM = pl.BlockSpec(memory_space=pltpu.VMEM)
SMEM = pl.BlockSpec(memory_space=pltpu.SMEM)
LIMIT = 12 * 2**20
WIDE_LIMIT = 48 * 2**20
ANY = pl.BlockSpec(memory_space=pl.ANY)
STAGES = (3, 1)
LONG = pl.CostEstimate(flops=8 * 10**9, bytes_accessed=1000, transcendentals=0)
BRIEF = pl.CostEstimate(flops=1000, bytes_accessed=1000, transcendentals=0)


def padded_2(cells, sides, width):
    for axis, dim in sides:
        count = lax.axis_size(axis)
        ends = count - 1
        head = lax.slice_in_dim(cells, 0, width, axis=dim)
        tail = lax.slice_in_dim(cells, cells.shape[dim] - width, cells.shape[dim], axis=dim)
        cells = jnp.concatenate(
            [
                lax.ppermute(tail, axis, [(i, (i + 1) % count) for i in range(ends)]),
                cells,
                lax.ppermute(head, axis, [((i + 1) % count, i) for i in range(ends)]),
            ],
            axis=dim,
        )
    return cells


def assemble(base_cols, tile_cols, type_cols, stencils, cell_tile):
    kinds_all = jnp.arange(3, dtype=jnp.int32)
    chooser = (type_cols[None, :] == kinds_all[:, None]).astype(jnp.float32)
    picked = lax.dot_general(
        stencils,
        chooser,
        (((0,), (0,)), ((), ())),
        precision=lax.Precision.HIGHEST,
        preferred_element_type=jnp.float32,
    )
    inside = cell_tile[:, None] == tile_cols[None, :]
    total = base_cols.astype(jnp.float32) + jnp.where(inside, picked / TILE, 0.0)
    return total.astype(jnp.bfloat16)


def matmul(left, right):
    return jnp.dot(left, right, precision=HIGHEST, preferred_element_type=jnp.float32)


def inverse_root(value):
    guess = lax.rsqrt(value)
    return guess * (1.5 - 0.5 * value * guess * guess)


def reciprocal(value):
    guess = pl.reciprocal(value, approx=True)
    guess = guess * (2.0 - value * guess)
    return guess * (2.0 - value * guess)


def lane(part, index):
    return jnp.broadcast_to(part[:, index : index + 1], part.shape)


def sublane(part, index):
    return jnp.broadcast_to(part[index : index + 1, :], part.shape)


def diagonal_inverse(block):
    groups = BLOCK // 8
    shape = (8, BLOCK)
    lanes = lax.broadcasted_iota(jnp.int32, shape, 1)
    subs = lax.broadcasted_iota(jnp.int32, shape, 0)
    parts = [block[8 * g : 8 * g + 8, :] for g in range(groups)]
    whole = []
    for p in range(groups):
        part, first = parts[p], 8 * p
        cols = [lane(part, first + k) for k in range(8)]
        inv = [None] * 8
        low = [jnp.zeros(shape, jnp.float32) for _ in range(8)]
        pivots = jnp.ones(shape, jnp.float32)
        for j in range(8):
            here = subs == j
            pivot = sublane(cols[j], j)
            ratio = reciprocal(pivot)
            pivots = jnp.where(here, pivot, pivots)
            for k in range(j):
                low[k] = jnp.where(here, inv[k], low[k])
            low[j] = jnp.where(here, 1.0, low[j])
            column = cols[j]
            for k in range(j + 1, 8):
                row = sublane(cols[k], j) * ratio
                cols[k] = jnp.where(here, row, cols[k] - column * row)
            for k in range(j):
                row = sublane(inv[k], j) * ratio
                inv[k] = jnp.where(here, row, inv[k] - column * row)
            inv[j] = jnp.where(here, ratio, -column * ratio)
        scale = inverse_root(pivots)
        inside = (lanes >= first) & (lanes < first + 8)
        unit = jnp.where(lanes - first == subs, 1.0, 0.0)
        rows = jnp.where(inside, unit, part)
        spread = [sublane(rows, k) for k in range(8)]
        solved = sum(low[k] * spread[k] for k in range(8)) * scale
        whole.append(jnp.where(lanes < first + 8, solved, 0.0))
        if p + 1 < groups:
            step = sum(inv[k] * spread[k] for k in range(8))
            step = [sublane(step, k) for k in range(8)]
            for g in range(p + 1, groups):
                taken = sum(lane(parts[g], first + k) * step[k] for k in range(8))
                parts[g] = jnp.where(inside, 0.0, parts[g]) - taken
    return jnp.concatenate(whole, axis=0)


def factor_steps(upper_ref, inverse_ref, first, last):
    blocks = upper_ref.shape[0] // BLOCK

    @pl.loop(first, last)
    def _(step):
        mine = pl.ds(pl.multiple_of(step * BLOCK, BLOCK), BLOCK)
        small = diagonal_inverse(upper_ref[mine, mine])
        upper_ref[mine, :] = matmul(small, upper_ref[mine, :])
        inverse_ref[mine, :] = matmul(small, inverse_ref[mine, :])

        @pl.loop(step + 1, blocks)
        def _(later):
            theirs = pl.ds(pl.multiple_of(later * BLOCK, BLOCK), BLOCK)
            factor = upper_ref[mine, theirs]

            def minus(target):
                target[theirs, :] -= lax.dot_general(
                    factor,
                    target[mine, :],
                    (((0,), (0,)), ((), ())),
                    precision=HIGHEST,
                    preferred_element_type=jnp.float32,
                )

            minus(upper_ref)
            minus(inverse_ref)


def start_inverse(inverse_ref):
    rows = lax.broadcasted_iota(jnp.int32, inverse_ref.shape, 0)
    cols = lax.broadcasted_iota(jnp.int32, inverse_ref.shape, 1)
    inverse_ref[...] = jnp.where(rows == cols, 1.0, 0.0)


def keep_upper(upper_ref):
    rows = lax.broadcasted_iota(jnp.int32, upper_ref.shape, 0)
    cols = lax.broadcasted_iota(jnp.int32, upper_ref.shape, 1)
    upper_ref[...] = jnp.where(rows <= cols, upper_ref[...], 0.0)


def solve_twice(inverse_ref, projected_ref):
    half = jnp.sum(inverse_ref[...] * projected_ref[...], axis=1, keepdims=True)
    return jnp.sum(inverse_ref[...] * half, axis=0, keepdims=True)


def factor_kernel(gram_ref, projected_ref, upper_ref, inverse_ref, multipliers_ref):
    upper_ref[...] = gram_ref[...]
    start_inverse(inverse_ref)
    factor_steps(upper_ref, inverse_ref, 0, upper_ref.shape[0] // BLOCK)
    keep_upper(upper_ref)
    multipliers_ref[...] = solve_twice(inverse_ref, projected_ref)


def factor(gram, projected):
    order = gram.shape[0]
    return pl.pallas_call(
        factor_kernel,
        out_shape=(
            jax.ShapeDtypeStruct((order, order), jnp.float32),
            jax.ShapeDtypeStruct((order, order), jnp.float32),
            jax.ShapeDtypeStruct((1, order), jnp.float32),
        ),
        in_specs=[pl.BlockSpec(memory_space=pltpu.VMEM)] * 2,
        out_specs=[pl.BlockSpec(memory_space=pltpu.VMEM)] * 3,
        compiler_params=pltpu.CompilerParams(vmem_limit_bytes=LIMIT),
        cost_estimate=pl.CostEstimate(
            flops=6 * order**3, bytes_accessed=12 * order**2, transcendentals=0
        ),
    )(gram, projected)


def features_kernel(field_ref, north_ref, south_ref, out_ref):
    field = field_ref[...]
    rows, width = field.shape
    lanes = lax.broadcasted_iota(jnp.int32, field.shape, 1)
    north = jnp.concatenate([north_ref[...], field[:-1]], axis=0)
    south = jnp.concatenate([field[1:], south_ref[...]], axis=0)
    west = jnp.where(lanes == 0, 0.0, pltpu.roll(field, 1, 1))
    east = jnp.where(lanes == width - 1, 0.0, pltpu.roll(field, width - 1, 1))
    laplace = 4.0 * field - (north + south + west + east)
    slope_x = 0.5 * (east - west)
    slope_y = 0.5 * (south - north)
    parts = []
    for stencil in (laplace, slope_x, slope_y):
        rest = stencil / TILE
        for _ in range(3):
            part = rest.astype(jnp.bfloat16).astype(jnp.float32)
            parts.append(part)
            rest = rest - part
    tiles = width // TILE
    shape = (FEATURES, width)
    owner = lax.broadcasted_iota(jnp.int32, shape, 0) // len(parts)
    tile = lax.broadcasted_iota(jnp.int32, shape, 1) // TILE
    blank = jnp.zeros((FEATURES - tiles * len(parts), width), jnp.float32)
    for row in range(rows):
        block = jnp.concatenate([part[row : row + 1] for part in parts], axis=0)
        whole = jnp.concatenate([block] * tiles + [blank], axis=0)
        out_ref[row] = jnp.where(owner == tile, whole, 0.0).astype(jnp.bfloat16)


def features(field, north, south):
    rows, width = field.shape
    return pl.pallas_call(
        features_kernel,
        out_shape=jax.ShapeDtypeStruct((rows, FEATURES, width), jnp.bfloat16),
        in_specs=[VMEM] * 3,
        out_specs=VMEM,
        compiler_params=pltpu.CompilerParams(vmem_limit_bytes=LIMIT),
        cost_estimate=BRIEF,
    )(field, north, south)


def assembled(base, feature, key, first):
    rows = lax.broadcasted_iota(jnp.int32, (FEATURES, key.shape[1]), 0) // 3 + first
    chooser = jnp.where(rows.astype(jnp.float32) == key, 1.0, 0.0).astype(jnp.bfloat16)
    added = lax.dot_general(
        feature, chooser, (((0,), (0,)), ((), ())), preferred_element_type=jnp.float32
    )
    return (base.astype(jnp.float32) + added).astype(jnp.bfloat16)


def transposed_dot(left, right):
    return lax.dot_general(
        left, right, (((0,), (0,)), ((), ())), preferred_element_type=jnp.float32
    )


def upper_blocks(order):
    count = order // BLOCK
    return [(a, b) for a in range(count) for b in range(a, count)]


def packed_rows(order):
    used = len(upper_blocks(order)) * BLOCK + order // BLOCK
    return -(-used // (8 * GROUP)) * 8 * GROUP


def own_kernel(
    place_ref, base_ref, feature_ref, key_ref, grad_ref, jac_ref, *refs
):
    outs = refs[:GROUP]
    gram, projected, packed = refs[GROUP:]
    step = pl.program_id(0)
    half = pl.num_programs(0) // 2
    order = base_ref.shape[1]
    jac = assembled(base_ref[...], feature_ref[0], key_ref[...], place_ref[2])

    @pl.when(step // half == place_ref[0])
    def _():
        jac_ref[...] = jac

    @pl.when(step == 0)
    def _():
        gram[...] = jnp.zeros_like(gram)
        projected[...] = jnp.zeros_like(projected)

    middle = order // 2
    gram[:middle, :] += transposed_dot(jac[:, :middle], jac)
    gram[middle:, middle:] += transposed_dot(jac[:, middle:], jac[:, middle:])
    projected[...] += jnp.dot(grad_ref[0], jac, preferred_element_type=jnp.float32)

    @pl.when(step == pl.num_programs(0) - 1)
    def _():
        packed[...] = jnp.zeros_like(packed)
        blocks = upper_blocks(order)
        for index, (a, b) in enumerate(blocks):
            packed[pl.ds(index * BLOCK, BLOCK), :] = gram[
                pl.ds(a * BLOCK, BLOCK), pl.ds(b * BLOCK, BLOCK)
            ]
        for c in range(order // BLOCK):
            packed[pl.ds(len(blocks) * BLOCK + c, 1), :] = projected[:, pl.ds(c * BLOCK, BLOCK)]
        size = outs[0].shape[0]
        for mask in range(GROUP):
            start = pl.multiple_of((place_ref[1] ^ mask) * size, 8)
            outs[mask][...] = packed[pl.ds(start, size), :]


def own_part(place, base, feature, key, gradient):
    cells, order = base.shape
    rows, width = gradient.shape
    half = rows // 2
    size = packed_rows(order) // GROUP
    return pl.pallas_call(
        own_kernel,
        grid_spec=pltpu.PrefetchScalarGridSpec(
            num_scalar_prefetch=1,
            grid=(rows,),
            in_specs=[
                pl.BlockSpec((width, order), lambda i, s: (i, 0)),
                pl.BlockSpec((1, FEATURES, width), lambda i, s: (i, 0, 0)),
                pl.BlockSpec((1, order), lambda i, s: (0, 0)),
                pl.BlockSpec((1, 1, width), lambda i, s: (i, 0, 0)),
            ],
            out_specs=[
                pl.BlockSpec(
                    (width, order), lambda i, s: (jnp.clip(i - s[0] * half, 0, half - 1), 0)
                )
            ]
            + [pl.BlockSpec((size, BLOCK), lambda i, s: (0, 0))] * GROUP,
            scratch_shapes=[
                pltpu.VMEM((order, order), jnp.float32),
                pltpu.VMEM((1, order), jnp.float32),
                pltpu.VMEM((GROUP * size, BLOCK), jnp.float32),
            ],
        ),
        out_shape=[jax.ShapeDtypeStruct((cells // 2, order), jnp.bfloat16)]
        + [jax.ShapeDtypeStruct((size, BLOCK), jnp.float32)] * GROUP,
        compiler_params=pltpu.CompilerParams(vmem_limit_bytes=WIDE_LIMIT),
        cost_estimate=BRIEF,
    )(place, base, feature, key, gradient.reshape(rows, 1, width))


def send_kernel(cuts, place_ref, base_ref, key_ref, *refs):
    outs, sems = refs[:-1], refs[-1]
    half = base_ref.shape[0] // 2
    first = pl.multiple_of((1 - place_ref[0]) * half, KEY_ROWS)
    piece = half // SEND_CUTS
    copies = []
    for start, end, out in zip(cuts, cuts[1:], outs):
        cols = pl.ds(start, end - start)
        sources = [(key_ref.at[:, cols], out.at[pl.ds(half, KEY_ROWS), :])]
        for k in range(SEND_CUTS):
            rows = pl.ds(first + k * piece, piece)
            sources.append((base_ref.at[rows, cols], out.at[pl.ds(k * piece, piece), :]))
        for source, target in sources:
            copies.append(pltpu.make_async_copy(source, target, sems.at[len(copies)]))
    for copy in copies:
        copy.start()
    for copy in copies:
        copy.wait()


def send_parts(place, base, key, cuts):
    rows = base.shape[0] // 2 + KEY_ROWS
    return pl.pallas_call(
        functools.partial(send_kernel, tuple(cuts)),
        out_shape=[
            jax.ShapeDtypeStruct((rows, end - start), base.dtype)
            for start, end in zip(cuts, cuts[1:])
        ],
        in_specs=[SMEM, ANY, ANY],
        out_specs=[ANY] * (len(cuts) - 1),
        scratch_shapes=[pltpu.SemaphoreType.DMA(((len(cuts) - 1) * (SEND_CUTS + 1),))],
        compiler_params=pltpu.CompilerParams(vmem_limit_bytes=WIDE_LIMIT + 2**23),
        cost_estimate=BRIEF,
    )(place, base, key)


def cross_kernel(place_ref, recv_ref, jac_ref, feature_ref, key_ref, *refs):
    outs = refs[-2 - GROUP : -2]
    total, out_ref = refs[-2:]
    step = pl.program_id(0)
    key = key_ref[0:1, :].astype(jnp.float32)
    other = assembled(recv_ref[...], feature_ref[0], key, place_ref[2])

    @pl.when(step == 0)
    def _():
        total[...] = jnp.zeros_like(total)

    total[...] += transposed_dot(other, jac_ref[...])
    count = total.shape[1] // BLOCK
    part = BLOCK // GROUP
    last = step == pl.num_programs(0) - 1

    blocks = total.shape[0] // BLOCK

    @pl.when(last & (place_ref[0] == 0))
    def _():
        for k in range(blocks):
            for q in range(GROUP):
                for c in range(count):
                    out_ref[q, pl.ds(BLOCK * k + part * c, part), :] = total[
                        pl.ds(BLOCK * k + part * q, part), pl.ds(BLOCK * c, BLOCK)
                    ]

    @pl.when(last & (place_ref[0] != 0))
    def _():
        for k in range(blocks):
            for c in range(count):
                block = total[pl.ds(BLOCK * k, BLOCK), pl.ds(BLOCK * c, BLOCK)].T
                for q in range(GROUP):
                    out_ref[q, pl.ds(BLOCK * k + part * c, part), :] = block[
                        part * q : part * q + part
                    ]

    @pl.when(last)
    def _():
        for mask in range(GROUP):
            outs[mask][...] = out_ref[place_ref[1] ^ mask]


def cross_part(place, recv, jac, feature, *after):
    cells, width_recv = jac.shape[0], recv.shape[1]
    order = jac.shape[1]
    rows, _, width = feature.shape
    steps = rows // 2
    return pl.pallas_call(
        cross_kernel,
        grid_spec=pltpu.PrefetchScalarGridSpec(
            num_scalar_prefetch=1,
            grid=(steps,),
            in_specs=[
                pl.BlockSpec((width, width_recv), lambda i, s: (i, 0)),
                pl.BlockSpec((width, order), lambda i, s: (i, 0)),
                pl.BlockSpec((1, FEATURES, width), lambda i, s: (s[0] * steps + i, 0, 0)),
                pl.BlockSpec((KEY_ROWS, width_recv), lambda i, s: (cells // KEY_ROWS, 0)),
            ]
            + [ANY] * len(after),
            out_specs=[pl.BlockSpec((width_recv, BLOCK), lambda i, s: (0, 0))] * GROUP,
            scratch_shapes=[
                pltpu.VMEM((width_recv, order), jnp.float32),
                pltpu.VMEM((GROUP, width_recv, BLOCK), jnp.float32),
            ],
        ),
        out_shape=[jax.ShapeDtypeStruct((width_recv, BLOCK), jnp.float32)] * GROUP,
        compiler_params=pltpu.CompilerParams(vmem_limit_bytes=LIMIT),
        cost_estimate=BRIEF,
    )(place, recv, jac, feature, recv, *after)


def swap(value, axis, mask):
    count = lax.axis_size(axis)
    return lax.ppermute(value, axis, [(i, i ^ mask) for i in range(count)])


def add_kernel(count, *refs):
    refs[-1][...] = sum(ref[...] for ref in refs[1:count]) + refs[0][...]


def add(values, *after):
    return pl.pallas_call(
        functools.partial(add_kernel, len(values)),
        out_shape=jax.ShapeDtypeStruct(values[0].shape, values[0].dtype),
        in_specs=[VMEM] * len(values) + [ANY] * len(after),
        out_specs=VMEM,
        compiler_params=pltpu.CompilerParams(vmem_limit_bytes=LIMIT),
        cost_estimate=BRIEF,
    )(*values, *after)


def add_pass_kernel(*refs):
    *values, passed_ref, out_ref, copy_ref = refs
    out_ref[...] = sum(ref[...] for ref in values[1:]) + values[0][...]
    copy_ref[...] = passed_ref[...]


def add_pass(values, passed):
    return pl.pallas_call(
        add_pass_kernel,
        out_shape=[jax.ShapeDtypeStruct(v.shape, v.dtype) for v in (values[0], passed)],
        in_specs=[VMEM] * (len(values) + 1),
        out_specs=[VMEM] * 2,
        compiler_params=pltpu.CompilerParams(vmem_limit_bytes=LIMIT),
        cost_estimate=BRIEF,
    )(*values, passed)


def stacked_kernel(count, *refs):
    first, second, out_ref = refs[:count], refs[count:-1], refs[-1]
    rows = first[0].shape[0]
    out_ref[:rows, :] = sum(ref[...] for ref in first[1:]) + first[0][...]
    out_ref[rows:, :] = sum(ref[...] for ref in second[1:]) + second[0][...]


def stacked(first, second):
    rows = first[0].shape[0] + second[0].shape[0]
    return pl.pallas_call(
        functools.partial(stacked_kernel, len(first)),
        out_shape=jax.ShapeDtypeStruct((rows, BLOCK), jnp.float32),
        in_specs=[VMEM] * (len(first) + len(second)),
        out_specs=VMEM,
        compiler_params=pltpu.CompilerParams(vmem_limit_bytes=LIMIT),
        cost_estimate=BRIEF,
    )(*first, *second)


def joined_kernel(own_ref, other_ref, out_ref):
    part = BLOCK // GROUP
    blocks = own_ref.shape[0] // BLOCK
    for a in range(blocks):
        for b in range(blocks):
            out_ref[pl.ds(part * b, part), pl.ds(BLOCK * a, BLOCK)] = (
                own_ref[pl.ds(BLOCK * a + part * b, part), :]
                + other_ref[pl.ds(BLOCK * b + part * a, part), :]
            )


def joined(own, other):
    order = own.shape[0]
    return pl.pallas_call(
        joined_kernel,
        out_shape=jax.ShapeDtypeStruct((order // GROUP, order), jnp.float32),
        in_specs=[VMEM] * 2,
        out_specs=VMEM,
        compiler_params=pltpu.CompilerParams(vmem_limit_bytes=LIMIT),
        cost_estimate=BRIEF,
    )(own, other)


def group_swaps(parts):
    return [parts[0]] + [swap(parts[mask], "rows", mask) for mask in range(1, GROUP)]


def group_sum(parts):
    got = group_swaps(parts)
    return got[0] + got[1] + got[2] + got[3]


def groups_sum(held):
    masks = range(GROUP, lax.axis_size("rows"), GROUP)
    return held + sum(swap(held, "rows", mask) for mask in masks)


def doubled(held, masks):
    for mask in masks:
        held = held + swap(held, "rows", mask)
    return held


def rows_gather(own):
    return [own] + [swap(own, "rows", mask) for mask in range(1, GROUP)]


def first_factor_kernel(last, place_ref, *refs):
    pieces = refs[:GROUP]
    upper_ref, inverse_ref, projected_ref, whole = refs[GROUP + 1 :]
    size = pieces[0].shape[0]
    for mask in range(GROUP):
        start = pl.multiple_of((place_ref[1] ^ mask) * size, 8)
        whole[pl.ds(start, size), :] = pieces[mask][...]
    order = upper_ref.shape[0]
    blocks = upper_blocks(order)
    upper_ref[...] = jnp.zeros_like(upper_ref)
    for index, (a, b) in enumerate(blocks):
        upper_ref[pl.ds(a * BLOCK, BLOCK), pl.ds(b * BLOCK, BLOCK)] = whole[
            pl.ds(index * BLOCK, BLOCK), :
        ]
    for c in range(order // BLOCK):
        projected_ref[:, pl.ds(c * BLOCK, BLOCK)] = whole[pl.ds(len(blocks) * BLOCK + c, 1), :]
    start_inverse(inverse_ref)
    factor_steps(upper_ref, inverse_ref, 0, last)


def square(order):
    return jax.ShapeDtypeStruct((order, order), jnp.float32)


def row(order):
    return jax.ShapeDtypeStruct((1, order), jnp.float32)


def first_factor(place, pieces, order, last, after):
    return pl.pallas_call(
        functools.partial(first_factor_kernel, last),
        out_shape=(square(order), square(order), row(order)),
        in_specs=[SMEM] + [VMEM] * GROUP + [ANY],
        out_specs=[VMEM] * 3,
        scratch_shapes=[pltpu.VMEM((packed_rows(order), BLOCK), jnp.float32)],
        compiler_params=pltpu.CompilerParams(vmem_limit_bytes=LIMIT),
        cost_estimate=BRIEF,
    )(place, *pieces, after)


def more_factor_kernel(first, last, upper_in, inverse_in, _, upper_ref, inverse_ref):
    upper_ref[...] = upper_in[...]
    inverse_ref[...] = inverse_in[...]
    factor_steps(upper_ref, inverse_ref, first, last)


def more_factor(upper, inverse, first, last, after, cost):
    order = upper.shape[0]
    return pl.pallas_call(
        functools.partial(more_factor_kernel, first, last),
        out_shape=[square(order)] * 2,
        in_specs=[VMEM] * 2 + [ANY],
        out_specs=[VMEM] * 2,
        compiler_params=pltpu.CompilerParams(vmem_limit_bytes=LIMIT),
        cost_estimate=cost,
    )(upper, inverse, after)


def lower_blocks(order):
    return [(a, b) for a in range(order // BLOCK) for b in range(a + 1)]


def lower_half(order):
    rows = len(lower_blocks(order)) * BLOCK + order // BLOCK
    return -(-rows // 16) * 8


def last_factor_kernel(
    first, place_ref, upper_in, inverse_in, projected, _, upper_ref, out_ref, half_ref, inverse, packed
):
    upper_ref[...] = upper_in[...]
    inverse[...] = inverse_in[...]
    order = upper_ref.shape[0]
    factor_steps(upper_ref, inverse, first, order // BLOCK)
    keep_upper(upper_ref)
    solved = solve_twice(inverse, projected)
    out_ref[...] = solved
    blocks = lower_blocks(order)
    for index, (a, b) in enumerate(blocks):
        packed[pl.ds(index * BLOCK, BLOCK), :] = inverse[
            pl.ds(a * BLOCK, BLOCK), pl.ds(b * BLOCK, BLOCK)
        ]
    start = len(blocks) * BLOCK
    packed[start:, :] = jnp.zeros((packed.shape[0] - start, BLOCK), jnp.float32)
    for c in range(order // BLOCK):
        packed[pl.ds(start + c, 1), :] = solved[:, c * BLOCK : (c + 1) * BLOCK]
    size = half_ref.shape[0]
    half_ref[...] = packed[pl.ds(pl.multiple_of(place_ref[1] % 2 * size, 8), size), :]


def last_factor(place, upper, inverse, projected, first, after, cost):
    order = upper.shape[0]
    size = lower_half(order)
    return pl.pallas_call(
        functools.partial(last_factor_kernel, first),
        out_shape=(square(order), row(order), jax.ShapeDtypeStruct((size, BLOCK), jnp.float32)),
        in_specs=[SMEM] + [VMEM] * 3 + [ANY],
        out_specs=[VMEM] * 3,
        scratch_shapes=[
            pltpu.VMEM((order, order), jnp.float32),
            pltpu.VMEM((2 * size, BLOCK), jnp.float32),
        ],
        compiler_params=pltpu.CompilerParams(vmem_limit_bytes=LIMIT),
        cost_estimate=cost,
    )(place, upper, inverse, projected, after)


def finish_kernel(place_ref, upper_ref, solved_ref, half_ref, other_ref, *refs):
    pieces = refs[:GROUP]
    out_ref, multipliers_ref, cross, packed, inverse = refs[GROUP:]
    order = upper_ref.shape[0]
    part = BLOCK // GROUP

    @pl.when(place_ref[0] == 0)
    def _():
        out_ref[...] = upper_ref[...]
        multipliers_ref[...] = solved_ref[...]

    @pl.when(place_ref[0] != 0)
    def _():
        size = half_ref.shape[0]
        core = place_ref[1] % 2
        packed[pl.ds(pl.multiple_of(core * size, 8), size), :] = half_ref[...]
        packed[pl.ds(pl.multiple_of((1 - core) * size, 8), size), :] = other_ref[...]
        blocks = lower_blocks(order)
        for index, (a, b) in enumerate(blocks):
            inverse[pl.ds(a * BLOCK, BLOCK), pl.ds(b * BLOCK, BLOCK)] = packed[
                pl.ds(index * BLOCK, BLOCK), :
            ]
        for c in range(order // BLOCK):
            multipliers_ref[:, pl.ds(c * BLOCK, BLOCK)] = packed[
                pl.ds(len(blocks) * BLOCK + c, 1), :
            ]
        for mask in range(GROUP):
            quarter = place_ref[1] ^ mask
            for b in range(order // BLOCK):
                start = pl.multiple_of(BLOCK * b + part * quarter, part)
                cross[pl.ds(start, part), :] = pieces[mask][pl.ds(part * b, part), :]
        for a in range(order // BLOCK):
            rows, depth = pl.ds(a * BLOCK, BLOCK), (a + 1) * BLOCK
            out_ref[rows, :] = lax.dot_general(
                inverse[rows, pl.ds(0, depth)],
                cross[:, pl.ds(0, depth)],
                (((1,), (1,)), ((), ())),
                precision=HIGHEST,
                preferred_element_type=jnp.float32,
            )


def finish(place, upper, solved, half, other, pieces):
    order = upper.shape[0]
    return pl.pallas_call(
        finish_kernel,
        out_shape=(square(order), row(order)),
        in_specs=[SMEM] + [VMEM] * (4 + GROUP),
        out_specs=[VMEM] * 2,
        scratch_shapes=[
            pltpu.VMEM((order, order), jnp.float32),
            pltpu.VMEM((2 * lower_half(order), BLOCK), jnp.float32),
            pltpu.VMEM((order, order), jnp.float32),
        ],
        compiler_params=pltpu.CompilerParams(vmem_limit_bytes=LIMIT),
        cost_estimate=BRIEF,
    )(place, upper, solved, half, other, *pieces)


def shards(sens_base, design_field, gradient, tile_index, type_codes):
    cells, order = sens_base.shape
    rows_here, width = design_field.shape
    side = lax.axis_index("cols")
    quarter = lax.axis_index("rows") % GROUP
    tiles = width // TILE
    first_tile = lax.axis_index("rows") * rows_here // TILE * tiles
    place = jnp.stack([side, quarter, 3 * first_tile]).astype(jnp.int32)
    key = (tile_index * 3 + type_codes)[None, :].astype(jnp.float32)

    cuts = [BLOCK * sum(STAGES[:s]) for s in range(len(STAGES) + 1)]
    keys = jnp.broadcast_to(key, (KEY_ROWS, order)).astype(sens_base.dtype)
    received = [
        swap(part, "cols", 1) for part in send_parts(place, sens_base, keys, cuts)
    ]

    count = lax.axis_size("rows")
    north = lax.ppermute(design_field[-1:], "rows", [(i, i + 1) for i in range(count - 1)])
    south = lax.ppermute(design_field[:1], "rows", [(i + 1, i) for i in range(count - 1)])
    feature = features(design_field, north, south)
    jac, *packed = own_part(place, sens_base, feature, key, gradient)
    pieces = rows_gather(groups_sum(group_sum(packed)))

    def stage(index, *after):
        return cross_part(place, received[index], jac, feature, *after)

    upper, inverse, projected = first_factor(place, pieces, order, 1, pieces[0])
    first = stage(0, upper)
    shares = group_swaps(first)
    upper, inverse = more_factor(upper, inverse, 1, 2, first[0], LONG)
    held = add(shares, inverse)
    shares = [held, swap(held, "rows", GROUP)]
    upper, inverse = more_factor(upper, inverse, 2, 3, held, LONG)
    middle = add(shares, inverse)
    far = range(2 * GROUP, count, 2 * GROUP)
    far_shares = [middle] + [swap(middle, "rows", mask) for mask in far]
    last = stage(1, middle)
    shares = group_swaps(last)
    upper, solved, half = last_factor(place, upper, inverse, projected, 3, last[0], LONG)
    held_last, half = add_pass(shares, half)
    shares = [held_last] + [swap(held_last, "rows", mask) for mask in range(GROUP, count, GROUP)]
    totals = stacked(far_shares, shares)
    others = lax.ppermute(totals, "cols", [(0, 1)])
    half = lax.ppermute(half, "cols", [(0, 1)])

    cross = joined(totals, others)
    r_panels, multipliers = finish(
        place, upper, solved, half, swap(half, "rows", 1), rows_gather(cross)
    )
    return (r_panels, multipliers[0])


def shards_general(sens_base, design_field, gradient, tile_index, type_codes):
    rows_here = design_field.shape[0]
    grid_width = design_field.shape[1]
    cols_here = sens_base.shape[1]
    factored = 2 * PW
    padded = padded_2(design_field, (("rows", 0),), 1)
    padded = jnp.pad(padded, ((0, 0), (1, 1)))
    north_cells = padded[:-2, 1:-1]
    south_cells = padded[2:, 1:-1]
    west_cells = padded[1:-1, :-2]
    east_cells = padded[1:-1, 2:]
    laplace = 4.0 * design_field - (north_cells + south_cells + west_cells + east_cells)
    slope_x = 0.5 * (east_cells - west_cells)
    slope_y = 0.5 * (south_cells - north_cells)
    stencils = jnp.stack([laplace, slope_x, slope_y]).reshape(3, -1)
    row_glob = lax.axis_index("rows") * rows_here + jnp.arange(rows_here, dtype=jnp.int32)
    col_ids = jnp.arange(grid_width, dtype=jnp.int32) // TILE
    cell_tile = ((row_glob // TILE)[:, None] * (grid_width // TILE) + col_ids[None, :]).reshape(-1)
    local_jac = assemble(sens_base, tile_index, type_codes, stencils, cell_tile)
    grad_flat = gradient.reshape(-1)
    row_major = lax.all_to_all(local_jac, "cols", split_axis=0, concat_axis=1, tiled=True)
    row_piece = row_major.shape[0]
    grad_part = lax.dynamic_slice_in_dim(
        grad_flat, lax.axis_index("cols") * row_piece, row_piece, 0
    )
    leading = row_major[:, :factored]
    gram_block = lax.dot_general(
        leading, row_major, (((0,), (0,)), ((), ())), preferred_element_type=jnp.float32
    )
    projected = jnp.dot(grad_part, leading, preferred_element_type=jnp.float32)
    gram_block, projected = lax.psum((gram_block, projected), ("rows", "cols"))
    gram_head = gram_block[:, :factored]
    gram_own = lax.dynamic_slice_in_dim(
        gram_block, lax.axis_index("cols") * cols_here, cols_here, 1
    )
    _, inverse, multipliers = factor(gram_head, projected[None, :])
    r_panels = matmul(inverse, gram_own)
    return (r_panels, multipliers[0])


def solution(mesh):
    placed = (P("rows", "cols"), P("rows", None), P("rows", None), P("cols"), P("cols"))
    pairs = mesh.shape["cols"] == 2 and mesh.shape["rows"] in (8, 16, 32, 64)
    return jax.shard_map(
        shards if pairs else shards_general,
        mesh=mesh,
        in_specs=placed,
        out_specs=(P(None, "cols"), P()),
        check_vma=False,
    )
```

```python
import functools

import jax
import jax.numpy as jnp
from jax import lax
from jax.experimental import pallas as pl
from jax.experimental.pallas import tpu as pltpu
from jax.sharding import PartitionSpec as P

TILE = 128
PW = 256
BLOCK = 128
FEATURES = 80
KEY_ROWS = 16
SEND_STEPS = 8
GROUP = 4
HIGHEST = lax.Precision.HIGHEST
VMEM = pl.BlockSpec(memory_space=pltpu.VMEM)
SMEM = pl.BlockSpec(memory_space=pltpu.SMEM)
LIMIT = 12 * 2**20
WIDE_LIMIT = 48 * 2**20
ANY = pl.BlockSpec(memory_space=pl.ANY)
STAGES = (3, 1)
LONG = pl.CostEstimate(flops=8 * 10**9, bytes_accessed=1000, transcendentals=0)
BRIEF = pl.CostEstimate(flops=1000, bytes_accessed=1000, transcendentals=0)


def padded_2(cells, sides, width):
    for axis, dim in sides:
        count = lax.axis_size(axis)
        ends = count - 1
        head = lax.slice_in_dim(cells, 0, width, axis=dim)
        tail = lax.slice_in_dim(cells, cells.shape[dim] - width, cells.shape[dim], axis=dim)
        cells = jnp.concatenate(
            [
                lax.ppermute(tail, axis, [(i, (i + 1) % count) for i in range(ends)]),
                cells,
                lax.ppermute(head, axis, [((i + 1) % count, i) for i in range(ends)]),
            ],
            axis=dim,
        )
    return cells


def assemble(base_cols, tile_cols, type_cols, stencils, cell_tile):
    kinds_all = jnp.arange(3, dtype=jnp.int32)
    chooser = (type_cols[None, :] == kinds_all[:, None]).astype(jnp.float32)
    picked = lax.dot_general(
        stencils,
        chooser,
        (((0,), (0,)), ((), ())),
        precision=lax.Precision.HIGHEST,
        preferred_element_type=jnp.float32,
    )
    inside = cell_tile[:, None] == tile_cols[None, :]
    total = base_cols.astype(jnp.float32) + jnp.where(inside, picked / TILE, 0.0)
    return total.astype(jnp.bfloat16)


def matmul(left, right):
    return jnp.dot(left, right, precision=HIGHEST, preferred_element_type=jnp.float32)


def inverse_root(value):
    guess = lax.rsqrt(value)
    return guess * (1.5 - 0.5 * value * guess * guess)


def reciprocal(value):
    guess = pl.reciprocal(value, approx=True)
    guess = guess * (2.0 - value * guess)
    return guess * (2.0 - value * guess)


def lane(part, index):
    return jnp.broadcast_to(part[:, index : index + 1], part.shape)


def sublane(part, index):
    return jnp.broadcast_to(part[index : index + 1, :], part.shape)


def diagonal_inverse(block):
    groups = BLOCK // 8
    shape = (8, BLOCK)
    lanes = lax.broadcasted_iota(jnp.int32, shape, 1)
    subs = lax.broadcasted_iota(jnp.int32, shape, 0)
    parts = [block[8 * g : 8 * g + 8, :] for g in range(groups)]
    whole = []
    for p in range(groups):
        part, first = parts[p], 8 * p
        cols = [lane(part, first + k) for k in range(8)]
        inv = [None] * 8
        low = [jnp.zeros(shape, jnp.float32) for _ in range(8)]
        pivots = jnp.ones(shape, jnp.float32)
        for j in range(8):
            here = subs == j
            pivot = sublane(cols[j], j)
            ratio = reciprocal(pivot)
            pivots = jnp.where(here, pivot, pivots)
            for k in range(j):
                low[k] = jnp.where(here, inv[k], low[k])
            low[j] = jnp.where(here, 1.0, low[j])
            column = cols[j]
            for k in range(j + 1, 8):
                row = sublane(cols[k], j) * ratio
                cols[k] = jnp.where(here, row, cols[k] - column * row)
            for k in range(j):
                row = sublane(inv[k], j) * ratio
                inv[k] = jnp.where(here, row, inv[k] - column * row)
            inv[j] = jnp.where(here, ratio, -column * ratio)
        scale = inverse_root(pivots)
        inside = (lanes >= first) & (lanes < first + 8)
        unit = jnp.where(lanes - first == subs, 1.0, 0.0)
        rows = jnp.where(inside, unit, part)
        spread = [sublane(rows, k) for k in range(8)]
        solved = sum(low[k] * spread[k] for k in range(8)) * scale
        whole.append(jnp.where(lanes < first + 8, solved, 0.0))
        if p + 1 < groups:
            step = sum(inv[k] * spread[k] for k in range(8))
            step = [sublane(step, k) for k in range(8)]
            for g in range(p + 1, groups):
                taken = sum(lane(parts[g], first + k) * step[k] for k in range(8))
                parts[g] = jnp.where(inside, 0.0, parts[g]) - taken
    return jnp.concatenate(whole, axis=0)


def factor_steps(upper_ref, inverse_ref, first, last):
    blocks = upper_ref.shape[0] // BLOCK

    @pl.loop(first, last)
    def _(step):
        mine = pl.ds(pl.multiple_of(step * BLOCK, BLOCK), BLOCK)
        small = diagonal_inverse(upper_ref[mine, mine])
        upper_ref[mine, :] = matmul(small, upper_ref[mine, :])
        inverse_ref[mine, :] = matmul(small, inverse_ref[mine, :])

        @pl.loop(step + 1, blocks)
        def _(later):
            theirs = pl.ds(pl.multiple_of(later * BLOCK, BLOCK), BLOCK)
            factor = upper_ref[mine, theirs]

            def minus(target):
                target[theirs, :] -= lax.dot_general(
                    factor,
                    target[mine, :],
                    (((0,), (0,)), ((), ())),
                    precision=HIGHEST,
                    preferred_element_type=jnp.float32,
                )

            minus(upper_ref)
            minus(inverse_ref)


def start_inverse(inverse_ref):
    rows = lax.broadcasted_iota(jnp.int32, inverse_ref.shape, 0)
    cols = lax.broadcasted_iota(jnp.int32, inverse_ref.shape, 1)
    inverse_ref[...] = jnp.where(rows == cols, 1.0, 0.0)


def keep_upper(upper_ref):
    rows = lax.broadcasted_iota(jnp.int32, upper_ref.shape, 0)
    cols = lax.broadcasted_iota(jnp.int32, upper_ref.shape, 1)
    upper_ref[...] = jnp.where(rows <= cols, upper_ref[...], 0.0)


def solve_twice(inverse_ref, projected_ref):
    half = jnp.sum(inverse_ref[...] * projected_ref[...], axis=1, keepdims=True)
    return jnp.sum(inverse_ref[...] * half, axis=0, keepdims=True)


def factor_kernel(gram_ref, projected_ref, upper_ref, inverse_ref, multipliers_ref):
    upper_ref[...] = gram_ref[...]
    start_inverse(inverse_ref)
    factor_steps(upper_ref, inverse_ref, 0, upper_ref.shape[0] // BLOCK)
    keep_upper(upper_ref)
    multipliers_ref[...] = solve_twice(inverse_ref, projected_ref)


def factor(gram, projected):
    order = gram.shape[0]
    return pl.pallas_call(
        factor_kernel,
        out_shape=(
            jax.ShapeDtypeStruct((order, order), jnp.float32),
            jax.ShapeDtypeStruct((order, order), jnp.float32),
            jax.ShapeDtypeStruct((1, order), jnp.float32),
        ),
        in_specs=[pl.BlockSpec(memory_space=pltpu.VMEM)] * 2,
        out_specs=[pl.BlockSpec(memory_space=pltpu.VMEM)] * 3,
        compiler_params=pltpu.CompilerParams(vmem_limit_bytes=LIMIT),
        cost_estimate=pl.CostEstimate(
            flops=6 * order**3, bytes_accessed=12 * order**2, transcendentals=0
        ),
    )(gram, projected)


def features_kernel(field_ref, north_ref, south_ref, out_ref):
    field = field_ref[...]
    rows, width = field.shape
    lanes = lax.broadcasted_iota(jnp.int32, field.shape, 1)
    north = jnp.concatenate([north_ref[...], field[:-1]], axis=0)
    south = jnp.concatenate([field[1:], south_ref[...]], axis=0)
    west = jnp.where(lanes == 0, 0.0, pltpu.roll(field, 1, 1))
    east = jnp.where(lanes == width - 1, 0.0, pltpu.roll(field, width - 1, 1))
    laplace = 4.0 * field - (north + south + west + east)
    slope_x = 0.5 * (east - west)
    slope_y = 0.5 * (south - north)
    parts = []
    for stencil in (laplace, slope_x, slope_y):
        rest = stencil / TILE
        for _ in range(3):
            part = rest.astype(jnp.bfloat16).astype(jnp.float32)
            parts.append(part)
            rest = rest - part
    tiles = width // TILE
    shape = (FEATURES, width)
    owner = lax.broadcasted_iota(jnp.int32, shape, 0) // len(parts)
    tile = lax.broadcasted_iota(jnp.int32, shape, 1) // TILE
    blank = jnp.zeros((FEATURES - tiles * len(parts), width), jnp.float32)
    for row in range(rows):
        block = jnp.concatenate([part[row : row + 1] for part in parts], axis=0)
        whole = jnp.concatenate([block] * tiles + [blank], axis=0)
        out_ref[row] = jnp.where(owner == tile, whole, 0.0).astype(jnp.bfloat16)


def features(field, north, south):
    rows, width = field.shape
    return pl.pallas_call(
        features_kernel,
        out_shape=jax.ShapeDtypeStruct((rows, FEATURES, width), jnp.bfloat16),
        in_specs=[VMEM] * 3,
        out_specs=VMEM,
        compiler_params=pltpu.CompilerParams(vmem_limit_bytes=LIMIT),
        cost_estimate=BRIEF,
    )(field, north, south)


def assembled(base, feature, key, first):
    rows = lax.broadcasted_iota(jnp.int32, (FEATURES, key.shape[1]), 0) // 3 + first
    chooser = jnp.where(rows.astype(jnp.float32) == key, 1.0, 0.0).astype(jnp.bfloat16)
    added = lax.dot_general(
        feature, chooser, (((0,), (0,)), ((), ())), preferred_element_type=jnp.float32
    )
    return (base.astype(jnp.float32) + added).astype(jnp.bfloat16)


def transposed_dot(left, right):
    return lax.dot_general(
        left, right, (((0,), (0,)), ((), ())), preferred_element_type=jnp.float32
    )


def upper_blocks(order):
    count = order // BLOCK
    return [(a, b) for a in range(count) for b in range(a, count)]


def packed_rows(order):
    used = len(upper_blocks(order)) * BLOCK + order // BLOCK
    return -(-used // (8 * GROUP)) * 8 * GROUP


def own_kernel(
    place_ref, base_ref, feature_ref, key_ref, grad_ref, jac_ref, *refs
):
    outs = refs[:GROUP]
    gram, projected, packed = refs[GROUP:]
    step = pl.program_id(0)
    half = pl.num_programs(0) // 2
    order = base_ref.shape[1]
    jac = assembled(base_ref[...], feature_ref[0], key_ref[...], place_ref[2])

    @pl.when(step // half == place_ref[0])
    def _():
        jac_ref[...] = jac

    @pl.when(step == 0)
    def _():
        gram[...] = jnp.zeros_like(gram)
        projected[...] = jnp.zeros_like(projected)

    middle = order // 2
    gram[:middle, :] += transposed_dot(jac[:, :middle], jac)
    gram[middle:, middle:] += transposed_dot(jac[:, middle:], jac[:, middle:])
    projected[...] += jnp.dot(grad_ref[0], jac, preferred_element_type=jnp.float32)

    @pl.when(step == pl.num_programs(0) - 1)
    def _():
        packed[...] = jnp.zeros_like(packed)
        blocks = upper_blocks(order)
        for index, (a, b) in enumerate(blocks):
            packed[pl.ds(index * BLOCK, BLOCK), :] = gram[
                pl.ds(a * BLOCK, BLOCK), pl.ds(b * BLOCK, BLOCK)
            ]
        for c in range(order // BLOCK):
            packed[pl.ds(len(blocks) * BLOCK + c, 1), :] = projected[:, pl.ds(c * BLOCK, BLOCK)]
        size = outs[0].shape[0]
        for mask in range(GROUP):
            start = pl.multiple_of((place_ref[1] ^ mask) * size, 8)
            outs[mask][...] = packed[pl.ds(start, size), :]


def own_part(place, base, feature, key, gradient):
    cells, order = base.shape
    rows, width = gradient.shape
    half = rows // 2
    size = packed_rows(order) // GROUP
    return pl.pallas_call(
        own_kernel,
        grid_spec=pltpu.PrefetchScalarGridSpec(
            num_scalar_prefetch=1,
            grid=(rows,),
            in_specs=[
                pl.BlockSpec((width, order), lambda i, s: (i, 0)),
                pl.BlockSpec((1, FEATURES, width), lambda i, s: (i, 0, 0)),
                pl.BlockSpec((1, order), lambda i, s: (0, 0)),
                pl.BlockSpec((1, 1, width), lambda i, s: (i, 0, 0)),
            ],
            out_specs=[
                pl.BlockSpec(
                    (width, order), lambda i, s: (jnp.clip(i - s[0] * half, 0, half - 1), 0)
                )
            ]
            + [pl.BlockSpec((size, BLOCK), lambda i, s: (0, 0))] * GROUP,
            scratch_shapes=[
                pltpu.VMEM((order, order), jnp.float32),
                pltpu.VMEM((1, order), jnp.float32),
                pltpu.VMEM((GROUP * size, BLOCK), jnp.float32),
            ],
        ),
        out_shape=[jax.ShapeDtypeStruct((cells // 2, order), jnp.bfloat16)]
        + [jax.ShapeDtypeStruct((size, BLOCK), jnp.float32)] * GROUP,
        compiler_params=pltpu.CompilerParams(vmem_limit_bytes=WIDE_LIMIT),
        cost_estimate=BRIEF,
    )(place, base, feature, key, gradient.reshape(rows, 1, width))


def send_kernel(cuts, place_ref, base_ref, key_ref, *outs):
    step = pl.program_id(0)
    height = base_ref.shape[0]
    here = pl.ds(pl.multiple_of(step * height, height), height)
    for start, end, out in zip(cuts, cuts[1:], outs):
        out[here, :] = base_ref[:, start:end]

    @pl.when(step == 0)
    def _():
        for start, end, out in zip(cuts, cuts[1:], outs):
            key = jnp.broadcast_to(key_ref[:, start:end], (KEY_ROWS, end - start))
            out[pl.ds(pl.num_programs(0) * height, KEY_ROWS), :] = key.astype(jnp.bfloat16)


def send_parts(place, base, key, cuts):
    cells, order = base.shape
    height = cells // 2 // SEND_STEPS
    return pl.pallas_call(
        functools.partial(send_kernel, tuple(cuts)),
        grid_spec=pltpu.PrefetchScalarGridSpec(
            num_scalar_prefetch=1,
            grid=(SEND_STEPS,),
            in_specs=[
                pl.BlockSpec((height, order), lambda i, s: ((1 - s[0]) * SEND_STEPS + i, 0)),
                pl.BlockSpec((1, order), lambda i, s: (0, 0)),
            ],
            out_specs=[VMEM] * (len(cuts) - 1),
        ),
        out_shape=[
            jax.ShapeDtypeStruct((cells // 2 + KEY_ROWS, end - start), base.dtype)
            for start, end in zip(cuts, cuts[1:])
        ],
        compiler_params=pltpu.CompilerParams(vmem_limit_bytes=WIDE_LIMIT + 6 * 2**20),
        cost_estimate=BRIEF,
    )(place, base, key)


def cross_kernel(place_ref, recv_ref, jac_ref, feature_ref, key_ref, *refs):
    outs = refs[-2 - GROUP : -2]
    total, out_ref = refs[-2:]
    step = pl.program_id(0)
    key = key_ref[0:1, :].astype(jnp.float32)
    other = assembled(recv_ref[...], feature_ref[0], key, place_ref[2])

    @pl.when(step == 0)
    def _():
        total[...] = jnp.zeros_like(total)

    total[...] += transposed_dot(other, jac_ref[...])
    count = total.shape[1] // BLOCK
    part = BLOCK // GROUP
    last = step == pl.num_programs(0) - 1

    blocks = total.shape[0] // BLOCK

    @pl.when(last & (place_ref[0] == 0))
    def _():
        for k in range(blocks):
            for q in range(GROUP):
                for c in range(count):
                    out_ref[q, pl.ds(BLOCK * k + part * c, part), :] = total[
                        pl.ds(BLOCK * k + part * q, part), pl.ds(BLOCK * c, BLOCK)
                    ]

    @pl.when(last & (place_ref[0] != 0))
    def _():
        for k in range(blocks):
            for c in range(count):
                block = total[pl.ds(BLOCK * k, BLOCK), pl.ds(BLOCK * c, BLOCK)].T
                for q in range(GROUP):
                    out_ref[q, pl.ds(BLOCK * k + part * c, part), :] = block[
                        part * q : part * q + part
                    ]

    @pl.when(last)
    def _():
        for mask in range(GROUP):
            outs[mask][...] = out_ref[place_ref[1] ^ mask]


def cross_part(place, recv, jac, feature, *after):
    cells, width_recv = jac.shape[0], recv.shape[1]
    order = jac.shape[1]
    rows, _, width = feature.shape
    steps = rows // 2
    return pl.pallas_call(
        cross_kernel,
        grid_spec=pltpu.PrefetchScalarGridSpec(
            num_scalar_prefetch=1,
            grid=(steps,),
            in_specs=[
                pl.BlockSpec((width, width_recv), lambda i, s: (i, 0)),
                pl.BlockSpec((width, order), lambda i, s: (i, 0)),
                pl.BlockSpec((1, FEATURES, width), lambda i, s: (s[0] * steps + i, 0, 0)),
                pl.BlockSpec((KEY_ROWS, width_recv), lambda i, s: (cells // KEY_ROWS, 0)),
            ]
            + [ANY] * len(after),
            out_specs=[pl.BlockSpec((width_recv, BLOCK), lambda i, s: (0, 0))] * GROUP,
            scratch_shapes=[
                pltpu.VMEM((width_recv, order), jnp.float32),
                pltpu.VMEM((GROUP, width_recv, BLOCK), jnp.float32),
            ],
        ),
        out_shape=[jax.ShapeDtypeStruct((width_recv, BLOCK), jnp.float32)] * GROUP,
        compiler_params=pltpu.CompilerParams(vmem_limit_bytes=LIMIT),
        cost_estimate=BRIEF,
    )(place, recv, jac, feature, recv, *after)


def swap(value, axis, mask):
    count = lax.axis_size(axis)
    return lax.ppermute(value, axis, [(i, i ^ mask) for i in range(count)])


def add_kernel(count, *refs):
    refs[-1][...] = sum(ref[...] for ref in refs[1:count]) + refs[0][...]


def add(values, *after):
    return pl.pallas_call(
        functools.partial(add_kernel, len(values)),
        out_shape=jax.ShapeDtypeStruct(values[0].shape, values[0].dtype),
        in_specs=[VMEM] * len(values) + [ANY] * len(after),
        out_specs=VMEM,
        compiler_params=pltpu.CompilerParams(vmem_limit_bytes=LIMIT),
        cost_estimate=BRIEF,
    )(*values, *after)


def add_pass_kernel(*refs):
    *values, passed_ref, out_ref, copy_ref = refs
    out_ref[...] = sum(ref[...] for ref in values[1:]) + values[0][...]
    copy_ref[...] = passed_ref[...]


def add_pass(values, passed):
    return pl.pallas_call(
        add_pass_kernel,
        out_shape=[jax.ShapeDtypeStruct(v.shape, v.dtype) for v in (values[0], passed)],
        in_specs=[VMEM] * (len(values) + 1),
        out_specs=[VMEM] * 2,
        compiler_params=pltpu.CompilerParams(vmem_limit_bytes=LIMIT),
        cost_estimate=BRIEF,
    )(*values, passed)


def stacked_kernel(count, *refs):
    first, second, out_ref = refs[:count], refs[count:-1], refs[-1]
    rows = first[0].shape[0]
    out_ref[:rows, :] = sum(ref[...] for ref in first[1:]) + first[0][...]
    out_ref[rows:, :] = sum(ref[...] for ref in second[1:]) + second[0][...]


def stacked(first, second):
    rows = first[0].shape[0] + second[0].shape[0]
    return pl.pallas_call(
        functools.partial(stacked_kernel, len(first)),
        out_shape=jax.ShapeDtypeStruct((rows, BLOCK), jnp.float32),
        in_specs=[VMEM] * (len(first) + len(second)),
        out_specs=VMEM,
        compiler_params=pltpu.CompilerParams(vmem_limit_bytes=LIMIT),
        cost_estimate=BRIEF,
    )(*first, *second)


def joined_kernel(place_ref, own_ref, other_ref, out_ref):
    part = BLOCK // GROUP
    blocks = own_ref.shape[0] // BLOCK

    def join(second, first):
        for a in range(blocks):
            for b in range(blocks):
                out_ref[pl.ds(part * b, part), pl.ds(BLOCK * a, BLOCK)] = (
                    second[pl.ds(BLOCK * a + part * b, part), :]
                    + first[pl.ds(BLOCK * b + part * a, part), :]
                )

    @pl.when(place_ref[0] == 0)
    def _():
        join(other_ref, own_ref)

    @pl.when(place_ref[0] != 0)
    def _():
        join(own_ref, other_ref)


def joined(place, own, other):
    order = own.shape[0]
    return pl.pallas_call(
        joined_kernel,
        out_shape=jax.ShapeDtypeStruct((order // GROUP, order), jnp.float32),
        in_specs=[SMEM] + [VMEM] * 2,
        out_specs=VMEM,
        compiler_params=pltpu.CompilerParams(vmem_limit_bytes=LIMIT),
        cost_estimate=BRIEF,
    )(place, own, other)


def group_swaps(parts):
    return [parts[0]] + [swap(parts[mask], "rows", mask) for mask in range(1, GROUP)]


def group_sum(parts):
    got = group_swaps(parts)
    return got[0] + got[1] + got[2] + got[3]


def groups_sum(held):
    masks = range(GROUP, lax.axis_size("rows"), GROUP)
    return held + sum(swap(held, "rows", mask) for mask in masks)


def doubled(held, masks):
    for mask in masks:
        held = held + swap(held, "rows", mask)
    return held


def rows_gather(own):
    return [own] + [swap(own, "rows", mask) for mask in range(1, GROUP)]


def side_gather(own):
    rows = lax.axis_size("rows")
    got = [own]
    for mask in range(1, GROUP):
        source = 0 if mask == GROUP - 1 else 1
        pairs = [(2 * (row ^ mask) + source, 2 * row + 1) for row in range(rows)]
        got.append(lax.ppermute(own, ("rows", "cols"), pairs))
    return got


def first_factor_kernel(last, place_ref, *refs):
    pieces = refs[:GROUP]
    upper_ref, inverse_ref, projected_ref, whole = refs[GROUP + 1 :]
    size = pieces[0].shape[0]
    for mask in range(GROUP):
        start = pl.multiple_of((place_ref[1] ^ mask) * size, 8)
        whole[pl.ds(start, size), :] = pieces[mask][...]
    order = upper_ref.shape[0]
    blocks = upper_blocks(order)
    upper_ref[...] = jnp.zeros_like(upper_ref)
    for index, (a, b) in enumerate(blocks):
        upper_ref[pl.ds(a * BLOCK, BLOCK), pl.ds(b * BLOCK, BLOCK)] = whole[
            pl.ds(index * BLOCK, BLOCK), :
        ]
    for c in range(order // BLOCK):
        projected_ref[:, pl.ds(c * BLOCK, BLOCK)] = whole[pl.ds(len(blocks) * BLOCK + c, 1), :]
    start_inverse(inverse_ref)
    factor_steps(upper_ref, inverse_ref, 0, last)


def square(order):
    return jax.ShapeDtypeStruct((order, order), jnp.float32)


def row(order):
    return jax.ShapeDtypeStruct((1, order), jnp.float32)


def first_factor(place, pieces, order, last, after):
    return pl.pallas_call(
        functools.partial(first_factor_kernel, last),
        out_shape=(square(order), square(order), row(order)),
        in_specs=[SMEM] + [VMEM] * GROUP + [ANY],
        out_specs=[VMEM] * 3,
        scratch_shapes=[pltpu.VMEM((packed_rows(order), BLOCK), jnp.float32)],
        compiler_params=pltpu.CompilerParams(vmem_limit_bytes=LIMIT),
        cost_estimate=BRIEF,
    )(place, *pieces, after)


def more_factor_kernel(first, last, upper_in, inverse_in, _, upper_ref, inverse_ref):
    del upper_in, inverse_in
    factor_steps(upper_ref, inverse_ref, first, last)


def more_factor(upper, inverse, first, last, after, cost):
    order = upper.shape[0]
    return pl.pallas_call(
        functools.partial(more_factor_kernel, first, last),
        out_shape=[square(order)] * 2,
        in_specs=[VMEM] * 2 + [ANY],
        out_specs=[VMEM] * 2,
        input_output_aliases={0: 0, 1: 1},
        compiler_params=pltpu.CompilerParams(vmem_limit_bytes=LIMIT),
        cost_estimate=cost,
    )(upper, inverse, after)


def lower_blocks(order):
    return [(a, b) for a in range(order // BLOCK) for b in range(a + 1)]


def lower_half(order):
    rows = len(lower_blocks(order)) * BLOCK + order // BLOCK
    return -(-rows // 16) * 8


def last_factor_kernel(
    first, place_ref, upper_in, inverse_in, projected, _, upper_ref, inverse, out_ref, half_ref, packed
):
    del upper_in, inverse_in
    order = upper_ref.shape[0]
    factor_steps(upper_ref, inverse, first, order // BLOCK)
    keep_upper(upper_ref)
    solved = solve_twice(inverse, projected)
    out_ref[...] = solved
    blocks = lower_blocks(order)
    for index, (a, b) in enumerate(blocks):
        packed[pl.ds(index * BLOCK, BLOCK), :] = inverse[
            pl.ds(a * BLOCK, BLOCK), pl.ds(b * BLOCK, BLOCK)
        ]
    start = len(blocks) * BLOCK
    packed[start:, :] = jnp.zeros((packed.shape[0] - start, BLOCK), jnp.float32)
    for c in range(order // BLOCK):
        packed[pl.ds(start + c, 1), :] = solved[:, c * BLOCK : (c + 1) * BLOCK]
    size = half_ref.shape[0]
    half_ref[...] = packed[pl.ds(pl.multiple_of(place_ref[1] % 2 * size, 8), size), :]


def last_factor(place, upper, inverse, projected, first, after, cost):
    order = upper.shape[0]
    size = lower_half(order)
    return pl.pallas_call(
        functools.partial(last_factor_kernel, first),
        out_shape=(
            square(order),
            square(order),
            row(order),
            jax.ShapeDtypeStruct((size, BLOCK), jnp.float32),
        ),
        in_specs=[SMEM] + [VMEM] * 3 + [ANY],
        out_specs=[VMEM] * 4,
        input_output_aliases={1: 0, 2: 1},
        scratch_shapes=[pltpu.VMEM((2 * size, BLOCK), jnp.float32)],
        compiler_params=pltpu.CompilerParams(vmem_limit_bytes=LIMIT),
        cost_estimate=cost,
    )(place, upper, inverse, projected, after)


def finish_kernel(place_ref, upper_ref, solved_ref, half_ref, other_ref, *refs):
    pieces = refs[:GROUP]
    out_ref, multipliers_ref, cross, packed, inverse = refs[GROUP:]
    order = upper_ref.shape[0]
    part = BLOCK // GROUP

    @pl.when(place_ref[0] == 0)
    def _():
        out_ref[...] = upper_ref[...]
        multipliers_ref[...] = solved_ref[...]

    @pl.when(place_ref[0] != 0)
    def _():
        size = half_ref.shape[0]
        core = place_ref[1] % 2
        packed[pl.ds(pl.multiple_of(core * size, 8), size), :] = half_ref[...]
        packed[pl.ds(pl.multiple_of((1 - core) * size, 8), size), :] = other_ref[...]
        blocks = lower_blocks(order)
        for index, (a, b) in enumerate(blocks):
            inverse[pl.ds(a * BLOCK, BLOCK), pl.ds(b * BLOCK, BLOCK)] = packed[
                pl.ds(index * BLOCK, BLOCK), :
            ]
        for c in range(order // BLOCK):
            multipliers_ref[:, pl.ds(c * BLOCK, BLOCK)] = packed[
                pl.ds(len(blocks) * BLOCK + c, 1), :
            ]
        for mask in range(GROUP):
            quarter = place_ref[1] ^ mask
            for b in range(order // BLOCK):
                start = pl.multiple_of(BLOCK * b + part * quarter, part)
                cross[pl.ds(start, part), :] = pieces[mask][pl.ds(part * b, part), :]
        for a in range(order // BLOCK):
            rows, depth = pl.ds(a * BLOCK, BLOCK), (a + 1) * BLOCK
            out_ref[rows, :] = lax.dot_general(
                inverse[rows, pl.ds(0, depth)],
                cross[:, pl.ds(0, depth)],
                (((1,), (1,)), ((), ())),
                precision=HIGHEST,
                preferred_element_type=jnp.float32,
            )


def finish(place, upper, solved, half, other, pieces):
    order = upper.shape[0]
    return pl.pallas_call(
        finish_kernel,
        out_shape=(square(order), row(order)),
        in_specs=[SMEM] + [VMEM] * (4 + GROUP),
        out_specs=[VMEM] * 2,
        scratch_shapes=[
            pltpu.VMEM((order, order), jnp.float32),
            pltpu.VMEM((2 * lower_half(order), BLOCK), jnp.float32),
            pltpu.VMEM((order, order), jnp.float32),
        ],
        compiler_params=pltpu.CompilerParams(vmem_limit_bytes=LIMIT),
        cost_estimate=BRIEF,
    )(place, upper, solved, half, other, *pieces)


def shards(sens_base, design_field, gradient, tile_index, type_codes):
    cells, order = sens_base.shape
    rows_here, width = design_field.shape
    side = lax.axis_index("cols")
    quarter = lax.axis_index("rows") % GROUP
    tiles = width // TILE
    first_tile = lax.axis_index("rows") * rows_here // TILE * tiles
    place = jnp.stack([side, quarter, 3 * first_tile]).astype(jnp.int32)
    key = (tile_index * 3 + type_codes)[None, :].astype(jnp.float32)

    cuts = [BLOCK * sum(STAGES[:s]) for s in range(len(STAGES) + 1)]
    received = [swap(part, "cols", 1) for part in send_parts(place, sens_base, key, cuts)]

    count = lax.axis_size("rows")
    north = lax.ppermute(design_field[-1:], "rows", [(i, i + 1) for i in range(count - 1)])
    south = lax.ppermute(design_field[:1], "rows", [(i + 1, i) for i in range(count - 1)])
    feature = features(design_field, north, south)
    jac, *packed = own_part(place, sens_base, feature, key, gradient)
    pieces = rows_gather(groups_sum(group_sum(packed)))

    def stage(index, *after):
        return cross_part(place, received[index], jac, feature, *after)

    upper, inverse, projected = first_factor(place, pieces, order, 1, pieces[0])
    first = stage(0, upper)
    shares = group_swaps(first)
    upper, inverse = more_factor(upper, inverse, 1, 2, first[0], LONG)
    held = add(shares, inverse)
    shares = [held, swap(held, "rows", GROUP)]
    upper, inverse = more_factor(upper, inverse, 2, 3, held, LONG)
    middle = add(shares, inverse)
    far = range(2 * GROUP, count, 2 * GROUP)
    far_shares = [middle] + [swap(middle, "rows", mask) for mask in far]
    last = stage(1, middle)
    shares = group_swaps(last)
    upper, _, solved, half = last_factor(place, upper, inverse, projected, 3, last[0], LONG)
    held_last, half = add_pass(shares, half)
    shares = [held_last] + [swap(held_last, "rows", mask) for mask in range(GROUP, count, GROUP)]
    totals = stacked(far_shares, shares)
    others = swap(totals, "cols", 1)
    half = lax.ppermute(half, "cols", [(0, 1)])

    cross = joined(place, totals, others)
    r_panels, multipliers = finish(
        place, upper, solved, half, swap(half, "rows", 1), side_gather(cross)
    )
    return (r_panels, multipliers[0])


def shards_general(sens_base, design_field, gradient, tile_index, type_codes):
    rows_here = design_field.shape[0]
    grid_width = design_field.shape[1]
    cols_here = sens_base.shape[1]
    factored = 2 * PW
    padded = padded_2(design_field, (("rows", 0),), 1)
    padded = jnp.pad(padded, ((0, 0), (1, 1)))
    north_cells = padded[:-2, 1:-1]
    south_cells = padded[2:, 1:-1]
    west_cells = padded[1:-1, :-2]
    east_cells = padded[1:-1, 2:]
    laplace = 4.0 * design_field - (north_cells + south_cells + west_cells + east_cells)
    slope_x = 0.5 * (east_cells - west_cells)
    slope_y = 0.5 * (south_cells - north_cells)
    stencils = jnp.stack([laplace, slope_x, slope_y]).reshape(3, -1)
    row_glob = lax.axis_index("rows") * rows_here + jnp.arange(rows_here, dtype=jnp.int32)
    col_ids = jnp.arange(grid_width, dtype=jnp.int32) // TILE
    cell_tile = ((row_glob // TILE)[:, None] * (grid_width // TILE) + col_ids[None, :]).reshape(-1)
    local_jac = assemble(sens_base, tile_index, type_codes, stencils, cell_tile)
    grad_flat = gradient.reshape(-1)
    row_major = lax.all_to_all(local_jac, "cols", split_axis=0, concat_axis=1, tiled=True)
    row_piece = row_major.shape[0]
    grad_part = lax.dynamic_slice_in_dim(
        grad_flat, lax.axis_index("cols") * row_piece, row_piece, 0
    )
    leading = row_major[:, :factored]
    gram_block = lax.dot_general(
        leading, row_major, (((0,), (0,)), ((), ())), preferred_element_type=jnp.float32
    )
    projected = jnp.dot(grad_part, leading, preferred_element_type=jnp.float32)
    gram_block, projected = lax.psum((gram_block, projected), ("rows", "cols"))
    gram_head = gram_block[:, :factored]
    gram_own = lax.dynamic_slice_in_dim(
        gram_block, lax.axis_index("cols") * cols_here, cols_here, 1
    )
    _, inverse, multipliers = factor(gram_head, projected[None, :])
    r_panels = matmul(inverse, gram_own)
    return (r_panels, multipliers[0])


def solution(mesh):
    placed = (P("rows", "cols"), P("rows", None), P("rows", None), P("cols"), P("cols"))
    pairs = mesh.shape["cols"] == 2 and mesh.shape["rows"] in (8, 16, 32, 64)
    return jax.shard_map(
        shards if pairs else shards_general,
        mesh=mesh,
        in_specs=placed,
        out_specs=(P(None, "cols"), P()),
        check_vma=False,
    )
```

```python
import functools

import jax
import jax.numpy as jnp
from jax import lax
from jax.experimental import pallas as pl
from jax.experimental.pallas import tpu as pltpu
from jax.sharding import PartitionSpec as P

TILE = 128
PW = 256
BLOCK = 128
FEATURES = 80
KEY_ROWS = 16
SEND_STEPS = 8
OWN_CUTS = 4
GROUP = 4
HIGHEST = lax.Precision.HIGHEST
VMEM = pl.BlockSpec(memory_space=pltpu.VMEM)
SMEM = pl.BlockSpec(memory_space=pltpu.SMEM)
LIMIT = 12 * 2**20
WIDE_LIMIT = 48 * 2**20
ANY = pl.BlockSpec(memory_space=pl.ANY)
STAGES = (3, 1)
LONG = pl.CostEstimate(flops=8 * 10**9, bytes_accessed=1000, transcendentals=0)
BRIEF = pl.CostEstimate(flops=1000, bytes_accessed=1000, transcendentals=0)


def padded_2(cells, sides, width):
    for axis, dim in sides:
        count = lax.axis_size(axis)
        ends = count - 1
        head = lax.slice_in_dim(cells, 0, width, axis=dim)
        tail = lax.slice_in_dim(cells, cells.shape[dim] - width, cells.shape[dim], axis=dim)
        cells = jnp.concatenate(
            [
                lax.ppermute(tail, axis, [(i, (i + 1) % count) for i in range(ends)]),
                cells,
                lax.ppermute(head, axis, [((i + 1) % count, i) for i in range(ends)]),
            ],
            axis=dim,
        )
    return cells


def assemble(base_cols, tile_cols, type_cols, stencils, cell_tile):
    kinds_all = jnp.arange(3, dtype=jnp.int32)
    chooser = (type_cols[None, :] == kinds_all[:, None]).astype(jnp.float32)
    picked = lax.dot_general(
        stencils,
        chooser,
        (((0,), (0,)), ((), ())),
        precision=lax.Precision.HIGHEST,
        preferred_element_type=jnp.float32,
    )
    inside = cell_tile[:, None] == tile_cols[None, :]
    total = base_cols.astype(jnp.float32) + jnp.where(inside, picked / TILE, 0.0)
    return total.astype(jnp.bfloat16)


def matmul(left, right):
    return jnp.dot(left, right, precision=HIGHEST, preferred_element_type=jnp.float32)


def inverse_root(value):
    guess = lax.rsqrt(value)
    return guess * (1.5 - 0.5 * value * guess * guess)


def reciprocal(value):
    guess = pl.reciprocal(value, approx=True)
    guess = guess * (2.0 - value * guess)
    return guess * (2.0 - value * guess)


def lane(part, index):
    return jnp.broadcast_to(part[:, index : index + 1], part.shape)


def sublane(part, index):
    return jnp.broadcast_to(part[index : index + 1, :], part.shape)


def diagonal_inverse(block):
    groups = BLOCK // 8
    shape = (8, BLOCK)
    lanes = lax.broadcasted_iota(jnp.int32, shape, 1)
    subs = lax.broadcasted_iota(jnp.int32, shape, 0)
    parts = [block[8 * g : 8 * g + 8, :] for g in range(groups)]
    whole = []
    for p in range(groups):
        part, first = parts[p], 8 * p
        cols = [lane(part, first + k) for k in range(8)]
        inv = [None] * 8
        low = [jnp.zeros(shape, jnp.float32) for _ in range(8)]
        pivots = jnp.ones(shape, jnp.float32)
        for j in range(8):
            here = subs == j
            pivot = sublane(cols[j], j)
            ratio = reciprocal(pivot)
            pivots = jnp.where(here, pivot, pivots)
            for k in range(j):
                low[k] = jnp.where(here, inv[k], low[k])
            low[j] = jnp.where(here, 1.0, low[j])
            column = cols[j]
            for k in range(j + 1, 8):
                row = sublane(cols[k], j) * ratio
                cols[k] = jnp.where(here, row, cols[k] - column * row)
            for k in range(j):
                row = sublane(inv[k], j) * ratio
                inv[k] = jnp.where(here, row, inv[k] - column * row)
            inv[j] = jnp.where(here, ratio, -column * ratio)
        scale = inverse_root(pivots)
        inside = (lanes >= first) & (lanes < first + 8)
        unit = jnp.where(lanes - first == subs, 1.0, 0.0)
        rows = jnp.where(inside, unit, part)
        spread = [sublane(rows, k) for k in range(8)]
        solved = sum(low[k] * spread[k] for k in range(8)) * scale
        whole.append(jnp.where(lanes < first + 8, solved, 0.0))
        if p + 1 < groups:
            step = sum(inv[k] * spread[k] for k in range(8))
            step = [sublane(step, k) for k in range(8)]
            for g in range(p + 1, groups):
                taken = sum(lane(parts[g], first + k) * step[k] for k in range(8))
                parts[g] = jnp.where(inside, 0.0, parts[g]) - taken
    return jnp.concatenate(whole, axis=0)


def factor_steps(upper_ref, inverse_ref, first, last):
    blocks = upper_ref.shape[0] // BLOCK

    @pl.loop(first, last)
    def _(step):
        mine = pl.ds(pl.multiple_of(step * BLOCK, BLOCK), BLOCK)
        small = diagonal_inverse(upper_ref[mine, mine])
        upper_ref[mine, :] = matmul(small, upper_ref[mine, :])
        inverse_ref[mine, :] = matmul(small, inverse_ref[mine, :])

        @pl.loop(step + 1, blocks)
        def _(later):
            theirs = pl.ds(pl.multiple_of(later * BLOCK, BLOCK), BLOCK)
            factor = upper_ref[mine, theirs]

            def minus(target):
                target[theirs, :] -= lax.dot_general(
                    factor,
                    target[mine, :],
                    (((0,), (0,)), ((), ())),
                    precision=HIGHEST,
                    preferred_element_type=jnp.float32,
                )

            minus(upper_ref)
            minus(inverse_ref)


def start_inverse(inverse_ref):
    rows = lax.broadcasted_iota(jnp.int32, inverse_ref.shape, 0)
    cols = lax.broadcasted_iota(jnp.int32, inverse_ref.shape, 1)
    inverse_ref[...] = jnp.where(rows == cols, 1.0, 0.0)


def keep_upper(upper_ref):
    rows = lax.broadcasted_iota(jnp.int32, upper_ref.shape, 0)
    cols = lax.broadcasted_iota(jnp.int32, upper_ref.shape, 1)
    upper_ref[...] = jnp.where(rows <= cols, upper_ref[...], 0.0)


def solve_twice(inverse_ref, projected_ref):
    half = jnp.sum(inverse_ref[...] * projected_ref[...], axis=1, keepdims=True)
    return jnp.sum(inverse_ref[...] * half, axis=0, keepdims=True)


def factor_kernel(gram_ref, projected_ref, upper_ref, inverse_ref, multipliers_ref):
    upper_ref[...] = gram_ref[...]
    start_inverse(inverse_ref)
    factor_steps(upper_ref, inverse_ref, 0, upper_ref.shape[0] // BLOCK)
    keep_upper(upper_ref)
    multipliers_ref[...] = solve_twice(inverse_ref, projected_ref)


def factor(gram, projected):
    order = gram.shape[0]
    return pl.pallas_call(
        factor_kernel,
        out_shape=(
            jax.ShapeDtypeStruct((order, order), jnp.float32),
            jax.ShapeDtypeStruct((order, order), jnp.float32),
            jax.ShapeDtypeStruct((1, order), jnp.float32),
        ),
        in_specs=[pl.BlockSpec(memory_space=pltpu.VMEM)] * 2,
        out_specs=[pl.BlockSpec(memory_space=pltpu.VMEM)] * 3,
        compiler_params=pltpu.CompilerParams(vmem_limit_bytes=LIMIT),
        cost_estimate=pl.CostEstimate(
            flops=6 * order**3, bytes_accessed=12 * order**2, transcendentals=0
        ),
    )(gram, projected)


def features_kernel(field_ref, north_ref, south_ref, out_ref):
    field = field_ref[...]
    rows, width = field.shape
    lanes = lax.broadcasted_iota(jnp.int32, field.shape, 1)
    north = jnp.concatenate([north_ref[...], field[:-1]], axis=0)
    south = jnp.concatenate([field[1:], south_ref[...]], axis=0)
    west = jnp.where(lanes == 0, 0.0, pltpu.roll(field, 1, 1))
    east = jnp.where(lanes == width - 1, 0.0, pltpu.roll(field, width - 1, 1))
    laplace = 4.0 * field - (north + south + west + east)
    slope_x = 0.5 * (east - west)
    slope_y = 0.5 * (south - north)
    parts = []
    for stencil in (laplace, slope_x, slope_y):
        rest = stencil / TILE
        for _ in range(3):
            part = rest.astype(jnp.bfloat16).astype(jnp.float32)
            parts.append(part)
            rest = rest - part
    tiles = width // TILE
    shape = (FEATURES, width)
    owner = lax.broadcasted_iota(jnp.int32, shape, 0) // len(parts)
    tile = lax.broadcasted_iota(jnp.int32, shape, 1) // TILE
    blank = jnp.zeros((FEATURES - tiles * len(parts), width), jnp.float32)
    for row in range(rows):
        block = jnp.concatenate([part[row : row + 1] for part in parts], axis=0)
        whole = jnp.concatenate([block] * tiles + [blank], axis=0)
        out_ref[row] = jnp.where(owner == tile, whole, 0.0).astype(jnp.bfloat16)


def features(field, north, south):
    rows, width = field.shape
    return pl.pallas_call(
        features_kernel,
        out_shape=jax.ShapeDtypeStruct((rows, FEATURES, width), jnp.bfloat16),
        in_specs=[VMEM] * 3,
        out_specs=VMEM,
        compiler_params=pltpu.CompilerParams(vmem_limit_bytes=LIMIT),
        cost_estimate=BRIEF,
    )(field, north, south)


def assembled(base, feature, key, first):
    rows = lax.broadcasted_iota(jnp.int32, (FEATURES, key.shape[1]), 0) // 3 + first
    chooser = jnp.where(rows.astype(jnp.float32) == key, 1.0, 0.0).astype(jnp.bfloat16)
    added = lax.dot_general(
        feature, chooser, (((0,), (0,)), ((), ())), preferred_element_type=jnp.float32
    )
    return (base.astype(jnp.float32) + added).astype(jnp.bfloat16)


def transposed_dot(left, right):
    return lax.dot_general(
        left, right, (((0,), (0,)), ((), ())), preferred_element_type=jnp.float32
    )


def upper_blocks(order):
    count = order // BLOCK
    return [(a, b) for a in range(count) for b in range(a, count)]


def packed_rows(order):
    used = len(upper_blocks(order)) * BLOCK + order // BLOCK
    return -(-used // (8 * GROUP)) * 8 * GROUP


def own_kernel(
    place_ref, *refs
):
    bases = refs[:OWN_CUTS]
    feature_ref, key_ref, grad_ref, jac_ref = refs[OWN_CUTS : OWN_CUTS + 4]
    outs = refs[OWN_CUTS + 4 : OWN_CUTS + 4 + GROUP]
    gram, projected, packed = refs[OWN_CUTS + 4 + GROUP :]
    step = pl.program_id(0)
    half = pl.num_programs(0) // 2
    order = gram.shape[0]
    base = jnp.concatenate([ref[...] for ref in bases], axis=0)
    jac = assembled(base, feature_ref[0], key_ref[...], place_ref[2])

    @pl.when(step // half == place_ref[0])
    def _():
        jac_ref[...] = jac

    @pl.when(step == 0)
    def _():
        gram[...] = jnp.zeros_like(gram)
        projected[...] = jnp.zeros_like(projected)

    middle = order // 2
    gram[:middle, :] += transposed_dot(jac[:, :middle], jac)
    gram[middle:, middle:] += transposed_dot(jac[:, middle:], jac[:, middle:])
    projected[...] += jnp.dot(grad_ref[0], jac, preferred_element_type=jnp.float32)

    @pl.when(step == pl.num_programs(0) - 1)
    def _():
        packed[...] = jnp.zeros_like(packed)
        blocks = upper_blocks(order)
        for index, (a, b) in enumerate(blocks):
            packed[pl.ds(index * BLOCK, BLOCK), :] = gram[
                pl.ds(a * BLOCK, BLOCK), pl.ds(b * BLOCK, BLOCK)
            ]
        for c in range(order // BLOCK):
            packed[pl.ds(len(blocks) * BLOCK + c, 1), :] = projected[:, pl.ds(c * BLOCK, BLOCK)]
        size = outs[0].shape[0]
        for mask in range(GROUP):
            start = pl.multiple_of((place_ref[1] ^ mask) * size, 8)
            outs[mask][...] = packed[pl.ds(start, size), :]


def cut_index(cut, i, place):
    return (OWN_CUTS * i + cut, 0)


def own_part(place, base, feature, key, gradient):
    cells, order = base.shape
    rows, width = gradient.shape
    half = rows // 2
    size = packed_rows(order) // GROUP
    return pl.pallas_call(
        own_kernel,
        grid_spec=pltpu.PrefetchScalarGridSpec(
            num_scalar_prefetch=1,
            grid=(rows,),
            in_specs=[
                pl.BlockSpec((width // OWN_CUTS, order), functools.partial(cut_index, k))
                for k in range(OWN_CUTS)
            ]
            + [
                pl.BlockSpec((1, FEATURES, width), lambda i, s: (i, 0, 0)),
                pl.BlockSpec((1, order), lambda i, s: (0, 0)),
                pl.BlockSpec((1, 1, width), lambda i, s: (i, 0, 0)),
            ],
            out_specs=[
                pl.BlockSpec(
                    (width, order), lambda i, s: (jnp.clip(i - s[0] * half, 0, half - 1), 0)
                )
            ]
            + [pl.BlockSpec((size, BLOCK), lambda i, s: (0, 0))] * GROUP,
            scratch_shapes=[
                pltpu.VMEM((order, order), jnp.float32),
                pltpu.VMEM((1, order), jnp.float32),
                pltpu.VMEM((GROUP * size, BLOCK), jnp.float32),
            ],
        ),
        out_shape=[jax.ShapeDtypeStruct((cells // 2, order), jnp.bfloat16)]
        + [jax.ShapeDtypeStruct((size, BLOCK), jnp.float32)] * GROUP,
        compiler_params=pltpu.CompilerParams(vmem_limit_bytes=WIDE_LIMIT),
        cost_estimate=BRIEF,
    )(place, *[base] * OWN_CUTS, feature, key, gradient.reshape(rows, 1, width))


def send_kernel(cuts, place_ref, base_ref, key_ref, *refs):
    outs, (held, sems) = refs[:-2], refs[-2:]
    steps, height, _ = held.shape
    first = (1 - place_ref[0]) * steps * height
    copies = [
        pltpu.make_async_copy(
            base_ref.at[pl.ds(pl.multiple_of(first + k * height, height), height), :],
            held.at[k],
            sems.at[k],
        )
        for k in range(steps)
    ]
    for copy in copies:
        copy.start()
    for start, end, out in zip(cuts, cuts[1:], outs):
        key = jnp.broadcast_to(key_ref[:, start:end], (KEY_ROWS, end - start))
        out[pl.ds(steps * height, KEY_ROWS), :] = key.astype(jnp.bfloat16)
    for k, copy in enumerate(copies):
        copy.wait()
        for start, end, out in zip(cuts, cuts[1:], outs):
            out[pl.ds(k * height, height), :] = held[k, :, start:end]


def send_parts(place, base, key, cuts):
    cells, order = base.shape
    return pl.pallas_call(
        functools.partial(send_kernel, tuple(cuts)),
        in_specs=[SMEM, ANY, VMEM],
        out_specs=[VMEM] * (len(cuts) - 1),
        out_shape=[
            jax.ShapeDtypeStruct((cells // 2 + KEY_ROWS, end - start), base.dtype)
            for start, end in zip(cuts, cuts[1:])
        ],
        scratch_shapes=[
            pltpu.VMEM((SEND_STEPS, cells // 2 // SEND_STEPS, order), base.dtype),
            pltpu.SemaphoreType.DMA((SEND_STEPS,)),
        ],
        compiler_params=pltpu.CompilerParams(vmem_limit_bytes=WIDE_LIMIT + 6 * 2**20),
        cost_estimate=BRIEF,
    )(place, base, key)


def cross_kernel(place_ref, recv_ref, jac_ref, feature_ref, *refs):
    outs = refs[-2 - GROUP : -2]
    total, out_ref = refs[-2:]
    cells, width = jac_ref.shape[0], feature_ref.shape[2]
    steps = cells // width
    key = recv_ref[pl.ds(cells, KEY_ROWS), :][0:1, :].astype(jnp.float32)
    total[...] = jnp.zeros_like(total)

    @pl.loop(0, steps)
    def _(step):
        rows = pl.ds(pl.multiple_of(step * width, width), width)
        feature = feature_ref[place_ref[0] * steps + step]
        other = assembled(recv_ref[rows, :], feature, key, place_ref[2])
        total[...] += transposed_dot(other, jac_ref[rows, :])

    count = total.shape[1] // BLOCK
    part = BLOCK // GROUP

    blocks = total.shape[0] // BLOCK

    @pl.when(place_ref[0] == 0)
    def _():
        for k in range(blocks):
            for q in range(GROUP):
                for c in range(count):
                    out_ref[q, pl.ds(BLOCK * k + part * c, part), :] = total[
                        pl.ds(BLOCK * k + part * q, part), pl.ds(BLOCK * c, BLOCK)
                    ]

    @pl.when(place_ref[0] != 0)
    def _():
        for k in range(blocks):
            for c in range(count):
                block = total[pl.ds(BLOCK * k, BLOCK), pl.ds(BLOCK * c, BLOCK)].T
                for q in range(GROUP):
                    out_ref[q, pl.ds(BLOCK * k + part * c, part), :] = block[
                        part * q : part * q + part
                    ]

    for mask in range(GROUP):
        outs[mask][...] = out_ref[place_ref[1] ^ mask]


def cross_part(place, recv, jac, feature, *after):
    width_recv, order = recv.shape[1], jac.shape[1]
    return pl.pallas_call(
        cross_kernel,
        in_specs=[SMEM] + [VMEM] * 3 + [ANY] * len(after),
        out_specs=[VMEM] * GROUP,
        out_shape=[jax.ShapeDtypeStruct((width_recv, BLOCK), jnp.float32)] * GROUP,
        scratch_shapes=[
            pltpu.VMEM((width_recv, order), jnp.float32),
            pltpu.VMEM((GROUP, width_recv, BLOCK), jnp.float32),
        ],
        compiler_params=pltpu.CompilerParams(vmem_limit_bytes=LIMIT),
        cost_estimate=BRIEF,
    )(place, recv, jac, feature, *after)


def swap(value, axis, mask):
    count = lax.axis_size(axis)
    return lax.ppermute(value, axis, [(i, i ^ mask) for i in range(count)])


def add_kernel(count, *refs):
    refs[-1][...] = sum(ref[...] for ref in refs[1:count]) + refs[0][...]


def add(values, *after):
    return pl.pallas_call(
        functools.partial(add_kernel, len(values)),
        out_shape=jax.ShapeDtypeStruct(values[0].shape, values[0].dtype),
        in_specs=[VMEM] * len(values) + [ANY] * len(after),
        out_specs=VMEM,
        compiler_params=pltpu.CompilerParams(vmem_limit_bytes=LIMIT),
        cost_estimate=BRIEF,
    )(*values, *after)


def add_pass_kernel(*refs):
    *values, passed_ref, out_ref, copy_ref = refs
    out_ref[...] = sum(ref[...] for ref in values[1:]) + values[0][...]
    copy_ref[...] = passed_ref[...]


def add_pass(values, passed):
    return pl.pallas_call(
        add_pass_kernel,
        out_shape=[jax.ShapeDtypeStruct(v.shape, v.dtype) for v in (values[0], passed)],
        in_specs=[VMEM] * (len(values) + 1),
        out_specs=[VMEM] * 2,
        compiler_params=pltpu.CompilerParams(vmem_limit_bytes=LIMIT),
        cost_estimate=BRIEF,
    )(*values, passed)


def stacked_kernel(count, *refs):
    first, second, out_ref = refs[:count], refs[count:-1], refs[-1]
    rows = first[0].shape[0]
    out_ref[:rows, :] = sum(ref[...] for ref in first[1:]) + first[0][...]
    out_ref[rows:, :] = sum(ref[...] for ref in second[1:]) + second[0][...]


def stacked(first, second):
    rows = first[0].shape[0] + second[0].shape[0]
    return pl.pallas_call(
        functools.partial(stacked_kernel, len(first)),
        out_shape=jax.ShapeDtypeStruct((rows, BLOCK), jnp.float32),
        in_specs=[VMEM] * (len(first) + len(second)),
        out_specs=VMEM,
        compiler_params=pltpu.CompilerParams(vmem_limit_bytes=LIMIT),
        cost_estimate=BRIEF,
    )(*first, *second)


def joined_kernel(place_ref, own_ref, other_ref, out_ref):
    part = BLOCK // GROUP
    blocks = own_ref.shape[0] // BLOCK

    def join(second, first):
        for a in range(blocks):
            for b in range(blocks):
                out_ref[pl.ds(part * b, part), pl.ds(BLOCK * a, BLOCK)] = (
                    second[pl.ds(BLOCK * a + part * b, part), :]
                    + first[pl.ds(BLOCK * b + part * a, part), :]
                )

    @pl.when(place_ref[0] == 0)
    def _():
        join(other_ref, own_ref)

    @pl.when(place_ref[0] != 0)
    def _():
        join(own_ref, other_ref)


def joined(place, own, other):
    order = own.shape[0]
    return pl.pallas_call(
        joined_kernel,
        out_shape=jax.ShapeDtypeStruct((order // GROUP, order), jnp.float32),
        in_specs=[SMEM] + [VMEM] * 2,
        out_specs=VMEM,
        compiler_params=pltpu.CompilerParams(vmem_limit_bytes=LIMIT),
        cost_estimate=BRIEF,
    )(place, own, other)


def group_swaps(parts):
    return [parts[0]] + [swap(parts[mask], "rows", mask) for mask in range(1, GROUP)]


def group_sum(parts):
    got = group_swaps(parts)
    return got[0] + got[1] + got[2] + got[3]


def groups_sum(held):
    masks = range(GROUP, lax.axis_size("rows"), GROUP)
    return held + sum(swap(held, "rows", mask) for mask in masks)


def doubled(held, masks):
    for mask in masks:
        held = held + swap(held, "rows", mask)
    return held


def rows_gather(own):
    return [own] + [swap(own, "rows", mask) for mask in range(1, GROUP)]


def near_gather(own):
    near, far = swap(own, "rows", 1), swap(own, "rows", 2)
    return [own, near, far, swap(far, "rows", 1)]


def first_factor_kernel(last, place_ref, *refs):
    pieces = refs[:GROUP]
    upper_ref, inverse_ref, projected_ref, whole = refs[GROUP + 1 :]
    size = pieces[0].shape[0]
    for mask in range(GROUP):
        start = pl.multiple_of((place_ref[1] ^ mask) * size, 8)
        whole[pl.ds(start, size), :] = pieces[mask][...]
    order = upper_ref.shape[0]
    blocks = upper_blocks(order)
    upper_ref[...] = jnp.zeros_like(upper_ref)
    for index, (a, b) in enumerate(blocks):
        upper_ref[pl.ds(a * BLOCK, BLOCK), pl.ds(b * BLOCK, BLOCK)] = whole[
            pl.ds(index * BLOCK, BLOCK), :
        ]
    for c in range(order // BLOCK):
        projected_ref[:, pl.ds(c * BLOCK, BLOCK)] = whole[pl.ds(len(blocks) * BLOCK + c, 1), :]
    start_inverse(inverse_ref)
    factor_steps(upper_ref, inverse_ref, 0, last)


def square(order):
    return jax.ShapeDtypeStruct((order, order), jnp.float32)


def row(order):
    return jax.ShapeDtypeStruct((1, order), jnp.float32)


def first_factor(place, pieces, order, last, after):
    return pl.pallas_call(
        functools.partial(first_factor_kernel, last),
        out_shape=(square(order), square(order), row(order)),
        in_specs=[SMEM] + [VMEM] * GROUP + [ANY],
        out_specs=[VMEM] * 3,
        scratch_shapes=[pltpu.VMEM((packed_rows(order), BLOCK), jnp.float32)],
        compiler_params=pltpu.CompilerParams(vmem_limit_bytes=LIMIT),
        cost_estimate=BRIEF,
    )(place, *pieces, after)


def more_factor_kernel(first, last, upper_in, inverse_in, _, upper_ref, inverse_ref):
    del upper_in, inverse_in
    factor_steps(upper_ref, inverse_ref, first, last)


def more_factor(upper, inverse, first, last, after, cost):
    order = upper.shape[0]
    return pl.pallas_call(
        functools.partial(more_factor_kernel, first, last),
        out_shape=[square(order)] * 2,
        in_specs=[VMEM] * 2 + [ANY],
        out_specs=[VMEM] * 2,
        input_output_aliases={0: 0, 1: 1},
        compiler_params=pltpu.CompilerParams(vmem_limit_bytes=LIMIT),
        cost_estimate=cost,
    )(upper, inverse, after)


def lower_blocks(order):
    return [(a, b) for a in range(order // BLOCK) for b in range(a + 1)]


def lower_half(order):
    rows = len(lower_blocks(order)) * BLOCK + order // BLOCK
    return -(-rows // 16) * 8


def last_factor_kernel(
    first, place_ref, upper_in, inverse_in, projected, _, upper_ref, inverse, out_ref, half_ref, packed
):
    del upper_in, inverse_in
    order = upper_ref.shape[0]
    factor_steps(upper_ref, inverse, first, order // BLOCK)
    keep_upper(upper_ref)
    solved = solve_twice(inverse, projected)
    out_ref[...] = solved
    blocks = lower_blocks(order)
    for index, (a, b) in enumerate(blocks):
        packed[pl.ds(index * BLOCK, BLOCK), :] = inverse[
            pl.ds(a * BLOCK, BLOCK), pl.ds(b * BLOCK, BLOCK)
        ]
    start = len(blocks) * BLOCK
    packed[start:, :] = jnp.zeros((packed.shape[0] - start, BLOCK), jnp.float32)
    for c in range(order // BLOCK):
        packed[pl.ds(start + c, 1), :] = solved[:, c * BLOCK : (c + 1) * BLOCK]
    size = half_ref.shape[0]
    half_ref[...] = packed[pl.ds(pl.multiple_of(place_ref[1] % 2 * size, 8), size), :]


def last_factor(place, upper, inverse, projected, first, after, cost):
    order = upper.shape[0]
    size = lower_half(order)
    return pl.pallas_call(
        functools.partial(last_factor_kernel, first),
        out_shape=(
            square(order),
            square(order),
            row(order),
            jax.ShapeDtypeStruct((size, BLOCK), jnp.float32),
        ),
        in_specs=[SMEM] + [VMEM] * 3 + [ANY],
        out_specs=[VMEM] * 4,
        input_output_aliases={1: 0, 2: 1},
        scratch_shapes=[pltpu.VMEM((2 * size, BLOCK), jnp.float32)],
        compiler_params=pltpu.CompilerParams(vmem_limit_bytes=LIMIT),
        cost_estimate=cost,
    )(place, upper, inverse, projected, after)


def finish_kernel(place_ref, upper_ref, solved_ref, half_ref, other_ref, *refs):
    pieces = refs[:GROUP]
    out_ref, multipliers_ref, cross, packed, inverse = refs[GROUP:]
    order = upper_ref.shape[0]
    part = BLOCK // GROUP

    @pl.when(place_ref[0] == 0)
    def _():
        out_ref[...] = upper_ref[...]
        multipliers_ref[...] = solved_ref[...]

    @pl.when(place_ref[0] != 0)
    def _():
        size = half_ref.shape[0]
        core = place_ref[1] % 2
        packed[pl.ds(pl.multiple_of(core * size, 8), size), :] = half_ref[...]
        packed[pl.ds(pl.multiple_of((1 - core) * size, 8), size), :] = other_ref[...]
        blocks = lower_blocks(order)
        for index, (a, b) in enumerate(blocks):
            inverse[pl.ds(a * BLOCK, BLOCK), pl.ds(b * BLOCK, BLOCK)] = packed[
                pl.ds(index * BLOCK, BLOCK), :
            ]
        for c in range(order // BLOCK):
            multipliers_ref[:, pl.ds(c * BLOCK, BLOCK)] = packed[
                pl.ds(len(blocks) * BLOCK + c, 1), :
            ]
        for mask in range(GROUP):
            quarter = place_ref[1] ^ mask
            for b in range(order // BLOCK):
                start = pl.multiple_of(BLOCK * b + part * quarter, part)
                cross[pl.ds(start, part), :] = pieces[mask][pl.ds(part * b, part), :]
        for a in range(order // BLOCK):
            rows, depth = pl.ds(a * BLOCK, BLOCK), (a + 1) * BLOCK
            out_ref[rows, :] = lax.dot_general(
                inverse[rows, pl.ds(0, depth)],
                cross[:, pl.ds(0, depth)],
                (((1,), (1,)), ((), ())),
                precision=HIGHEST,
                preferred_element_type=jnp.float32,
            )


def finish(place, upper, solved, half, other, pieces):
    order = upper.shape[0]
    return pl.pallas_call(
        finish_kernel,
        out_shape=(square(order), row(order)),
        in_specs=[SMEM] + [VMEM] * (4 + GROUP),
        out_specs=[VMEM] * 2,
        scratch_shapes=[
            pltpu.VMEM((order, order), jnp.float32),
            pltpu.VMEM((2 * lower_half(order), BLOCK), jnp.float32),
            pltpu.VMEM((order, order), jnp.float32),
        ],
        compiler_params=pltpu.CompilerParams(vmem_limit_bytes=LIMIT),
        cost_estimate=BRIEF,
    )(place, upper, solved, half, other, *pieces)


def shards(sens_base, design_field, gradient, tile_index, type_codes):
    cells, order = sens_base.shape
    rows_here, width = design_field.shape
    side = lax.axis_index("cols")
    quarter = lax.axis_index("rows") % GROUP
    tiles = width // TILE
    first_tile = lax.axis_index("rows") * rows_here // TILE * tiles
    place = jnp.stack([side, quarter, 3 * first_tile]).astype(jnp.int32)
    key = (tile_index * 3 + type_codes)[None, :].astype(jnp.float32)

    cuts = [BLOCK * sum(STAGES[:s]) for s in range(len(STAGES) + 1)]
    received = [swap(part, "cols", 1) for part in send_parts(place, sens_base, key, cuts)]

    count = lax.axis_size("rows")
    north = lax.ppermute(design_field[-1:], "rows", [(i, i + 1) for i in range(count - 1)])
    south = lax.ppermute(design_field[:1], "rows", [(i + 1, i) for i in range(count - 1)])
    feature = features(design_field, north, south)
    jac, *packed = own_part(place, sens_base, feature, key, gradient)
    pieces = rows_gather(groups_sum(group_sum(packed)))

    def stage(index, *after):
        return cross_part(place, received[index], jac, feature, *after)

    upper, inverse, projected = first_factor(place, pieces, order, 1, pieces[0])
    first = stage(0, upper)
    shares = group_swaps(first)
    upper, inverse = more_factor(upper, inverse, 1, 2, first[0], LONG)
    held = add(shares, inverse)
    shares = [held, swap(held, "rows", GROUP)]
    upper, inverse = more_factor(upper, inverse, 2, 3, held, LONG)
    middle = add(shares, inverse)
    far = range(2 * GROUP, count, 2 * GROUP)
    far_shares = [middle] + [swap(middle, "rows", mask) for mask in far]
    last = stage(1, middle)
    shares = group_swaps(last)
    upper, _, solved, half = last_factor(place, upper, inverse, projected, 3, last[0], LONG)
    held_last, half = add_pass(shares, half)
    shares = [held_last] + [swap(held_last, "rows", mask) for mask in range(GROUP, count, GROUP)]
    totals = stacked(far_shares, shares)
    others = swap(totals, "cols", 1)
    half = lax.ppermute(half, "cols", [(0, 1)])

    cross = joined(place, totals, others)
    r_panels, multipliers = finish(
        place, upper, solved, half, swap(half, "rows", 1), near_gather(cross)
    )
    return (r_panels, multipliers[0])


def shards_general(sens_base, design_field, gradient, tile_index, type_codes):
    rows_here = design_field.shape[0]
    grid_width = design_field.shape[1]
    cols_here = sens_base.shape[1]
    factored = 2 * PW
    padded = padded_2(design_field, (("rows", 0),), 1)
    padded = jnp.pad(padded, ((0, 0), (1, 1)))
    north_cells = padded[:-2, 1:-1]
    south_cells = padded[2:, 1:-1]
    west_cells = padded[1:-1, :-2]
    east_cells = padded[1:-1, 2:]
    laplace = 4.0 * design_field - (north_cells + south_cells + west_cells + east_cells)
    slope_x = 0.5 * (east_cells - west_cells)
    slope_y = 0.5 * (south_cells - north_cells)
    stencils = jnp.stack([laplace, slope_x, slope_y]).reshape(3, -1)
    row_glob = lax.axis_index("rows") * rows_here + jnp.arange(rows_here, dtype=jnp.int32)
    col_ids = jnp.arange(grid_width, dtype=jnp.int32) // TILE
    cell_tile = ((row_glob // TILE)[:, None] * (grid_width // TILE) + col_ids[None, :]).reshape(-1)
    local_jac = assemble(sens_base, tile_index, type_codes, stencils, cell_tile)
    grad_flat = gradient.reshape(-1)
    row_major = lax.all_to_all(local_jac, "cols", split_axis=0, concat_axis=1, tiled=True)
    row_piece = row_major.shape[0]
    grad_part = lax.dynamic_slice_in_dim(
        grad_flat, lax.axis_index("cols") * row_piece, row_piece, 0
    )
    leading = row_major[:, :factored]
    gram_block = lax.dot_general(
        leading, row_major, (((0,), (0,)), ((), ())), preferred_element_type=jnp.float32
    )
    projected = jnp.dot(grad_part, leading, preferred_element_type=jnp.float32)
    gram_block, projected = lax.psum((gram_block, projected), ("rows", "cols"))
    gram_head = gram_block[:, :factored]
    gram_own = lax.dynamic_slice_in_dim(
        gram_block, lax.axis_index("cols") * cols_here, cols_here, 1
    )
    _, inverse, multipliers = factor(gram_head, projected[None, :])
    r_panels = matmul(inverse, gram_own)
    return (r_panels, multipliers[0])


def solution(mesh):
    placed = (P("rows", "cols"), P("rows", None), P("rows", None), P("cols"), P("cols"))
    pairs = mesh.shape["cols"] == 2 and mesh.shape["rows"] in (8, 16, 32, 64)
    return jax.shard_map(
        shards if pairs else shards_general,
        mesh=mesh,
        in_specs=placed,
        out_specs=(P(None, "cols"), P()),
        check_vma=False,
    )
```

```python
import functools

import jax
import jax.numpy as jnp
from jax import lax
from jax.experimental import pallas as pl
from jax.experimental.pallas import tpu as pltpu
from jax.sharding import PartitionSpec as P

TILE = 128
PW = 256
BLOCK = 128
FEATURES = 80
KEY_ROWS = 16
STEP_ROWS = 1024
COPY_ROWS = 256
OWN_CUTS = 4
GROUP = 4
HIGHEST = lax.Precision.HIGHEST
VMEM = pl.BlockSpec(memory_space=pltpu.VMEM)
SMEM = pl.BlockSpec(memory_space=pltpu.SMEM)
LIMIT = 12 * 2**20
WIDE_LIMIT = 48 * 2**20
ANY = pl.BlockSpec(memory_space=pl.ANY)
LONG = pl.CostEstimate(flops=8 * 10**9, bytes_accessed=1000, transcendentals=0)
BRIEF = pl.CostEstimate(flops=1000, bytes_accessed=1000, transcendentals=0)


def padded_2(cells, sides, width):
    for axis, dim in sides:
        count = lax.axis_size(axis)
        ends = count - 1
        head = lax.slice_in_dim(cells, 0, width, axis=dim)
        tail = lax.slice_in_dim(cells, cells.shape[dim] - width, cells.shape[dim], axis=dim)
        cells = jnp.concatenate(
            [
                lax.ppermute(tail, axis, [(i, (i + 1) % count) for i in range(ends)]),
                cells,
                lax.ppermute(head, axis, [((i + 1) % count, i) for i in range(ends)]),
            ],
            axis=dim,
        )
    return cells


def assemble(base_cols, tile_cols, type_cols, stencils, cell_tile):
    kinds_all = jnp.arange(3, dtype=jnp.int32)
    chooser = (type_cols[None, :] == kinds_all[:, None]).astype(jnp.float32)
    picked = lax.dot_general(
        stencils,
        chooser,
        (((0,), (0,)), ((), ())),
        precision=lax.Precision.HIGHEST,
        preferred_element_type=jnp.float32,
    )
    inside = cell_tile[:, None] == tile_cols[None, :]
    total = base_cols.astype(jnp.float32) + jnp.where(inside, picked / TILE, 0.0)
    return total.astype(jnp.bfloat16)


def matmul(left, right):
    return jnp.dot(left, right, precision=HIGHEST, preferred_element_type=jnp.float32)


def inverse_root(value):
    guess = lax.rsqrt(value)
    return guess * (1.5 - 0.5 * value * guess * guess)


def reciprocal(value):
    guess = pl.reciprocal(value, approx=True)
    guess = guess * (2.0 - value * guess)
    return guess * (2.0 - value * guess)


def lane(part, index):
    return jnp.broadcast_to(part[:, index : index + 1], part.shape)


def sublane(part, index):
    return jnp.broadcast_to(part[index : index + 1, :], part.shape)


def diagonal_inverse(block):
    groups = BLOCK // 8
    shape = (8, BLOCK)
    lanes = lax.broadcasted_iota(jnp.int32, shape, 1)
    subs = lax.broadcasted_iota(jnp.int32, shape, 0)
    parts = [block[8 * g : 8 * g + 8, :] for g in range(groups)]
    whole = []
    for p in range(groups):
        part, first = parts[p], 8 * p
        cols = [lane(part, first + k) for k in range(8)]
        inv = [None] * 8
        low = [jnp.zeros(shape, jnp.float32) for _ in range(8)]
        pivots = jnp.ones(shape, jnp.float32)
        for j in range(8):
            here = subs == j
            pivot = sublane(cols[j], j)
            ratio = reciprocal(pivot)
            pivots = jnp.where(here, pivot, pivots)
            for k in range(j):
                low[k] = jnp.where(here, inv[k], low[k])
            low[j] = jnp.where(here, 1.0, low[j])
            column = cols[j]
            for k in range(j + 1, 8):
                row = sublane(cols[k], j) * ratio
                cols[k] = jnp.where(here, row, cols[k] - column * row)
            for k in range(j):
                row = sublane(inv[k], j) * ratio
                inv[k] = jnp.where(here, row, inv[k] - column * row)
            inv[j] = jnp.where(here, ratio, -column * ratio)
        scale = inverse_root(pivots)
        inside = (lanes >= first) & (lanes < first + 8)
        unit = jnp.where(lanes - first == subs, 1.0, 0.0)
        rows = jnp.where(inside, unit, part)
        spread = [sublane(rows, k) for k in range(8)]
        solved = sum(low[k] * spread[k] for k in range(8)) * scale
        whole.append(jnp.where(lanes < first + 8, solved, 0.0))
        if p + 1 < groups:
            step = sum(inv[k] * spread[k] for k in range(8))
            step = [sublane(step, k) for k in range(8)]
            for g in range(p + 1, groups):
                taken = sum(lane(parts[g], first + k) * step[k] for k in range(8))
                parts[g] = jnp.where(inside, 0.0, parts[g]) - taken
    return jnp.concatenate(whole, axis=0)


def factor_steps(upper_ref, inverse_ref, first, last):
    blocks = upper_ref.shape[0] // BLOCK

    @pl.loop(first, last)
    def _(step):
        mine = pl.ds(pl.multiple_of(step * BLOCK, BLOCK), BLOCK)
        small = diagonal_inverse(upper_ref[mine, mine])
        upper_ref[mine, :] = matmul(small, upper_ref[mine, :])
        inverse_ref[mine, :] = matmul(small, inverse_ref[mine, :])

        @pl.loop(step + 1, blocks)
        def _(later):
            theirs = pl.ds(pl.multiple_of(later * BLOCK, BLOCK), BLOCK)
            factor = upper_ref[mine, theirs]

            def minus(target):
                target[theirs, :] -= lax.dot_general(
                    factor,
                    target[mine, :],
                    (((0,), (0,)), ((), ())),
                    precision=HIGHEST,
                    preferred_element_type=jnp.float32,
                )

            minus(upper_ref)
            minus(inverse_ref)


def start_inverse(inverse_ref):
    rows = lax.broadcasted_iota(jnp.int32, inverse_ref.shape, 0)
    cols = lax.broadcasted_iota(jnp.int32, inverse_ref.shape, 1)
    inverse_ref[...] = jnp.where(rows == cols, 1.0, 0.0)


def keep_upper(upper_ref):
    rows = lax.broadcasted_iota(jnp.int32, upper_ref.shape, 0)
    cols = lax.broadcasted_iota(jnp.int32, upper_ref.shape, 1)
    upper_ref[...] = jnp.where(rows <= cols, upper_ref[...], 0.0)


def solve_twice(inverse_ref, projected_ref):
    half = jnp.sum(inverse_ref[...] * projected_ref[...], axis=1, keepdims=True)
    return jnp.sum(inverse_ref[...] * half, axis=0, keepdims=True)


def factor_kernel(gram_ref, projected_ref, upper_ref, inverse_ref, multipliers_ref):
    upper_ref[...] = gram_ref[...]
    start_inverse(inverse_ref)
    factor_steps(upper_ref, inverse_ref, 0, upper_ref.shape[0] // BLOCK)
    keep_upper(upper_ref)
    multipliers_ref[...] = solve_twice(inverse_ref, projected_ref)


def factor(gram, projected):
    order = gram.shape[0]
    return pl.pallas_call(
        factor_kernel,
        out_shape=(
            jax.ShapeDtypeStruct((order, order), jnp.float32),
            jax.ShapeDtypeStruct((order, order), jnp.float32),
            jax.ShapeDtypeStruct((1, order), jnp.float32),
        ),
        in_specs=[pl.BlockSpec(memory_space=pltpu.VMEM)] * 2,
        out_specs=[pl.BlockSpec(memory_space=pltpu.VMEM)] * 3,
        compiler_params=pltpu.CompilerParams(vmem_limit_bytes=LIMIT),
        cost_estimate=pl.CostEstimate(
            flops=6 * order**3, bytes_accessed=12 * order**2, transcendentals=0
        ),
    )(gram, projected)


def features_kernel(field_ref, north_ref, south_ref, out_ref):
    field = field_ref[...]
    rows, width = field.shape
    lanes = lax.broadcasted_iota(jnp.int32, field.shape, 1)
    north = jnp.concatenate([north_ref[...], field[:-1]], axis=0)
    south = jnp.concatenate([field[1:], south_ref[...]], axis=0)
    west = jnp.where(lanes == 0, 0.0, pltpu.roll(field, 1, 1))
    east = jnp.where(lanes == width - 1, 0.0, pltpu.roll(field, width - 1, 1))
    laplace = 4.0 * field - (north + south + west + east)
    slope_x = 0.5 * (east - west)
    slope_y = 0.5 * (south - north)
    parts = []
    for stencil in (laplace, slope_x, slope_y):
        rest = stencil / TILE
        for _ in range(3):
            part = rest.astype(jnp.bfloat16).astype(jnp.float32)
            parts.append(part)
            rest = rest - part
    tiles = width // TILE
    shape = (FEATURES, width)
    owner = lax.broadcasted_iota(jnp.int32, shape, 0) // len(parts)
    tile = lax.broadcasted_iota(jnp.int32, shape, 1) // TILE
    blank = jnp.zeros((FEATURES - tiles * len(parts), width), jnp.float32)
    for row in range(rows):
        block = jnp.concatenate([part[row : row + 1] for part in parts], axis=0)
        whole = jnp.concatenate([block] * tiles + [blank], axis=0)
        out_ref[row] = jnp.where(owner == tile, whole, 0.0).astype(jnp.bfloat16)


def features(field, north, south):
    rows, width = field.shape
    return pl.pallas_call(
        features_kernel,
        out_shape=jax.ShapeDtypeStruct((rows, FEATURES, width), jnp.bfloat16),
        in_specs=[VMEM] * 3,
        out_specs=VMEM,
        compiler_params=pltpu.CompilerParams(vmem_limit_bytes=LIMIT),
        cost_estimate=BRIEF,
    )(field, north, south)


def assembled(base, feature, key, first):
    rows = lax.broadcasted_iota(jnp.int32, (FEATURES, key.shape[1]), 0) // 3 + first
    chooser = jnp.where(rows.astype(jnp.float32) == key, 1.0, 0.0).astype(jnp.bfloat16)
    added = lax.dot_general(
        feature, chooser, (((0,), (0,)), ((), ())), preferred_element_type=jnp.float32
    )
    return (base.astype(jnp.float32) + added).astype(jnp.bfloat16)


def transposed_dot(left, right):
    return lax.dot_general(
        left, right, (((0,), (0,)), ((), ())), preferred_element_type=jnp.float32
    )


def strict_blocks(order):
    count = order // BLOCK
    return [(a, b) for a in range(count) for b in range(a + 1, count)]


def packed_rows(order):
    count = order // BLOCK
    used = (len(strict_blocks(order)) + count // 2) * BLOCK + count // 2 + count
    return -(-used // (8 * GROUP)) * 8 * GROUP


def triangles():
    rows = lax.broadcasted_iota(jnp.int32, (BLOCK, BLOCK), 0)
    cols = lax.broadcasted_iota(jnp.int32, (BLOCK, BLOCK), 1)
    return rows < cols, rows == cols


def at(index):
    return pl.ds(index * BLOCK, BLOCK)


def pack_gram(packed, gram, projected):
    order = gram.shape[0]
    packed[...] = jnp.zeros_like(packed)
    blocks = strict_blocks(order)
    for index, (a, b) in enumerate(blocks):
        packed[at(index), :] = gram[at(a), at(b)]
    above, diagonal = triangles()
    pairs = order // BLOCK // 2
    row = (len(blocks) + pairs) * BLOCK
    for p in range(pairs):
        second = gram[at(2 * p + 1), at(2 * p + 1)]
        packed[at(len(blocks) + p), :] = jnp.where(
            above | diagonal, gram[at(2 * p), at(2 * p)], second
        )
        packed[pl.ds(row + p, 1), :] = jnp.sum(
            jnp.where(diagonal, second, 0.0), axis=0, keepdims=True
        )
    for c in range(order // BLOCK):
        packed[pl.ds(row + pairs + c, 1), :] = projected[:, at(c)]


def unpack_gram(packed, upper_ref, projected_ref):
    order = upper_ref.shape[0]
    upper_ref[...] = jnp.zeros_like(upper_ref)
    blocks = strict_blocks(order)
    for index, (a, b) in enumerate(blocks):
        upper_ref[at(a), at(b)] = packed[at(index), :]
    above, diagonal = triangles()
    pairs = order // BLOCK // 2
    row = (len(blocks) + pairs) * BLOCK
    for p in range(pairs):
        both = packed[at(len(blocks) + p), :]
        turned = both.T
        upper_ref[at(2 * p), at(2 * p)] = jnp.where(above | diagonal, both, turned)
        upper_ref[at(2 * p + 1), at(2 * p + 1)] = jnp.where(
            diagonal, packed[pl.ds(row + p, 1), :], jnp.where(above, turned, both)
        )
    for c in range(order // BLOCK):
        projected_ref[:, at(c)] = packed[pl.ds(row + pairs + c, 1), :]


def own_kernel(
    place_ref, *refs
):
    bases = refs[:OWN_CUTS]
    feature_ref, tile_ref, type_ref, grad_ref, jac_ref = refs[OWN_CUTS : OWN_CUTS + 5]
    outs = refs[OWN_CUTS + 5 : OWN_CUTS + 5 + GROUP]
    gram, projected, packed = refs[OWN_CUTS + 5 + GROUP :]
    step = pl.program_id(0)
    half = pl.num_programs(0) // 2
    order = gram.shape[0]
    base = jnp.concatenate([ref[...] for ref in bases], axis=0)
    key = (tile_ref[...] * 3 + type_ref[...]).astype(jnp.float32)
    jac = assembled(base, feature_ref[0], key, place_ref[2])

    @pl.when(step // half == place_ref[0])
    def _():
        jac_ref[...] = jac

    @pl.when(step == 0)
    def _():
        gram[...] = jnp.zeros_like(gram)
        projected[...] = jnp.zeros_like(projected)

    middle = order // 2
    gram[:middle, :] += transposed_dot(jac[:, :middle], jac)
    gram[middle:, middle:] += transposed_dot(jac[:, middle:], jac[:, middle:])
    projected[...] += jnp.dot(grad_ref[0], jac, preferred_element_type=jnp.float32)

    @pl.when(step == pl.num_programs(0) - 1)
    def _():
        pack_gram(packed, gram, projected)
        size = outs[0].shape[0]
        for mask in range(GROUP):
            start = pl.multiple_of((place_ref[1] ^ mask) * size, 8)
            outs[mask][...] = packed[pl.ds(start, size), :]


def cut_index(cut, i, place):
    return (OWN_CUTS * i + cut, 0)


def own_part(place, base, feature, tile_row, type_row, gradient):
    cells, order = base.shape
    rows, width = gradient.shape
    half = rows // 2
    size = packed_rows(order) // GROUP
    return pl.pallas_call(
        own_kernel,
        grid_spec=pltpu.PrefetchScalarGridSpec(
            num_scalar_prefetch=1,
            grid=(rows,),
            in_specs=[
                pl.BlockSpec((width // OWN_CUTS, order), functools.partial(cut_index, k))
                for k in range(OWN_CUTS)
            ]
            + [
                pl.BlockSpec((1, FEATURES, width), lambda i, s: (i, 0, 0)),
                pl.BlockSpec((1, order), lambda i, s: (0, 0)),
                pl.BlockSpec((1, order), lambda i, s: (0, 0)),
                pl.BlockSpec((1, 1, width), lambda i, s: (i, 0, 0)),
            ],
            out_specs=[
                pl.BlockSpec(
                    (width, order), lambda i, s: (jnp.clip(i - s[0] * half, 0, half - 1), 0)
                )
            ]
            + [pl.BlockSpec((size, BLOCK), lambda i, s: (0, 0))] * GROUP,
            scratch_shapes=[
                pltpu.VMEM((order, order), jnp.float32),
                pltpu.VMEM((1, order), jnp.float32),
                pltpu.VMEM((GROUP * size, BLOCK), jnp.float32),
            ],
        ),
        out_shape=[jax.ShapeDtypeStruct((cells // 2, order), jnp.bfloat16)]
        + [jax.ShapeDtypeStruct((size, BLOCK), jnp.float32)] * GROUP,
        compiler_params=pltpu.CompilerParams(vmem_limit_bytes=WIDE_LIMIT),
        cost_estimate=BRIEF,
    )(place, *[base] * OWN_CUTS, feature, tile_row, type_row, gradient.reshape(rows, 1, width))


def send_kernel(pieces, place_ref, base_ref, tile_ref, type_ref, *refs):
    outs, (held, tiles, types, sems) = refs[-4 - len(pieces) : -4], refs[-4:]
    half = base_ref.shape[0] // 2
    low = min(piece[0] for piece in pieces)
    first = (1 - place_ref[0]) * half + low
    chunks = held.shape[0] // COPY_ROWS
    copies = [
        pltpu.make_async_copy(
            base_ref.at[pl.ds(pl.multiple_of(first + k * COPY_ROWS, COPY_ROWS), COPY_ROWS), :],
            held.at[pl.ds(k * COPY_ROWS, COPY_ROWS), :],
            sems.at[k],
        )
        for k in range(chunks)
    ]
    copies.append(pltpu.make_async_copy(tile_ref, tiles, sems.at[chunks]))
    copies.append(pltpu.make_async_copy(type_ref, types, sems.at[chunks + 1]))
    for copy in copies:
        copy.start()
    for k in range(chunks):
        copies[k].wait()
        for (top, end, left, right, _), out in zip(pieces, outs):
            row = low + k * COPY_ROWS
            if top <= row < end:
                out[pl.ds(row - top, COPY_ROWS), :] = held[
                    pl.ds(k * COPY_ROWS, COPY_ROWS), left:right
                ]
    copies[chunks].wait()
    copies[chunks + 1].wait()
    for (top, end, left, right, keyed), out in zip(pieces, outs):
        if keyed:
            key = (tiles[:, left:right] * 3 + types[:, left:right]).astype(jnp.float32)
            key = jnp.broadcast_to(key, (KEY_ROWS, right - left))
            out[pl.ds(end - top, KEY_ROWS), :] = key.astype(jnp.bfloat16)


def send_parts(place, base, tile_row, type_row, pieces):
    order = base.shape[1]
    span = max(piece[1] for piece in pieces) - min(piece[0] for piece in pieces)
    return pl.pallas_call(
        functools.partial(send_kernel, tuple(pieces)),
        in_specs=[SMEM, ANY, ANY, ANY],
        out_specs=[VMEM] * len(pieces),
        out_shape=[
            jax.ShapeDtypeStruct((end - top + KEY_ROWS * keyed, right - left), base.dtype)
            for top, end, left, right, keyed in pieces
        ],
        scratch_shapes=[
            pltpu.VMEM((span, order), base.dtype),
            pltpu.VMEM((1, order), jnp.int32),
            pltpu.VMEM((1, order), jnp.int32),
            pltpu.SemaphoreType.DMA((span // COPY_ROWS + 2,)),
        ],
        compiler_params=pltpu.CompilerParams(vmem_limit_bytes=WIDE_LIMIT + 6 * 2**20),
        cost_estimate=BRIEF,
    )(place, base, tile_row, type_row)


def cross_kernel(pieces, place_ref, jac_ref, feature_ref, *refs):
    received = refs[:pieces]
    outs = refs[-2 - GROUP : -2]
    total, out_ref = refs[-2:]
    cells, width = jac_ref.shape[0], feature_ref.shape[2]
    cuts = width // STEP_ROWS
    first = place_ref[0] * (cells // width)
    keyed = received[0].shape[0] - KEY_ROWS
    key = received[0][pl.ds(keyed, KEY_ROWS), :][0:1, :].astype(jnp.float32)
    total[...] = jnp.zeros_like(total)
    done = 0
    for piece in received:
        count = piece.shape[0] // STEP_ROWS

        @pl.loop(0, count)
        def _(step, piece=piece, done=done):
            rows = pl.ds(pl.multiple_of(step * STEP_ROWS, STEP_ROWS), STEP_ROWS)
            step = step + done
            mine = pl.ds(pl.multiple_of(step * STEP_ROWS, STEP_ROWS), STEP_ROWS)
            lanes = pl.ds(pl.multiple_of(step % cuts * STEP_ROWS, STEP_ROWS), STEP_ROWS)
            feature = feature_ref[first + step // cuts, :, lanes]
            other = assembled(piece[rows, :], feature, key, place_ref[2])
            total[...] += transposed_dot(other, jac_ref[mine, :])

        done += count

    count = total.shape[1] // BLOCK
    part = BLOCK // GROUP

    blocks = total.shape[0] // BLOCK

    @pl.when(place_ref[0] == 0)
    def _():
        for k in range(blocks):
            for q in range(GROUP):
                for c in range(count):
                    out_ref[q, pl.ds(BLOCK * k + part * c, part), :] = total[
                        pl.ds(BLOCK * k + part * q, part), pl.ds(BLOCK * c, BLOCK)
                    ]

    @pl.when(place_ref[0] != 0)
    def _():
        for k in range(blocks):
            for c in range(count):
                block = total[pl.ds(BLOCK * k, BLOCK), pl.ds(BLOCK * c, BLOCK)].T
                for q in range(GROUP):
                    out_ref[q, pl.ds(BLOCK * k + part * c, part), :] = block[
                        part * q : part * q + part
                    ]

    for mask in range(GROUP):
        outs[mask][...] = out_ref[place_ref[1] ^ mask]


def cross_part(place, received, jac, feature, *after):
    width_recv, order = received[0].shape[1], jac.shape[1]
    return pl.pallas_call(
        functools.partial(cross_kernel, len(received)),
        in_specs=[SMEM] + [VMEM] * (2 + len(received)) + [ANY] * len(after),
        out_specs=[VMEM] * GROUP,
        out_shape=[jax.ShapeDtypeStruct((width_recv, BLOCK), jnp.float32)] * GROUP,
        scratch_shapes=[
            pltpu.VMEM((width_recv, order), jnp.float32),
            pltpu.VMEM((GROUP, width_recv, BLOCK), jnp.float32),
        ],
        compiler_params=pltpu.CompilerParams(vmem_limit_bytes=LIMIT),
        cost_estimate=BRIEF,
    )(place, jac, feature, *received, *after)


def swap(value, axis, mask):
    count = lax.axis_size(axis)
    return lax.ppermute(value, axis, [(i, i ^ mask) for i in range(count)])


def add_kernel(count, *refs):
    refs[-1][...] = sum(ref[...] for ref in refs[1:count]) + refs[0][...]


def add(values, *after):
    return pl.pallas_call(
        functools.partial(add_kernel, len(values)),
        out_shape=jax.ShapeDtypeStruct(values[0].shape, values[0].dtype),
        in_specs=[VMEM] * len(values) + [ANY] * len(after),
        out_specs=VMEM,
        compiler_params=pltpu.CompilerParams(vmem_limit_bytes=LIMIT),
        cost_estimate=BRIEF,
    )(*values, *after)


def add_pass_kernel(*refs):
    *values, passed_ref, out_ref, copy_ref = refs
    out_ref[...] = sum(ref[...] for ref in values[1:]) + values[0][...]
    copy_ref[...] = passed_ref[...]


def add_pass(values, passed):
    return pl.pallas_call(
        add_pass_kernel,
        out_shape=[jax.ShapeDtypeStruct(v.shape, v.dtype) for v in (values[0], passed)],
        in_specs=[VMEM] * (len(values) + 1),
        out_specs=[VMEM] * 2,
        compiler_params=pltpu.CompilerParams(vmem_limit_bytes=LIMIT),
        cost_estimate=BRIEF,
    )(*values, passed)


def stacked_kernel(count, *refs):
    first, second, out_ref = refs[:count], refs[count:-1], refs[-1]
    rows = first[0].shape[0]
    out_ref[:rows, :] = sum(ref[...] for ref in first[1:]) + first[0][...]
    out_ref[rows:, :] = sum(ref[...] for ref in second[1:]) + second[0][...]


def stacked(first, second):
    rows = first[0].shape[0] + second[0].shape[0]
    return pl.pallas_call(
        functools.partial(stacked_kernel, len(first)),
        out_shape=jax.ShapeDtypeStruct((rows, BLOCK), jnp.float32),
        in_specs=[VMEM] * (len(first) + len(second)),
        out_specs=VMEM,
        compiler_params=pltpu.CompilerParams(vmem_limit_bytes=LIMIT),
        cost_estimate=BRIEF,
    )(*first, *second)


def joined_kernel(own_ref, other_ref, out_ref):
    part = BLOCK // GROUP
    blocks = own_ref.shape[0] // BLOCK
    for a in range(blocks):
        for b in range(blocks):
            out_ref[pl.ds(part * b, part), at(a)] = (
                own_ref[pl.ds(BLOCK * a + part * b, part), :]
                + other_ref[pl.ds(BLOCK * b + part * a, part), :]
            )


def joined(own, other):
    order = own.shape[0]
    return pl.pallas_call(
        joined_kernel,
        out_shape=jax.ShapeDtypeStruct((order // GROUP, order), jnp.float32),
        in_specs=[VMEM] * 2,
        out_specs=VMEM,
        compiler_params=pltpu.CompilerParams(vmem_limit_bytes=LIMIT),
        cost_estimate=BRIEF,
    )(own, other)


def group_swaps(parts):
    return [parts[0]] + [swap(parts[mask], "rows", mask) for mask in range(1, GROUP)]


def group_sum(parts):
    got = group_swaps(parts)
    return got[0] + got[1] + got[2] + got[3]


def groups_sum(held):
    masks = range(GROUP, lax.axis_size("rows"), GROUP)
    return held + sum(swap(held, "rows", mask) for mask in masks)


def doubled(held, masks):
    for mask in masks:
        held = held + swap(held, "rows", mask)
    return held


def rows_gather(own):
    return [own] + [swap(own, "rows", mask) for mask in range(1, GROUP)]


def near_gather(own):
    near, far = swap(own, "rows", 1), swap(own, "rows", 2)
    return [own, near, far, swap(far, "rows", 1)]


def first_factor_kernel(last, place_ref, *refs):
    pieces = refs[:GROUP]
    upper_ref, inverse_ref, projected_ref, whole = refs[GROUP + 1 :]
    size = pieces[0].shape[0]
    for mask in range(GROUP):
        start = pl.multiple_of((place_ref[1] ^ mask) * size, 8)
        whole[pl.ds(start, size), :] = pieces[mask][...]
    unpack_gram(whole, upper_ref, projected_ref)
    start_inverse(inverse_ref)
    factor_steps(upper_ref, inverse_ref, 0, last)


def square(order):
    return jax.ShapeDtypeStruct((order, order), jnp.float32)


def row(order):
    return jax.ShapeDtypeStruct((1, order), jnp.float32)


def first_factor(place, pieces, order, last, after):
    return pl.pallas_call(
        functools.partial(first_factor_kernel, last),
        out_shape=(square(order), square(order), row(order)),
        in_specs=[SMEM] + [VMEM] * GROUP + [ANY],
        out_specs=[VMEM] * 3,
        scratch_shapes=[pltpu.VMEM((packed_rows(order), BLOCK), jnp.float32)],
        compiler_params=pltpu.CompilerParams(vmem_limit_bytes=LIMIT),
        cost_estimate=BRIEF,
    )(place, *pieces, after)


def more_factor_kernel(first, last, upper_in, inverse_in, _, upper_ref, inverse_ref):
    del upper_in, inverse_in
    factor_steps(upper_ref, inverse_ref, first, last)


def more_factor(upper, inverse, first, last, after, cost):
    order = upper.shape[0]
    return pl.pallas_call(
        functools.partial(more_factor_kernel, first, last),
        out_shape=[square(order)] * 2,
        in_specs=[VMEM] * 2 + [ANY],
        out_specs=[VMEM] * 2,
        input_output_aliases={0: 0, 1: 1},
        compiler_params=pltpu.CompilerParams(vmem_limit_bytes=LIMIT),
        cost_estimate=cost,
    )(upper, inverse, after)


def lower_blocks(order):
    return [(a, b) for a in range(order // BLOCK) for b in range(a + 1)]


def lower_half(order):
    rows = len(lower_blocks(order)) * BLOCK + order // BLOCK
    return -(-rows // 16) * 8


def last_factor_kernel(
    first, place_ref, upper_in, inverse_in, projected, _, upper_ref, inverse, out_ref, half_ref, packed
):
    del upper_in, inverse_in
    order = upper_ref.shape[0]
    factor_steps(upper_ref, inverse, first, order // BLOCK)
    keep_upper(upper_ref)
    solved = solve_twice(inverse, projected)
    out_ref[...] = solved
    blocks = lower_blocks(order)
    for index, (a, b) in enumerate(blocks):
        packed[pl.ds(index * BLOCK, BLOCK), :] = inverse[
            pl.ds(a * BLOCK, BLOCK), pl.ds(b * BLOCK, BLOCK)
        ]
    start = len(blocks) * BLOCK
    packed[start:, :] = jnp.zeros((packed.shape[0] - start, BLOCK), jnp.float32)
    for c in range(order // BLOCK):
        packed[pl.ds(start + c, 1), :] = solved[:, c * BLOCK : (c + 1) * BLOCK]
    size = half_ref.shape[0]
    half_ref[...] = packed[pl.ds(pl.multiple_of(place_ref[1] % 2 * size, 8), size), :]


def last_factor(place, upper, inverse, projected, first, after, cost):
    order = upper.shape[0]
    size = lower_half(order)
    return pl.pallas_call(
        functools.partial(last_factor_kernel, first),
        out_shape=(
            square(order),
            square(order),
            row(order),
            jax.ShapeDtypeStruct((size, BLOCK), jnp.float32),
        ),
        in_specs=[SMEM] + [VMEM] * 3 + [ANY],
        out_specs=[VMEM] * 4,
        input_output_aliases={1: 0, 2: 1},
        scratch_shapes=[pltpu.VMEM((2 * size, BLOCK), jnp.float32)],
        compiler_params=pltpu.CompilerParams(vmem_limit_bytes=LIMIT),
        cost_estimate=cost,
    )(place, upper, inverse, projected, after)


def three_products(left, right):
    def parts(value):
        high = value.astype(jnp.bfloat16)
        return high, (value - high.astype(jnp.float32)).astype(jnp.bfloat16)

    def dot(a, b):
        return lax.dot_general(
            a, b, (((1,), (1,)), ((), ())), preferred_element_type=jnp.float32
        )

    (high, low), (other_high, other_low) = parts(left), parts(right)
    return dot(high, other_high) + (dot(high, other_low) + dot(low, other_high))


def finish_kernel(place_ref, upper_ref, solved_ref, half_ref, other_ref, *refs):
    pieces = refs[:GROUP]
    out_ref, multipliers_ref, cross, packed, inverse = refs[GROUP:]
    order = upper_ref.shape[0]
    part = BLOCK // GROUP

    @pl.when(place_ref[0] == 0)
    def _():
        out_ref[...] = upper_ref[...]
        multipliers_ref[...] = solved_ref[...]

    @pl.when(place_ref[0] != 0)
    def _():
        size = half_ref.shape[0]
        core = place_ref[1] % 2
        packed[pl.ds(pl.multiple_of(core * size, 8), size), :] = half_ref[...]
        packed[pl.ds(pl.multiple_of((1 - core) * size, 8), size), :] = other_ref[...]
        blocks = lower_blocks(order)
        for index, (a, b) in enumerate(blocks):
            inverse[pl.ds(a * BLOCK, BLOCK), pl.ds(b * BLOCK, BLOCK)] = packed[
                pl.ds(index * BLOCK, BLOCK), :
            ]
        for c in range(order // BLOCK):
            multipliers_ref[:, pl.ds(c * BLOCK, BLOCK)] = packed[
                pl.ds(len(blocks) * BLOCK + c, 1), :
            ]
        for mask in range(GROUP):
            quarter = place_ref[1] ^ mask
            for b in range(order // BLOCK):
                start = pl.multiple_of(BLOCK * b + part * quarter, part)
                cross[pl.ds(start, part), :] = pieces[mask][pl.ds(part * b, part), :]
        for a in range(order // BLOCK):
            rows, depth = pl.ds(a * BLOCK, BLOCK), (a + 1) * BLOCK
            out_ref[rows, :] = three_products(
                inverse[rows, pl.ds(0, depth)], cross[:, pl.ds(0, depth)]
            )


def finish(place, upper, solved, half, other, pieces):
    order = upper.shape[0]
    return pl.pallas_call(
        finish_kernel,
        out_shape=(square(order), row(order)),
        in_specs=[SMEM] + [VMEM] * (4 + GROUP),
        out_specs=[VMEM] * 2,
        scratch_shapes=[
            pltpu.VMEM((order, order), jnp.float32),
            pltpu.VMEM((2 * lower_half(order), BLOCK), jnp.float32),
            pltpu.VMEM((order, order), jnp.float32),
        ],
        compiler_params=pltpu.CompilerParams(vmem_limit_bytes=LIMIT),
        cost_estimate=BRIEF,
    )(place, upper, solved, half, other, *pieces)


def shards(sens_base, design_field, gradient, tile_index, type_codes):
    cells, order = sens_base.shape
    rows_here, width = design_field.shape
    side = lax.axis_index("cols")
    quarter = lax.axis_index("rows") % GROUP
    tiles = width // TILE
    first_tile = lax.axis_index("rows") * rows_here // TILE * tiles
    place = jnp.stack([side, quarter, 3 * first_tile]).astype(jnp.int32)
    tile_row, type_row = tile_index[None, :], type_codes[None, :]

    half, split = cells // 2, order - BLOCK
    sent = send_parts(
        place,
        sens_base,
        tile_row,
        type_row,
        [(0, half, 0, split, True), (0, half, split, order, True)],
    )
    received = [[swap(part, "cols", 1)] for part in sent]

    count = lax.axis_size("rows")
    north = lax.ppermute(design_field[-1:], "rows", [(i, i + 1) for i in range(count - 1)])
    south = lax.ppermute(design_field[:1], "rows", [(i + 1, i) for i in range(count - 1)])
    feature = features(design_field, north, south)
    jac, *packed = own_part(place, sens_base, feature, tile_row, type_row, gradient)
    pieces = rows_gather(groups_sum(group_sum(packed)))

    def stage(index, *after):
        return cross_part(place, received[index], jac, feature, *after)

    upper, inverse, projected = first_factor(place, pieces, order, 1, pieces[0])
    first = stage(0, upper)
    shares = group_swaps(first)
    upper, inverse = more_factor(upper, inverse, 1, 2, first[0], LONG)
    held = add(shares, inverse)
    shares = [held, swap(held, "rows", GROUP)]
    upper, inverse = more_factor(upper, inverse, 2, 3, held, LONG)
    middle = add(shares, inverse)
    far = range(2 * GROUP, count, 2 * GROUP)
    far_shares = [middle] + [swap(middle, "rows", mask) for mask in far]
    last = stage(1, middle)
    shares = group_swaps(last)
    upper, _, solved, half = last_factor(place, upper, inverse, projected, 3, last[0], LONG)
    held_last, half = add_pass(shares, half)
    shares = [held_last] + [swap(held_last, "rows", mask) for mask in range(GROUP, count, GROUP)]
    totals = stacked(far_shares, shares)
    others = lax.ppermute(totals, "cols", [(0, 1)])
    half = lax.ppermute(half, "cols", [(0, 1)])

    cross = joined(totals, others)
    r_panels, multipliers = finish(
        place, upper, solved, half, swap(half, "rows", 1), near_gather(cross)
    )
    return (r_panels, multipliers[0])


def shards_general(sens_base, design_field, gradient, tile_index, type_codes):
    rows_here = design_field.shape[0]
    grid_width = design_field.shape[1]
    cols_here = sens_base.shape[1]
    factored = 2 * PW
    padded = padded_2(design_field, (("rows", 0),), 1)
    padded = jnp.pad(padded, ((0, 0), (1, 1)))
    north_cells = padded[:-2, 1:-1]
    south_cells = padded[2:, 1:-1]
    west_cells = padded[1:-1, :-2]
    east_cells = padded[1:-1, 2:]
    laplace = 4.0 * design_field - (north_cells + south_cells + west_cells + east_cells)
    slope_x = 0.5 * (east_cells - west_cells)
    slope_y = 0.5 * (south_cells - north_cells)
    stencils = jnp.stack([laplace, slope_x, slope_y]).reshape(3, -1)
    row_glob = lax.axis_index("rows") * rows_here + jnp.arange(rows_here, dtype=jnp.int32)
    col_ids = jnp.arange(grid_width, dtype=jnp.int32) // TILE
    cell_tile = ((row_glob // TILE)[:, None] * (grid_width // TILE) + col_ids[None, :]).reshape(-1)
    local_jac = assemble(sens_base, tile_index, type_codes, stencils, cell_tile)
    grad_flat = gradient.reshape(-1)
    row_major = lax.all_to_all(local_jac, "cols", split_axis=0, concat_axis=1, tiled=True)
    row_piece = row_major.shape[0]
    grad_part = lax.dynamic_slice_in_dim(
        grad_flat, lax.axis_index("cols") * row_piece, row_piece, 0
    )
    leading = row_major[:, :factored]
    gram_block = lax.dot_general(
        leading, row_major, (((0,), (0,)), ((), ())), preferred_element_type=jnp.float32
    )
    projected = jnp.dot(grad_part, leading, preferred_element_type=jnp.float32)
    gram_block, projected = lax.psum((gram_block, projected), ("rows", "cols"))
    gram_head = gram_block[:, :factored]
    gram_own = lax.dynamic_slice_in_dim(
        gram_block, lax.axis_index("cols") * cols_here, cols_here, 1
    )
    _, inverse, multipliers = factor(gram_head, projected[None, :])
    r_panels = matmul(inverse, gram_own)
    return (r_panels, multipliers[0])


def solution(mesh):
    placed = (P("rows", "cols"), P("rows", None), P("rows", None), P("cols"), P("cols"))
    pairs = mesh.shape["cols"] == 2 and mesh.shape["rows"] in (8, 16, 32, 64)
    return jax.shard_map(
        shards if pairs else shards_general,
        mesh=mesh,
        in_specs=placed,
        out_specs=(P(None, "cols"), P()),
        check_vma=False,
    )
```

```python
import functools

import jax
import jax.numpy as jnp
from jax import lax
from jax.experimental import pallas as pl
from jax.experimental.pallas import tpu as pltpu
from jax.sharding import PartitionSpec as P

TILE = 128
PW = 256
BLOCK = 128
FEATURES = 80
KEY_ROWS = 16
STEP_ROWS = 1024
COPY_ROWS = 256
OWN_CUTS = 4
GROUP = 4
HIGHEST = lax.Precision.HIGHEST
VMEM = pl.BlockSpec(memory_space=pltpu.VMEM)
SMEM = pl.BlockSpec(memory_space=pltpu.SMEM)
LIMIT = 12 * 2**20
WIDE_LIMIT = 48 * 2**20
TAIL_LIMIT = 36 * 2**20
ANY = pl.BlockSpec(memory_space=pl.ANY)
LONG = pl.CostEstimate(flops=8 * 10**9, bytes_accessed=1000, transcendentals=0)
BRIEF = pl.CostEstimate(flops=1000, bytes_accessed=1000, transcendentals=0)


def padded_2(cells, sides, width):
    for axis, dim in sides:
        count = lax.axis_size(axis)
        ends = count - 1
        head = lax.slice_in_dim(cells, 0, width, axis=dim)
        tail = lax.slice_in_dim(cells, cells.shape[dim] - width, cells.shape[dim], axis=dim)
        cells = jnp.concatenate(
            [
                lax.ppermute(tail, axis, [(i, (i + 1) % count) for i in range(ends)]),
                cells,
                lax.ppermute(head, axis, [((i + 1) % count, i) for i in range(ends)]),
            ],
            axis=dim,
        )
    return cells


def assemble(base_cols, tile_cols, type_cols, stencils, cell_tile):
    kinds_all = jnp.arange(3, dtype=jnp.int32)
    chooser = (type_cols[None, :] == kinds_all[:, None]).astype(jnp.float32)
    picked = lax.dot_general(
        stencils,
        chooser,
        (((0,), (0,)), ((), ())),
        precision=lax.Precision.HIGHEST,
        preferred_element_type=jnp.float32,
    )
    inside = cell_tile[:, None] == tile_cols[None, :]
    total = base_cols.astype(jnp.float32) + jnp.where(inside, picked / TILE, 0.0)
    return total.astype(jnp.bfloat16)


def matmul(left, right):
    return jnp.dot(left, right, precision=HIGHEST, preferred_element_type=jnp.float32)


def inverse_root(value):
    guess = lax.rsqrt(value)
    return guess * (1.5 - 0.5 * value * guess * guess)


def reciprocal(value):
    guess = pl.reciprocal(value, approx=True)
    guess = guess * (2.0 - value * guess)
    return guess * (2.0 - value * guess)


def lane(part, index):
    return jnp.broadcast_to(part[:, index : index + 1], part.shape)


def sublane(part, index):
    return jnp.broadcast_to(part[index : index + 1, :], part.shape)


def diagonal_inverse(block):
    groups = BLOCK // 8
    shape = (8, BLOCK)
    lanes = lax.broadcasted_iota(jnp.int32, shape, 1)
    subs = lax.broadcasted_iota(jnp.int32, shape, 0)
    parts = [block[8 * g : 8 * g + 8, :] for g in range(groups)]
    whole = []
    for p in range(groups):
        part, first = parts[p], 8 * p
        cols = [lane(part, first + k) for k in range(8)]
        inv = [None] * 8
        low = [jnp.zeros(shape, jnp.float32) for _ in range(8)]
        pivots = jnp.ones(shape, jnp.float32)
        for j in range(8):
            here = subs == j
            pivot = sublane(cols[j], j)
            ratio = reciprocal(pivot)
            pivots = jnp.where(here, pivot, pivots)
            for k in range(j):
                low[k] = jnp.where(here, inv[k], low[k])
            low[j] = jnp.where(here, 1.0, low[j])
            column = cols[j]
            for k in range(j + 1, 8):
                row = sublane(cols[k], j) * ratio
                cols[k] = jnp.where(here, row, cols[k] - column * row)
            for k in range(j):
                row = sublane(inv[k], j) * ratio
                inv[k] = jnp.where(here, row, inv[k] - column * row)
            inv[j] = jnp.where(here, ratio, -column * ratio)
        scale = inverse_root(pivots)
        inside = (lanes >= first) & (lanes < first + 8)
        unit = jnp.where(lanes - first == subs, 1.0, 0.0)
        rows = jnp.where(inside, unit, part)
        spread = [sublane(rows, k) for k in range(8)]
        solved = sum(low[k] * spread[k] for k in range(8)) * scale
        whole.append(jnp.where(lanes < first + 8, solved, 0.0))
        if p + 1 < groups:
            step = sum(inv[k] * spread[k] for k in range(8))
            step = [sublane(step, k) for k in range(8)]
            for g in range(p + 1, groups):
                taken = sum(lane(parts[g], first + k) * step[k] for k in range(8))
                parts[g] = jnp.where(inside, 0.0, parts[g]) - taken
    return jnp.concatenate(whole, axis=0)


def factor_steps(upper_ref, inverse_ref, first, last):
    blocks = upper_ref.shape[0] // BLOCK

    @pl.loop(first, last)
    def _(step):
        mine = pl.ds(pl.multiple_of(step * BLOCK, BLOCK), BLOCK)
        small = diagonal_inverse(upper_ref[mine, mine])
        upper_ref[mine, :] = matmul(small, upper_ref[mine, :])
        inverse_ref[mine, :] = matmul(small, inverse_ref[mine, :])

        @pl.loop(step + 1, blocks)
        def _(later):
            theirs = pl.ds(pl.multiple_of(later * BLOCK, BLOCK), BLOCK)
            factor = upper_ref[mine, theirs]

            def minus(target):
                target[theirs, :] -= lax.dot_general(
                    factor,
                    target[mine, :],
                    (((0,), (0,)), ((), ())),
                    precision=HIGHEST,
                    preferred_element_type=jnp.float32,
                )

            minus(upper_ref)
            minus(inverse_ref)


def start_inverse(inverse_ref):
    rows = lax.broadcasted_iota(jnp.int32, inverse_ref.shape, 0)
    cols = lax.broadcasted_iota(jnp.int32, inverse_ref.shape, 1)
    inverse_ref[...] = jnp.where(rows == cols, 1.0, 0.0)


def keep_upper(upper_ref):
    rows = lax.broadcasted_iota(jnp.int32, upper_ref.shape, 0)
    cols = lax.broadcasted_iota(jnp.int32, upper_ref.shape, 1)
    upper_ref[...] = jnp.where(rows <= cols, upper_ref[...], 0.0)


def solve_twice(inverse_ref, projected_ref):
    half = jnp.sum(inverse_ref[...] * projected_ref[...], axis=1, keepdims=True)
    return jnp.sum(inverse_ref[...] * half, axis=0, keepdims=True)


def factor_kernel(gram_ref, projected_ref, upper_ref, inverse_ref, multipliers_ref):
    upper_ref[...] = gram_ref[...]
    start_inverse(inverse_ref)
    factor_steps(upper_ref, inverse_ref, 0, upper_ref.shape[0] // BLOCK)
    keep_upper(upper_ref)
    multipliers_ref[...] = solve_twice(inverse_ref, projected_ref)


def factor(gram, projected):
    order = gram.shape[0]
    return pl.pallas_call(
        factor_kernel,
        out_shape=(
            jax.ShapeDtypeStruct((order, order), jnp.float32),
            jax.ShapeDtypeStruct((order, order), jnp.float32),
            jax.ShapeDtypeStruct((1, order), jnp.float32),
        ),
        in_specs=[pl.BlockSpec(memory_space=pltpu.VMEM)] * 2,
        out_specs=[pl.BlockSpec(memory_space=pltpu.VMEM)] * 3,
        compiler_params=pltpu.CompilerParams(vmem_limit_bytes=LIMIT),
        cost_estimate=pl.CostEstimate(
            flops=6 * order**3, bytes_accessed=12 * order**2, transcendentals=0
        ),
    )(gram, projected)


def features_kernel(field_ref, north_ref, south_ref, out_ref):
    field = field_ref[...]
    rows, width = field.shape
    lanes = lax.broadcasted_iota(jnp.int32, field.shape, 1)
    north = jnp.concatenate([north_ref[...], field[:-1]], axis=0)
    south = jnp.concatenate([field[1:], south_ref[...]], axis=0)
    west = jnp.where(lanes == 0, 0.0, pltpu.roll(field, 1, 1))
    east = jnp.where(lanes == width - 1, 0.0, pltpu.roll(field, width - 1, 1))
    laplace = 4.0 * field - (north + south + west + east)
    slope_x = 0.5 * (east - west)
    slope_y = 0.5 * (south - north)
    parts = []
    for stencil in (laplace, slope_x, slope_y):
        rest = stencil / TILE
        for _ in range(3):
            part = rest.astype(jnp.bfloat16).astype(jnp.float32)
            parts.append(part)
            rest = rest - part
    tiles = width // TILE
    shape = (FEATURES, width)
    owner = lax.broadcasted_iota(jnp.int32, shape, 0) // len(parts)
    tile = lax.broadcasted_iota(jnp.int32, shape, 1) // TILE
    blank = jnp.zeros((FEATURES - tiles * len(parts), width), jnp.float32)
    for row in range(rows):
        block = jnp.concatenate([part[row : row + 1] for part in parts], axis=0)
        whole = jnp.concatenate([block] * tiles + [blank], axis=0)
        out_ref[row] = jnp.where(owner == tile, whole, 0.0).astype(jnp.bfloat16)


def features(field, north, south):
    rows, width = field.shape
    return pl.pallas_call(
        features_kernel,
        out_shape=jax.ShapeDtypeStruct((rows, FEATURES, width), jnp.bfloat16),
        in_specs=[VMEM] * 3,
        out_specs=VMEM,
        compiler_params=pltpu.CompilerParams(vmem_limit_bytes=LIMIT),
        cost_estimate=BRIEF,
    )(field, north, south)


def assembled(base, feature, key, first):
    rows = lax.broadcasted_iota(jnp.int32, (FEATURES, key.shape[1]), 0) // 3 + first
    chooser = jnp.where(rows.astype(jnp.float32) == key, 1.0, 0.0).astype(jnp.bfloat16)
    added = lax.dot_general(
        feature, chooser, (((0,), (0,)), ((), ())), preferred_element_type=jnp.float32
    )
    return (base.astype(jnp.float32) + added).astype(jnp.bfloat16)


def transposed_dot(left, right):
    return lax.dot_general(
        left, right, (((0,), (0,)), ((), ())), preferred_element_type=jnp.float32
    )


def strict_blocks(order):
    count = order // BLOCK
    return [(a, b) for a in range(count) for b in range(a + 1, count)]


def packed_rows(order):
    count = order // BLOCK
    used = (len(strict_blocks(order)) + count // 2) * BLOCK + count // 2 + count
    return -(-used // (8 * GROUP)) * 8 * GROUP


def triangles():
    rows = lax.broadcasted_iota(jnp.int32, (BLOCK, BLOCK), 0)
    cols = lax.broadcasted_iota(jnp.int32, (BLOCK, BLOCK), 1)
    return rows < cols, rows == cols


def at(index):
    return pl.ds(index * BLOCK, BLOCK)


def pack_gram(packed, gram, projected):
    order = gram.shape[0]
    packed[...] = jnp.zeros_like(packed)
    blocks = strict_blocks(order)
    for index, (a, b) in enumerate(blocks):
        packed[at(index), :] = gram[at(a), at(b)]
    above, diagonal = triangles()
    pairs = order // BLOCK // 2
    row = (len(blocks) + pairs) * BLOCK
    for p in range(pairs):
        second = gram[at(2 * p + 1), at(2 * p + 1)]
        packed[at(len(blocks) + p), :] = jnp.where(
            above | diagonal, gram[at(2 * p), at(2 * p)], second
        )
        packed[pl.ds(row + p, 1), :] = jnp.sum(
            jnp.where(diagonal, second, 0.0), axis=0, keepdims=True
        )
    for c in range(order // BLOCK):
        packed[pl.ds(row + pairs + c, 1), :] = projected[:, at(c)]


def unpack_gram(packed, upper_ref, projected_ref):
    order = upper_ref.shape[0]
    upper_ref[...] = jnp.zeros_like(upper_ref)
    blocks = strict_blocks(order)
    for index, (a, b) in enumerate(blocks):
        upper_ref[at(a), at(b)] = packed[at(index), :]
    above, diagonal = triangles()
    pairs = order // BLOCK // 2
    row = (len(blocks) + pairs) * BLOCK
    for p in range(pairs):
        both = packed[at(len(blocks) + p), :]
        turned = both.T
        upper_ref[at(2 * p), at(2 * p)] = jnp.where(above | diagonal, both, turned)
        upper_ref[at(2 * p + 1), at(2 * p + 1)] = jnp.where(
            diagonal, packed[pl.ds(row + p, 1), :], jnp.where(above, turned, both)
        )
    for c in range(order // BLOCK):
        projected_ref[:, at(c)] = packed[pl.ds(row + pairs + c, 1), :]


def own_kernel(
    place_ref, *refs
):
    bases = refs[:OWN_CUTS]
    feature_ref, tile_ref, type_ref, grad_ref, jac_ref = refs[OWN_CUTS : OWN_CUTS + 5]
    outs = refs[OWN_CUTS + 5 : OWN_CUTS + 5 + GROUP]
    gram, projected, packed = refs[OWN_CUTS + 5 + GROUP :]
    step = pl.program_id(0)
    half = pl.num_programs(0) // 2
    order = gram.shape[0]
    base = jnp.concatenate([ref[...] for ref in bases], axis=0)
    key = (tile_ref[...] * 3 + type_ref[...]).astype(jnp.float32)
    jac = assembled(base, feature_ref[0], key, place_ref[2])

    @pl.when(step // half == place_ref[0])
    def _():
        jac_ref[...] = jac

    @pl.when(step == 0)
    def _():
        gram[...] = jnp.zeros_like(gram)
        projected[...] = jnp.zeros_like(projected)

    middle = order // 2
    gram[:middle, :] += transposed_dot(jac[:, :middle], jac)
    gram[middle:, middle:] += transposed_dot(jac[:, middle:], jac[:, middle:])
    projected[...] += jnp.dot(grad_ref[0], jac, preferred_element_type=jnp.float32)

    @pl.when(step == pl.num_programs(0) - 1)
    def _():
        pack_gram(packed, gram, projected)
        size = outs[0].shape[0]
        for mask in range(GROUP):
            start = pl.multiple_of((place_ref[1] ^ mask) * size, 8)
            outs[mask][...] = packed[pl.ds(start, size), :]


def cut_index(cut, i, place):
    return (OWN_CUTS * i + cut, 0)


def own_part(place, base, feature, tile_row, type_row, gradient):
    cells, order = base.shape
    rows, width = gradient.shape
    half = rows // 2
    size = packed_rows(order) // GROUP
    return pl.pallas_call(
        own_kernel,
        grid_spec=pltpu.PrefetchScalarGridSpec(
            num_scalar_prefetch=1,
            grid=(rows,),
            in_specs=[
                pl.BlockSpec((width // OWN_CUTS, order), functools.partial(cut_index, k))
                for k in range(OWN_CUTS)
            ]
            + [
                pl.BlockSpec((1, FEATURES, width), lambda i, s: (i, 0, 0)),
                pl.BlockSpec((1, order), lambda i, s: (0, 0)),
                pl.BlockSpec((1, order), lambda i, s: (0, 0)),
                pl.BlockSpec((1, 1, width), lambda i, s: (i, 0, 0)),
            ],
            out_specs=[
                pl.BlockSpec(
                    (width, order), lambda i, s: (jnp.clip(i - s[0] * half, 0, half - 1), 0)
                )
            ]
            + [pl.BlockSpec((size, BLOCK), lambda i, s: (0, 0))] * GROUP,
            scratch_shapes=[
                pltpu.VMEM((order, order), jnp.float32),
                pltpu.VMEM((1, order), jnp.float32),
                pltpu.VMEM((GROUP * size, BLOCK), jnp.float32),
            ],
        ),
        out_shape=[jax.ShapeDtypeStruct((cells // 2, order), jnp.bfloat16)]
        + [jax.ShapeDtypeStruct((size, BLOCK), jnp.float32)] * GROUP,
        compiler_params=pltpu.CompilerParams(vmem_limit_bytes=WIDE_LIMIT),
        cost_estimate=BRIEF,
    )(place, *[base] * OWN_CUTS, feature, tile_row, type_row, gradient.reshape(rows, 1, width))


def send_kernel(pieces, place_ref, base_ref, tile_ref, type_ref, *refs):
    outs, (held, tiles, types, sems) = refs[-4 - len(pieces) : -4], refs[-4:]
    half = base_ref.shape[0] // 2
    low = min(piece[0] for piece in pieces)
    first = (1 - place_ref[0]) * half + low
    chunks = held.shape[0] // COPY_ROWS
    copies = [
        pltpu.make_async_copy(
            base_ref.at[pl.ds(pl.multiple_of(first + k * COPY_ROWS, COPY_ROWS), COPY_ROWS), :],
            held.at[pl.ds(k * COPY_ROWS, COPY_ROWS), :],
            sems.at[k],
        )
        for k in range(chunks)
    ]
    copies.append(pltpu.make_async_copy(tile_ref, tiles, sems.at[chunks]))
    copies.append(pltpu.make_async_copy(type_ref, types, sems.at[chunks + 1]))
    for copy in copies:
        copy.start()
    for k in range(chunks):
        copies[k].wait()
        for (top, end, left, right, _), out in zip(pieces, outs):
            row = low + k * COPY_ROWS
            if top <= row < end:
                out[pl.ds(row - top, COPY_ROWS), :] = held[
                    pl.ds(k * COPY_ROWS, COPY_ROWS), left:right
                ]
    copies[chunks].wait()
    copies[chunks + 1].wait()
    for (top, end, left, right, keyed), out in zip(pieces, outs):
        if keyed:
            key = (tiles[:, left:right] * 3 + types[:, left:right]).astype(jnp.float32)
            key = jnp.broadcast_to(key, (KEY_ROWS, right - left))
            out[pl.ds(end - top, KEY_ROWS), :] = key.astype(jnp.bfloat16)


def send_parts(place, base, tile_row, type_row, pieces, limit):
    order = base.shape[1]
    span = max(piece[1] for piece in pieces) - min(piece[0] for piece in pieces)
    return pl.pallas_call(
        functools.partial(send_kernel, tuple(pieces)),
        in_specs=[SMEM, ANY, ANY, ANY],
        out_specs=[VMEM] * len(pieces),
        out_shape=[
            jax.ShapeDtypeStruct((end - top + KEY_ROWS * keyed, right - left), base.dtype)
            for top, end, left, right, keyed in pieces
        ],
        scratch_shapes=[
            pltpu.VMEM((span, order), base.dtype),
            pltpu.VMEM((1, order), jnp.int32),
            pltpu.VMEM((1, order), jnp.int32),
            pltpu.SemaphoreType.DMA((span // COPY_ROWS + 2,)),
        ],
        compiler_params=pltpu.CompilerParams(vmem_limit_bytes=limit),
        cost_estimate=BRIEF,
    )(place, base, tile_row, type_row)


def cross_kernel(pieces, place_ref, jac_ref, feature_ref, *refs):
    received = refs[:pieces]
    outs = refs[-2 - GROUP : -2]
    total, out_ref = refs[-2:]
    cells, width = jac_ref.shape[0], feature_ref.shape[2]
    cuts = width // STEP_ROWS
    first = place_ref[0] * (cells // width)
    keyed = received[0].shape[0] - KEY_ROWS
    key = received[0][pl.ds(keyed, KEY_ROWS), :][0:1, :].astype(jnp.float32)
    total[...] = jnp.zeros_like(total)
    done = 0
    for piece in received:
        count = piece.shape[0] // STEP_ROWS

        @pl.loop(0, count)
        def _(step, piece=piece, done=done):
            rows = pl.ds(pl.multiple_of(step * STEP_ROWS, STEP_ROWS), STEP_ROWS)
            step = step + done
            mine = pl.ds(pl.multiple_of(step * STEP_ROWS, STEP_ROWS), STEP_ROWS)
            lanes = pl.ds(pl.multiple_of(step % cuts * STEP_ROWS, STEP_ROWS), STEP_ROWS)
            feature = feature_ref[first + step // cuts, :, lanes]
            other = assembled(piece[rows, :], feature, key, place_ref[2])
            total[...] += transposed_dot(other, jac_ref[mine, :])

        done += count

    count = total.shape[1] // BLOCK
    part = BLOCK // GROUP

    blocks = total.shape[0] // BLOCK

    @pl.when(place_ref[0] == 0)
    def _():
        for k in range(blocks):
            for q in range(GROUP):
                for c in range(count):
                    out_ref[q, pl.ds(BLOCK * k + part * c, part), :] = total[
                        pl.ds(BLOCK * k + part * q, part), pl.ds(BLOCK * c, BLOCK)
                    ]

    @pl.when(place_ref[0] != 0)
    def _():
        for k in range(blocks):
            for c in range(count):
                block = total[pl.ds(BLOCK * k, BLOCK), pl.ds(BLOCK * c, BLOCK)].T
                for q in range(GROUP):
                    out_ref[q, pl.ds(BLOCK * k + part * c, part), :] = block[
                        part * q : part * q + part
                    ]

    for mask in range(GROUP):
        outs[mask][...] = out_ref[place_ref[1] ^ mask]


def cross_part(place, received, jac, feature, *after):
    width_recv, order = received[0].shape[1], jac.shape[1]
    return pl.pallas_call(
        functools.partial(cross_kernel, len(received)),
        in_specs=[SMEM] + [VMEM] * (2 + len(received)) + [ANY] * len(after),
        out_specs=[VMEM] * GROUP,
        out_shape=[jax.ShapeDtypeStruct((width_recv, BLOCK), jnp.float32)] * GROUP,
        scratch_shapes=[
            pltpu.VMEM((width_recv, order), jnp.float32),
            pltpu.VMEM((GROUP, width_recv, BLOCK), jnp.float32),
        ],
        compiler_params=pltpu.CompilerParams(vmem_limit_bytes=LIMIT),
        cost_estimate=BRIEF,
    )(place, jac, feature, *received, *after)


def swap(value, axis, mask):
    count = lax.axis_size(axis)
    return lax.ppermute(value, axis, [(i, i ^ mask) for i in range(count)])


def add_kernel(count, *refs):
    refs[-1][...] = sum(ref[...] for ref in refs[1:count]) + refs[0][...]


def add(values, *after):
    return pl.pallas_call(
        functools.partial(add_kernel, len(values)),
        out_shape=jax.ShapeDtypeStruct(values[0].shape, values[0].dtype),
        in_specs=[VMEM] * len(values) + [ANY] * len(after),
        out_specs=VMEM,
        compiler_params=pltpu.CompilerParams(vmem_limit_bytes=LIMIT),
        cost_estimate=BRIEF,
    )(*values, *after)


def add_pass_kernel(*refs):
    *values, passed_ref, out_ref, copy_ref = refs
    out_ref[...] = sum(ref[...] for ref in values[1:]) + values[0][...]
    copy_ref[...] = passed_ref[...]


def add_pass(values, passed):
    return pl.pallas_call(
        add_pass_kernel,
        out_shape=[jax.ShapeDtypeStruct(v.shape, v.dtype) for v in (values[0], passed)],
        in_specs=[VMEM] * (len(values) + 1),
        out_specs=[VMEM] * 2,
        compiler_params=pltpu.CompilerParams(vmem_limit_bytes=LIMIT),
        cost_estimate=BRIEF,
    )(*values, passed)


def stacked_kernel(count, *refs):
    first, second, out_ref = refs[:count], refs[count:-1], refs[-1]
    rows = first[0].shape[0]
    out_ref[:rows, :] = sum(ref[...] for ref in first[1:]) + first[0][...]
    out_ref[rows:, :] = sum(ref[...] for ref in second[1:]) + second[0][...]


def stacked(first, second):
    rows = first[0].shape[0] + second[0].shape[0]
    return pl.pallas_call(
        functools.partial(stacked_kernel, len(first)),
        out_shape=jax.ShapeDtypeStruct((rows, BLOCK), jnp.float32),
        in_specs=[VMEM] * (len(first) + len(second)),
        out_specs=VMEM,
        compiler_params=pltpu.CompilerParams(vmem_limit_bytes=LIMIT),
        cost_estimate=BRIEF,
    )(*first, *second)


def joined_kernel(own_ref, other_ref, out_ref):
    part = BLOCK // GROUP
    blocks = own_ref.shape[0] // BLOCK
    for a in range(blocks):
        for b in range(blocks):
            out_ref[pl.ds(part * b, part), at(a)] = (
                own_ref[pl.ds(BLOCK * a + part * b, part), :]
                + other_ref[pl.ds(BLOCK * b + part * a, part), :]
            )


def joined(own, other):
    order = own.shape[0]
    return pl.pallas_call(
        joined_kernel,
        out_shape=jax.ShapeDtypeStruct((order // GROUP, order), jnp.float32),
        in_specs=[VMEM] * 2,
        out_specs=VMEM,
        compiler_params=pltpu.CompilerParams(vmem_limit_bytes=LIMIT),
        cost_estimate=BRIEF,
    )(own, other)


def group_swaps(parts):
    return [parts[0]] + [swap(parts[mask], "rows", mask) for mask in range(1, GROUP)]


def group_sum(parts):
    got = group_swaps(parts)
    return got[0] + got[1] + got[2] + got[3]


def groups_sum(held):
    masks = range(GROUP, lax.axis_size("rows"), GROUP)
    return held + sum(swap(held, "rows", mask) for mask in masks)


def doubled(held, masks):
    for mask in masks:
        held = held + swap(held, "rows", mask)
    return held


def rows_gather(own):
    return [own] + [swap(own, "rows", mask) for mask in range(1, GROUP)]


def near_gather(own):
    near, far = swap(own, "rows", 1), swap(own, "rows", 2)
    return [own, near, far, swap(far, "rows", 1)]


def first_factor_kernel(last, place_ref, *refs):
    pieces = refs[:GROUP]
    upper_ref, inverse_ref, projected_ref, whole = refs[GROUP + 1 :]
    size = pieces[0].shape[0]
    for mask in range(GROUP):
        start = pl.multiple_of((place_ref[1] ^ mask) * size, 8)
        whole[pl.ds(start, size), :] = pieces[mask][...]
    unpack_gram(whole, upper_ref, projected_ref)
    start_inverse(inverse_ref)
    factor_steps(upper_ref, inverse_ref, 0, last)


def square(order):
    return jax.ShapeDtypeStruct((order, order), jnp.float32)


def row(order):
    return jax.ShapeDtypeStruct((1, order), jnp.float32)


def first_factor(place, pieces, order, last, after):
    return pl.pallas_call(
        functools.partial(first_factor_kernel, last),
        out_shape=(square(order), square(order), row(order)),
        in_specs=[SMEM] + [VMEM] * GROUP + [ANY],
        out_specs=[VMEM] * 3,
        scratch_shapes=[pltpu.VMEM((packed_rows(order), BLOCK), jnp.float32)],
        compiler_params=pltpu.CompilerParams(vmem_limit_bytes=LIMIT),
        cost_estimate=BRIEF,
    )(place, *pieces, after)


def more_factor_kernel(first, last, upper_in, inverse_in, _, upper_ref, inverse_ref):
    del upper_in, inverse_in
    factor_steps(upper_ref, inverse_ref, first, last)


def more_factor(upper, inverse, first, last, after, cost):
    order = upper.shape[0]
    return pl.pallas_call(
        functools.partial(more_factor_kernel, first, last),
        out_shape=[square(order)] * 2,
        in_specs=[VMEM] * 2 + [ANY],
        out_specs=[VMEM] * 2,
        input_output_aliases={0: 0, 1: 1},
        compiler_params=pltpu.CompilerParams(vmem_limit_bytes=LIMIT),
        cost_estimate=cost,
    )(upper, inverse, after)


def lower_blocks(order):
    return [(a, b) for a in range(order // BLOCK) for b in range(a + 1)]


def lower_half(order):
    rows = len(lower_blocks(order)) * BLOCK + order // BLOCK
    return -(-rows // 16) * 8


def last_factor_kernel(
    first, place_ref, upper_in, inverse_in, projected, _, upper_ref, inverse, out_ref, half_ref, packed
):
    del upper_in, inverse_in
    order = upper_ref.shape[0]
    factor_steps(upper_ref, inverse, first, order // BLOCK)
    keep_upper(upper_ref)
    solved = solve_twice(inverse, projected)
    out_ref[...] = solved
    blocks = lower_blocks(order)
    for index, (a, b) in enumerate(blocks):
        packed[pl.ds(index * BLOCK, BLOCK), :] = inverse[
            pl.ds(a * BLOCK, BLOCK), pl.ds(b * BLOCK, BLOCK)
        ]
    start = len(blocks) * BLOCK
    packed[start:, :] = jnp.zeros((packed.shape[0] - start, BLOCK), jnp.float32)
    for c in range(order // BLOCK):
        packed[pl.ds(start + c, 1), :] = solved[:, c * BLOCK : (c + 1) * BLOCK]
    size = half_ref.shape[0]
    half_ref[...] = packed[pl.ds(pl.multiple_of(place_ref[1] % 2 * size, 8), size), :]


def last_factor(place, upper, inverse, projected, first, after, cost):
    order = upper.shape[0]
    size = lower_half(order)
    return pl.pallas_call(
        functools.partial(last_factor_kernel, first),
        out_shape=(
            square(order),
            square(order),
            row(order),
            jax.ShapeDtypeStruct((size, BLOCK), jnp.float32),
        ),
        in_specs=[SMEM] + [VMEM] * 3 + [ANY],
        out_specs=[VMEM] * 4,
        input_output_aliases={1: 0, 2: 1},
        scratch_shapes=[pltpu.VMEM((2 * size, BLOCK), jnp.float32)],
        compiler_params=pltpu.CompilerParams(vmem_limit_bytes=LIMIT),
        cost_estimate=cost,
    )(place, upper, inverse, projected, after)


def three_products(left, right):
    def parts(value):
        high = value.astype(jnp.bfloat16)
        return high, (value - high.astype(jnp.float32)).astype(jnp.bfloat16)

    def dot(a, b):
        return lax.dot_general(
            a, b, (((1,), (1,)), ((), ())), preferred_element_type=jnp.float32
        )

    (high, low), (other_high, other_low) = parts(left), parts(right)
    return dot(high, other_high) + (dot(high, other_low) + dot(low, other_high))


def finish_kernel(place_ref, upper_ref, solved_ref, half_ref, other_ref, *refs):
    pieces = refs[:GROUP]
    out_ref, multipliers_ref, cross, packed, inverse = refs[GROUP:]
    order = upper_ref.shape[0]
    part = BLOCK // GROUP

    @pl.when(place_ref[0] == 0)
    def _():
        out_ref[...] = upper_ref[...]
        multipliers_ref[...] = solved_ref[...]

    @pl.when(place_ref[0] != 0)
    def _():
        size = half_ref.shape[0]
        core = place_ref[1] % 2
        packed[pl.ds(pl.multiple_of(core * size, 8), size), :] = half_ref[...]
        packed[pl.ds(pl.multiple_of((1 - core) * size, 8), size), :] = other_ref[...]
        blocks = lower_blocks(order)
        for index, (a, b) in enumerate(blocks):
            inverse[pl.ds(a * BLOCK, BLOCK), pl.ds(b * BLOCK, BLOCK)] = packed[
                pl.ds(index * BLOCK, BLOCK), :
            ]
        for c in range(order // BLOCK):
            multipliers_ref[:, pl.ds(c * BLOCK, BLOCK)] = packed[
                pl.ds(len(blocks) * BLOCK + c, 1), :
            ]
        for mask in range(GROUP):
            quarter = place_ref[1] ^ mask
            for b in range(order // BLOCK):
                start = pl.multiple_of(BLOCK * b + part * quarter, part)
                cross[pl.ds(start, part), :] = pieces[mask][pl.ds(part * b, part), :]
        for a in range(order // BLOCK):
            rows, depth = pl.ds(a * BLOCK, BLOCK), (a + 1) * BLOCK
            out_ref[rows, :] = three_products(
                inverse[rows, pl.ds(0, depth)], cross[:, pl.ds(0, depth)]
            )


def finish(place, upper, solved, half, other, pieces):
    order = upper.shape[0]
    return pl.pallas_call(
        finish_kernel,
        out_shape=(square(order), row(order)),
        in_specs=[SMEM] + [VMEM] * (4 + GROUP),
        out_specs=[VMEM] * 2,
        scratch_shapes=[
            pltpu.VMEM((order, order), jnp.float32),
            pltpu.VMEM((2 * lower_half(order), BLOCK), jnp.float32),
            pltpu.VMEM((order, order), jnp.float32),
        ],
        compiler_params=pltpu.CompilerParams(vmem_limit_bytes=LIMIT),
        cost_estimate=BRIEF,
    )(place, upper, solved, half, other, *pieces)


def shards(sens_base, design_field, gradient, tile_index, type_codes):
    cells, order = sens_base.shape
    rows_here, width = design_field.shape
    side = lax.axis_index("cols")
    quarter = lax.axis_index("rows") % GROUP
    tiles = width // TILE
    first_tile = lax.axis_index("rows") * rows_here // TILE * tiles
    place = jnp.stack([side, quarter, 3 * first_tile]).astype(jnp.int32)
    tile_row, type_row = tile_index[None, :], type_codes[None, :]

    half, split = cells // 2, order - BLOCK
    middle = half // 2
    rows = [
        [(0, middle, 0, split, True)],
        [(middle, half, 0, split, False)],
        [(0, half, split, order, True)],
    ]
    wide = WIDE_LIMIT + 6 * 2**20
    sent = [
        send_parts(place, sens_base, tile_row, type_row, pieces, limit)[0]
        for pieces, limit in zip(rows, (wide, wide, TAIL_LIMIT))
    ]
    lead, rest, tail = [swap(part, "cols", 1) for part in sent]
    received = [[lead, rest], [tail]]

    count = lax.axis_size("rows")
    north = lax.ppermute(design_field[-1:], "rows", [(i, i + 1) for i in range(count - 1)])
    south = lax.ppermute(design_field[:1], "rows", [(i + 1, i) for i in range(count - 1)])
    feature = features(design_field, north, south)
    jac, *packed = own_part(place, sens_base, feature, tile_row, type_row, gradient)
    pieces = rows_gather(groups_sum(group_sum(packed)))

    def stage(index, *after):
        return cross_part(place, received[index], jac, feature, *after)

    upper, inverse, projected = first_factor(place, pieces, order, 1, pieces[0])
    first = stage(0, upper)
    shares = group_swaps(first)
    upper, inverse = more_factor(upper, inverse, 1, 2, first[0], LONG)
    held = add(shares, inverse)
    shares = [held, swap(held, "rows", GROUP)]
    upper, inverse = more_factor(upper, inverse, 2, 3, held, LONG)
    middle = add(shares, inverse)
    far = range(2 * GROUP, count, 2 * GROUP)
    far_shares = [middle] + [swap(middle, "rows", mask) for mask in far]
    last = stage(1, middle)
    shares = group_swaps(last)
    upper, _, solved, half = last_factor(place, upper, inverse, projected, 3, last[0], LONG)
    held_last, half = add_pass(shares, half)
    shares = [held_last] + [swap(held_last, "rows", mask) for mask in range(GROUP, count, GROUP)]
    totals = stacked(far_shares, shares)
    others = lax.ppermute(totals, "cols", [(0, 1)])
    half = lax.ppermute(half, "cols", [(0, 1)])

    cross = joined(totals, others)
    r_panels, multipliers = finish(
        place, upper, solved, half, swap(half, "rows", 1), near_gather(cross)
    )
    return (r_panels, multipliers[0])


def shards_general(sens_base, design_field, gradient, tile_index, type_codes):
    rows_here = design_field.shape[0]
    grid_width = design_field.shape[1]
    cols_here = sens_base.shape[1]
    factored = 2 * PW
    padded = padded_2(design_field, (("rows", 0),), 1)
    padded = jnp.pad(padded, ((0, 0), (1, 1)))
    north_cells = padded[:-2, 1:-1]
    south_cells = padded[2:, 1:-1]
    west_cells = padded[1:-1, :-2]
    east_cells = padded[1:-1, 2:]
    laplace = 4.0 * design_field - (north_cells + south_cells + west_cells + east_cells)
    slope_x = 0.5 * (east_cells - west_cells)
    slope_y = 0.5 * (south_cells - north_cells)
    stencils = jnp.stack([laplace, slope_x, slope_y]).reshape(3, -1)
    row_glob = lax.axis_index("rows") * rows_here + jnp.arange(rows_here, dtype=jnp.int32)
    col_ids = jnp.arange(grid_width, dtype=jnp.int32) // TILE
    cell_tile = ((row_glob // TILE)[:, None] * (grid_width // TILE) + col_ids[None, :]).reshape(-1)
    local_jac = assemble(sens_base, tile_index, type_codes, stencils, cell_tile)
    grad_flat = gradient.reshape(-1)
    row_major = lax.all_to_all(local_jac, "cols", split_axis=0, concat_axis=1, tiled=True)
    row_piece = row_major.shape[0]
    grad_part = lax.dynamic_slice_in_dim(
        grad_flat, lax.axis_index("cols") * row_piece, row_piece, 0
    )
    leading = row_major[:, :factored]
    gram_block = lax.dot_general(
        leading, row_major, (((0,), (0,)), ((), ())), preferred_element_type=jnp.float32
    )
    projected = jnp.dot(grad_part, leading, preferred_element_type=jnp.float32)
    gram_block, projected = lax.psum((gram_block, projected), ("rows", "cols"))
    gram_head = gram_block[:, :factored]
    gram_own = lax.dynamic_slice_in_dim(
        gram_block, lax.axis_index("cols") * cols_here, cols_here, 1
    )
    _, inverse, multipliers = factor(gram_head, projected[None, :])
    r_panels = matmul(inverse, gram_own)
    return (r_panels, multipliers[0])


def solution(mesh):
    placed = (P("rows", "cols"), P("rows", None), P("rows", None), P("cols"), P("cols"))
    pairs = mesh.shape["cols"] == 2 and mesh.shape["rows"] in (8, 16, 32, 64)
    return jax.shard_map(
        shards if pairs else shards_general,
        mesh=mesh,
        in_specs=placed,
        out_specs=(P(None, "cols"), P()),
        check_vma=False,
    )
```

```python
import functools

import jax
import jax.numpy as jnp
from jax import lax
from jax.experimental import pallas as pl
from jax.experimental.pallas import tpu as pltpu
from jax.sharding import PartitionSpec as P

TILE = 128
PW = 256
BLOCK = 128
FEATURES = 80
KEY_ROWS = 16
STEP_ROWS = 1024
COPY_ROWS = 256
OWN_CUTS = 4
GROUP = 4
HIGHEST = lax.Precision.HIGHEST
VMEM = pl.BlockSpec(memory_space=pltpu.VMEM)
SMEM = pl.BlockSpec(memory_space=pltpu.SMEM)
LIMIT = 12 * 2**20
WIDE_LIMIT = 48 * 2**20
TAIL_LIMIT = 36 * 2**20
ANY = pl.BlockSpec(memory_space=pl.ANY)
LONG = pl.CostEstimate(flops=8 * 10**9, bytes_accessed=1000, transcendentals=0)
BRIEF = pl.CostEstimate(flops=1000, bytes_accessed=1000, transcendentals=0)


def padded_2(cells, sides, width):
    for axis, dim in sides:
        count = lax.axis_size(axis)
        ends = count - 1
        head = lax.slice_in_dim(cells, 0, width, axis=dim)
        tail = lax.slice_in_dim(cells, cells.shape[dim] - width, cells.shape[dim], axis=dim)
        cells = jnp.concatenate(
            [
                lax.ppermute(tail, axis, [(i, (i + 1) % count) for i in range(ends)]),
                cells,
                lax.ppermute(head, axis, [((i + 1) % count, i) for i in range(ends)]),
            ],
            axis=dim,
        )
    return cells


def assemble(base_cols, tile_cols, type_cols, stencils, cell_tile):
    kinds_all = jnp.arange(3, dtype=jnp.int32)
    chooser = (type_cols[None, :] == kinds_all[:, None]).astype(jnp.float32)
    picked = lax.dot_general(
        stencils,
        chooser,
        (((0,), (0,)), ((), ())),
        precision=lax.Precision.HIGHEST,
        preferred_element_type=jnp.float32,
    )
    inside = cell_tile[:, None] == tile_cols[None, :]
    total = base_cols.astype(jnp.float32) + jnp.where(inside, picked / TILE, 0.0)
    return total.astype(jnp.bfloat16)


def matmul(left, right):
    return jnp.dot(left, right, precision=HIGHEST, preferred_element_type=jnp.float32)


def tree_sum(terms):
    while len(terms) > 1:
        terms = [a + b for a, b in zip(terms[::2], terms[1::2])] + terms[len(terms) // 2 * 2 :]
    return terms[0]


def lane(part, index):
    return jnp.broadcast_to(part[:, index : index + 1], part.shape)


def sublane(part, index):
    return jnp.broadcast_to(part[index : index + 1, :], part.shape)


def diagonal_inverse(block):
    groups = BLOCK // 8
    shape = (8, BLOCK)
    lanes = lax.broadcasted_iota(jnp.int32, shape, 1)
    subs = lax.broadcasted_iota(jnp.int32, shape, 0)
    parts = [block[8 * g : 8 * g + 8, :] for g in range(groups)]
    whole = []
    for p in range(groups):
        part, first = parts[p], 8 * p
        cols = [lane(part, first + k) for k in range(8)]
        inv = [None] * 8
        low = [jnp.zeros(shape, jnp.float32) for _ in range(8)]
        scale = jnp.ones(shape, jnp.float32)
        for j in range(8):
            here = subs == j
            root = lax.rsqrt(sublane(cols[j], j))
            ratio = root * root
            scale = jnp.where(here, root, scale)
            for k in range(j):
                low[k] = jnp.where(here, inv[k], low[k])
            low[j] = jnp.where(here, 1.0, low[j])
            column = cols[j]
            for part_list, chosen in ((cols, range(j + 1, 8)), (inv, range(j))):
                for k in chosen:
                    row = sublane(part_list[k], j)
                    share = jnp.where(here, -row, column * row)
                    part_list[k] = jnp.where(here, 0.0, part_list[k]) - share * ratio
            inv[j] = jnp.where(here, 1.0, -column) * ratio
        inside = (lanes >= first) & (lanes < first + 8)
        unit = jnp.where(lanes - first == subs, 1.0, 0.0)
        rows = jnp.where(inside, unit, part)
        spread = [sublane(rows, k) for k in range(8)]
        solved = tree_sum([low[k] * spread[k] for k in range(8)]) * scale
        whole.append(jnp.where(lanes < first + 8, solved, 0.0))
        if p + 1 < groups:
            step = tree_sum([inv[k] * spread[k] for k in range(8)])
            step = [sublane(step, k) for k in range(8)]
            for g in range(p + 1, groups):
                taken = tree_sum([lane(parts[g], first + k) * step[k] for k in range(8)])
                parts[g] = jnp.where(inside, 0.0, parts[g]) - taken
    return jnp.concatenate(whole, axis=0)


def factor_steps(upper_ref, inverse_ref, first, last):
    blocks = upper_ref.shape[0] // BLOCK

    @pl.loop(first, last)
    def _(step):
        mine = pl.ds(pl.multiple_of(step * BLOCK, BLOCK), BLOCK)
        small = diagonal_inverse(upper_ref[mine, mine])
        upper_ref[mine, :] = matmul(small, upper_ref[mine, :])
        inverse_ref[mine, :] = matmul(small, inverse_ref[mine, :])

        @pl.loop(step + 1, blocks)
        def _(later):
            theirs = pl.ds(pl.multiple_of(later * BLOCK, BLOCK), BLOCK)
            factor = upper_ref[mine, theirs]

            def minus(target):
                target[theirs, :] -= lax.dot_general(
                    factor,
                    target[mine, :],
                    (((0,), (0,)), ((), ())),
                    precision=HIGHEST,
                    preferred_element_type=jnp.float32,
                )

            minus(upper_ref)
            minus(inverse_ref)


def start_inverse(inverse_ref):
    rows = lax.broadcasted_iota(jnp.int32, inverse_ref.shape, 0)
    cols = lax.broadcasted_iota(jnp.int32, inverse_ref.shape, 1)
    inverse_ref[...] = jnp.where(rows == cols, 1.0, 0.0)


def keep_upper(upper_ref):
    rows = lax.broadcasted_iota(jnp.int32, upper_ref.shape, 0)
    cols = lax.broadcasted_iota(jnp.int32, upper_ref.shape, 1)
    upper_ref[...] = jnp.where(rows <= cols, upper_ref[...], 0.0)


def solve_twice(inverse_ref, projected_ref):
    half = jnp.sum(inverse_ref[...] * projected_ref[...], axis=1, keepdims=True)
    return jnp.sum(inverse_ref[...] * half, axis=0, keepdims=True)


def factor_kernel(gram_ref, projected_ref, upper_ref, inverse_ref, multipliers_ref):
    upper_ref[...] = gram_ref[...]
    start_inverse(inverse_ref)
    factor_steps(upper_ref, inverse_ref, 0, upper_ref.shape[0] // BLOCK)
    keep_upper(upper_ref)
    multipliers_ref[...] = solve_twice(inverse_ref, projected_ref)


def factor(gram, projected):
    order = gram.shape[0]
    return pl.pallas_call(
        factor_kernel,
        out_shape=(
            jax.ShapeDtypeStruct((order, order), jnp.float32),
            jax.ShapeDtypeStruct((order, order), jnp.float32),
            jax.ShapeDtypeStruct((1, order), jnp.float32),
        ),
        in_specs=[pl.BlockSpec(memory_space=pltpu.VMEM)] * 2,
        out_specs=[pl.BlockSpec(memory_space=pltpu.VMEM)] * 3,
        compiler_params=pltpu.CompilerParams(vmem_limit_bytes=LIMIT),
        cost_estimate=pl.CostEstimate(
            flops=6 * order**3, bytes_accessed=12 * order**2, transcendentals=0
        ),
    )(gram, projected)


def features_kernel(field_ref, north_ref, south_ref, out_ref):
    field = field_ref[...]
    rows, width = field.shape
    lanes = lax.broadcasted_iota(jnp.int32, field.shape, 1)
    north = jnp.concatenate([north_ref[...], field[:-1]], axis=0)
    south = jnp.concatenate([field[1:], south_ref[...]], axis=0)
    west = jnp.where(lanes == 0, 0.0, pltpu.roll(field, 1, 1))
    east = jnp.where(lanes == width - 1, 0.0, pltpu.roll(field, width - 1, 1))
    laplace = 4.0 * field - (north + south + west + east)
    slope_x = 0.5 * (east - west)
    slope_y = 0.5 * (south - north)
    parts = []
    for stencil in (laplace, slope_x, slope_y):
        rest = stencil / TILE
        for _ in range(3):
            part = rest.astype(jnp.bfloat16).astype(jnp.float32)
            parts.append(part)
            rest = rest - part
    tiles = width // TILE
    shape = (FEATURES, width)
    owner = lax.broadcasted_iota(jnp.int32, shape, 0) // len(parts)
    tile = lax.broadcasted_iota(jnp.int32, shape, 1) // TILE
    blank = jnp.zeros((FEATURES - tiles * len(parts), width), jnp.float32)
    for row in range(rows):
        block = jnp.concatenate([part[row : row + 1] for part in parts], axis=0)
        whole = jnp.concatenate([block] * tiles + [blank], axis=0)
        out_ref[row] = jnp.where(owner == tile, whole, 0.0).astype(jnp.bfloat16)


def features(field, north, south):
    rows, width = field.shape
    return pl.pallas_call(
        features_kernel,
        out_shape=jax.ShapeDtypeStruct((rows, FEATURES, width), jnp.bfloat16),
        in_specs=[VMEM] * 3,
        out_specs=VMEM,
        compiler_params=pltpu.CompilerParams(vmem_limit_bytes=LIMIT),
        cost_estimate=BRIEF,
    )(field, north, south)


def assembled(base, feature, key, first):
    rows = lax.broadcasted_iota(jnp.int32, (FEATURES, key.shape[1]), 0) // 3 + first
    chooser = jnp.where(rows.astype(jnp.float32) == key, 1.0, 0.0).astype(jnp.bfloat16)
    added = lax.dot_general(
        feature, chooser, (((0,), (0,)), ((), ())), preferred_element_type=jnp.float32
    )
    return (base.astype(jnp.float32) + added).astype(jnp.bfloat16)


def transposed_dot(left, right):
    return lax.dot_general(
        left, right, (((0,), (0,)), ((), ())), preferred_element_type=jnp.float32
    )


def strict_blocks(order):
    count = order // BLOCK
    return [(a, b) for a in range(count) for b in range(a + 1, count)]


def packed_rows(order):
    count = order // BLOCK
    used = (len(strict_blocks(order)) + count // 2) * BLOCK + count // 2 + count
    return -(-used // (8 * GROUP)) * 8 * GROUP


def triangles():
    rows = lax.broadcasted_iota(jnp.int32, (BLOCK, BLOCK), 0)
    cols = lax.broadcasted_iota(jnp.int32, (BLOCK, BLOCK), 1)
    return rows < cols, rows == cols


def at(index):
    return pl.ds(index * BLOCK, BLOCK)


def pack_gram(packed, gram, projected):
    order = gram.shape[0]
    packed[...] = jnp.zeros_like(packed)
    blocks = strict_blocks(order)
    for index, (a, b) in enumerate(blocks):
        packed[at(index), :] = gram[at(a), at(b)]
    above, diagonal = triangles()
    pairs = order // BLOCK // 2
    row = (len(blocks) + pairs) * BLOCK
    for p in range(pairs):
        second = gram[at(2 * p + 1), at(2 * p + 1)]
        packed[at(len(blocks) + p), :] = jnp.where(
            above | diagonal, gram[at(2 * p), at(2 * p)], second
        )
        packed[pl.ds(row + p, 1), :] = jnp.sum(
            jnp.where(diagonal, second, 0.0), axis=0, keepdims=True
        )
    for c in range(order // BLOCK):
        packed[pl.ds(row + pairs + c, 1), :] = projected[:, at(c)]


def unpack_gram(packed, upper_ref, projected_ref):
    order = upper_ref.shape[0]
    upper_ref[...] = jnp.zeros_like(upper_ref)
    blocks = strict_blocks(order)
    for index, (a, b) in enumerate(blocks):
        upper_ref[at(a), at(b)] = packed[at(index), :]
    above, diagonal = triangles()
    pairs = order // BLOCK // 2
    row = (len(blocks) + pairs) * BLOCK
    for p in range(pairs):
        both = packed[at(len(blocks) + p), :]
        turned = both.T
        upper_ref[at(2 * p), at(2 * p)] = jnp.where(above | diagonal, both, turned)
        upper_ref[at(2 * p + 1), at(2 * p + 1)] = jnp.where(
            diagonal, packed[pl.ds(row + p, 1), :], jnp.where(above, turned, both)
        )
    for c in range(order // BLOCK):
        projected_ref[:, at(c)] = packed[pl.ds(row + pairs + c, 1), :]


def own_kernel(
    place_ref, *refs
):
    bases = refs[:OWN_CUTS]
    feature_ref, tile_ref, type_ref, grad_ref, jac_ref = refs[OWN_CUTS : OWN_CUTS + 5]
    outs = refs[OWN_CUTS + 5 : OWN_CUTS + 5 + GROUP]
    gram, projected, packed = refs[OWN_CUTS + 5 + GROUP :]
    step = pl.program_id(0)
    half = pl.num_programs(0) // 2
    order = gram.shape[0]
    base = jnp.concatenate([ref[...] for ref in bases], axis=0)
    key = (tile_ref[...] * 3 + type_ref[...]).astype(jnp.float32)
    jac = assembled(base, feature_ref[0], key, place_ref[2])

    @pl.when(step // half == place_ref[0])
    def _():
        jac_ref[...] = jac

    @pl.when(step == 0)
    def _():
        gram[...] = jnp.zeros_like(gram)
        projected[...] = jnp.zeros_like(projected)

    middle = order // 2
    gram[:middle, :] += transposed_dot(jac[:, :middle], jac)
    gram[middle:, middle:] += transposed_dot(jac[:, middle:], jac[:, middle:])
    projected[...] += jnp.dot(grad_ref[0], jac, preferred_element_type=jnp.float32)

    @pl.when(step == pl.num_programs(0) - 1)
    def _():
        pack_gram(packed, gram, projected)
        size = outs[0].shape[0]
        for mask in range(GROUP):
            start = pl.multiple_of((place_ref[1] ^ mask) * size, 8)
            outs[mask][...] = packed[pl.ds(start, size), :]


def cut_index(cut, i, place):
    return (OWN_CUTS * i + cut, 0)


def own_part(place, base, feature, tile_row, type_row, gradient):
    cells, order = base.shape
    rows, width = gradient.shape
    half = rows // 2
    size = packed_rows(order) // GROUP
    return pl.pallas_call(
        own_kernel,
        grid_spec=pltpu.PrefetchScalarGridSpec(
            num_scalar_prefetch=1,
            grid=(rows,),
            in_specs=[
                pl.BlockSpec((width // OWN_CUTS, order), functools.partial(cut_index, k))
                for k in range(OWN_CUTS)
            ]
            + [
                pl.BlockSpec((1, FEATURES, width), lambda i, s: (i, 0, 0)),
                pl.BlockSpec((1, order), lambda i, s: (0, 0)),
                pl.BlockSpec((1, order), lambda i, s: (0, 0)),
                pl.BlockSpec((1, 1, width), lambda i, s: (i, 0, 0)),
            ],
            out_specs=[
                pl.BlockSpec(
                    (width, order), lambda i, s: (jnp.clip(i - s[0] * half, 0, half - 1), 0)
                )
            ]
            + [pl.BlockSpec((size, BLOCK), lambda i, s: (0, 0))] * GROUP,
            scratch_shapes=[
                pltpu.VMEM((order, order), jnp.float32),
                pltpu.VMEM((1, order), jnp.float32),
                pltpu.VMEM((GROUP * size, BLOCK), jnp.float32),
            ],
        ),
        out_shape=[jax.ShapeDtypeStruct((cells // 2, order), jnp.bfloat16)]
        + [jax.ShapeDtypeStruct((size, BLOCK), jnp.float32)] * GROUP,
        compiler_params=pltpu.CompilerParams(vmem_limit_bytes=WIDE_LIMIT),
        cost_estimate=BRIEF,
    )(place, *[base] * OWN_CUTS, feature, tile_row, type_row, gradient.reshape(rows, 1, width))


def send_kernel(pieces, place_ref, base_ref, tile_ref, type_ref, *refs):
    outs, (held, tiles, types, sems) = refs[-4 - len(pieces) : -4], refs[-4:]
    half = base_ref.shape[0] // 2
    low = min(piece[0] for piece in pieces)
    first = (1 - place_ref[0]) * half + low
    chunks = held.shape[0] // COPY_ROWS
    copies = [
        pltpu.make_async_copy(
            base_ref.at[pl.ds(pl.multiple_of(first + k * COPY_ROWS, COPY_ROWS), COPY_ROWS), :],
            held.at[pl.ds(k * COPY_ROWS, COPY_ROWS), :],
            sems.at[k],
        )
        for k in range(chunks)
    ]
    copies.append(pltpu.make_async_copy(tile_ref, tiles, sems.at[chunks]))
    copies.append(pltpu.make_async_copy(type_ref, types, sems.at[chunks + 1]))
    for copy in copies:
        copy.start()
    for k in range(chunks):
        copies[k].wait()
        for (top, end, left, right, _), out in zip(pieces, outs):
            row = low + k * COPY_ROWS
            if top <= row < end:
                out[pl.ds(row - top, COPY_ROWS), :] = held[
                    pl.ds(k * COPY_ROWS, COPY_ROWS), left:right
                ]
    copies[chunks].wait()
    copies[chunks + 1].wait()
    for (top, end, left, right, keyed), out in zip(pieces, outs):
        if keyed:
            key = (tiles[:, left:right] * 3 + types[:, left:right]).astype(jnp.float32)
            key = jnp.broadcast_to(key, (KEY_ROWS, right - left))
            out[pl.ds(end - top, KEY_ROWS), :] = key.astype(jnp.bfloat16)


def send_parts(place, base, tile_row, type_row, pieces, limit):
    order = base.shape[1]
    span = max(piece[1] for piece in pieces) - min(piece[0] for piece in pieces)
    return pl.pallas_call(
        functools.partial(send_kernel, tuple(pieces)),
        in_specs=[SMEM, ANY, ANY, ANY],
        out_specs=[VMEM] * len(pieces),
        out_shape=[
            jax.ShapeDtypeStruct((end - top + KEY_ROWS * keyed, right - left), base.dtype)
            for top, end, left, right, keyed in pieces
        ],
        scratch_shapes=[
            pltpu.VMEM((span, order), base.dtype),
            pltpu.VMEM((1, order), jnp.int32),
            pltpu.VMEM((1, order), jnp.int32),
            pltpu.SemaphoreType.DMA((span // COPY_ROWS + 2,)),
        ],
        compiler_params=pltpu.CompilerParams(vmem_limit_bytes=limit),
        cost_estimate=BRIEF,
    )(place, base, tile_row, type_row)


def cross_kernel(pieces, place_ref, jac_ref, feature_ref, *refs):
    received = refs[:pieces]
    outs = refs[-2 - GROUP : -2]
    total, out_ref = refs[-2:]
    cells, width = jac_ref.shape[0], feature_ref.shape[2]
    cuts = width // STEP_ROWS
    first = place_ref[0] * (cells // width)
    keyed = received[0].shape[0] - KEY_ROWS
    key = received[0][pl.ds(keyed, KEY_ROWS), :][0:1, :].astype(jnp.float32)
    total[...] = jnp.zeros_like(total)
    done = 0
    for piece in received:
        for step in range(piece.shape[0] // STEP_ROWS):
            lanes = pl.ds(done % cuts * STEP_ROWS, STEP_ROWS)
            feature = feature_ref[first + done // cuts, :, lanes]
            other = assembled(piece[pl.ds(step * STEP_ROWS, STEP_ROWS), :], feature, key, place_ref[2])
            total[...] += transposed_dot(other, jac_ref[pl.ds(done * STEP_ROWS, STEP_ROWS), :])
            done += 1

    count = total.shape[1] // BLOCK
    part = BLOCK // GROUP

    blocks = total.shape[0] // BLOCK

    @pl.when(place_ref[0] == 0)
    def _():
        for k in range(blocks):
            for q in range(GROUP):
                for c in range(count):
                    out_ref[q, pl.ds(BLOCK * k + part * c, part), :] = total[
                        pl.ds(BLOCK * k + part * q, part), pl.ds(BLOCK * c, BLOCK)
                    ]

    @pl.when(place_ref[0] != 0)
    def _():
        for k in range(blocks):
            for c in range(count):
                block = total[pl.ds(BLOCK * k, BLOCK), pl.ds(BLOCK * c, BLOCK)].T
                for q in range(GROUP):
                    out_ref[q, pl.ds(BLOCK * k + part * c, part), :] = block[
                        part * q : part * q + part
                    ]

    for mask in range(GROUP):
        outs[mask][...] = out_ref[place_ref[1] ^ mask]


def cross_part(place, received, jac, feature, *after):
    width_recv, order = received[0].shape[1], jac.shape[1]
    return pl.pallas_call(
        functools.partial(cross_kernel, len(received)),
        in_specs=[SMEM] + [VMEM] * (2 + len(received)) + [ANY] * len(after),
        out_specs=[VMEM] * GROUP,
        out_shape=[jax.ShapeDtypeStruct((width_recv, BLOCK), jnp.float32)] * GROUP,
        scratch_shapes=[
            pltpu.VMEM((width_recv, order), jnp.float32),
            pltpu.VMEM((GROUP, width_recv, BLOCK), jnp.float32),
        ],
        compiler_params=pltpu.CompilerParams(vmem_limit_bytes=LIMIT),
        cost_estimate=BRIEF,
    )(place, jac, feature, *received, *after)


def swap(value, axis, mask):
    count = lax.axis_size(axis)
    return lax.ppermute(value, axis, [(i, i ^ mask) for i in range(count)])


def add_kernel(count, *refs):
    refs[-1][...] = sum(ref[...] for ref in refs[1:count]) + refs[0][...]


def add(values, *after):
    return pl.pallas_call(
        functools.partial(add_kernel, len(values)),
        out_shape=jax.ShapeDtypeStruct(values[0].shape, values[0].dtype),
        in_specs=[VMEM] * len(values) + [ANY] * len(after),
        out_specs=VMEM,
        compiler_params=pltpu.CompilerParams(vmem_limit_bytes=LIMIT),
        cost_estimate=BRIEF,
    )(*values, *after)


def add_pass_kernel(*refs):
    *values, passed_ref, out_ref, copy_ref = refs
    out_ref[...] = sum(ref[...] for ref in values[1:]) + values[0][...]
    copy_ref[...] = passed_ref[...]


def add_pass(values, passed):
    return pl.pallas_call(
        add_pass_kernel,
        out_shape=[jax.ShapeDtypeStruct(v.shape, v.dtype) for v in (values[0], passed)],
        in_specs=[VMEM] * (len(values) + 1),
        out_specs=[VMEM] * 2,
        compiler_params=pltpu.CompilerParams(vmem_limit_bytes=LIMIT),
        cost_estimate=BRIEF,
    )(*values, passed)


def stacked_kernel(count, *refs):
    first, second, out_ref = refs[:count], refs[count:-1], refs[-1]
    rows = first[0].shape[0]
    out_ref[:rows, :] = sum(ref[...] for ref in first[1:]) + first[0][...]
    out_ref[rows:, :] = sum(ref[...] for ref in second[1:]) + second[0][...]


def stacked(first, second):
    rows = first[0].shape[0] + second[0].shape[0]
    return pl.pallas_call(
        functools.partial(stacked_kernel, len(first)),
        out_shape=jax.ShapeDtypeStruct((rows, BLOCK), jnp.float32),
        in_specs=[VMEM] * (len(first) + len(second)),
        out_specs=VMEM,
        compiler_params=pltpu.CompilerParams(vmem_limit_bytes=LIMIT),
        cost_estimate=BRIEF,
    )(*first, *second)


def joined_kernel(own_ref, other_ref, out_ref):
    part = BLOCK // GROUP
    blocks = own_ref.shape[0] // BLOCK
    for a in range(blocks):
        for b in range(blocks):
            out_ref[pl.ds(part * b, part), at(a)] = (
                own_ref[pl.ds(BLOCK * a + part * b, part), :]
                + other_ref[pl.ds(BLOCK * b + part * a, part), :]
            )


def joined(own, other):
    order = own.shape[0]
    return pl.pallas_call(
        joined_kernel,
        out_shape=jax.ShapeDtypeStruct((order // GROUP, order), jnp.float32),
        in_specs=[VMEM] * 2,
        out_specs=VMEM,
        compiler_params=pltpu.CompilerParams(vmem_limit_bytes=LIMIT),
        cost_estimate=BRIEF,
    )(own, other)


def group_swaps(parts):
    return [parts[0]] + [swap(parts[mask], "rows", mask) for mask in range(1, GROUP)]


def group_sum(parts):
    got = group_swaps(parts)
    return got[0] + got[1] + got[2] + got[3]


def groups_sum(held):
    masks = range(GROUP, lax.axis_size("rows"), GROUP)
    return held + sum(swap(held, "rows", mask) for mask in masks)


def doubled(held, masks):
    for mask in masks:
        held = held + swap(held, "rows", mask)
    return held


def rows_gather(own):
    return [own] + [swap(own, "rows", mask) for mask in range(1, GROUP)]


def near_gather(own):
    near, far = swap(own, "rows", 1), swap(own, "rows", 2)
    return [own, near, far, swap(far, "rows", 1)]


def first_factor_kernel(last, place_ref, *refs):
    pieces = refs[:GROUP]
    upper_ref, inverse_ref, projected_ref, whole = refs[GROUP + 1 :]
    size = pieces[0].shape[0]
    for mask in range(GROUP):
        start = pl.multiple_of((place_ref[1] ^ mask) * size, 8)
        whole[pl.ds(start, size), :] = pieces[mask][...]
    unpack_gram(whole, upper_ref, projected_ref)
    start_inverse(inverse_ref)
    factor_steps(upper_ref, inverse_ref, 0, last)


def square(order):
    return jax.ShapeDtypeStruct((order, order), jnp.float32)


def row(order):
    return jax.ShapeDtypeStruct((1, order), jnp.float32)


def first_factor(place, pieces, order, last, after):
    return pl.pallas_call(
        functools.partial(first_factor_kernel, last),
        out_shape=(square(order), square(order), row(order)),
        in_specs=[SMEM] + [VMEM] * GROUP + [ANY],
        out_specs=[VMEM] * 3,
        scratch_shapes=[pltpu.VMEM((packed_rows(order), BLOCK), jnp.float32)],
        compiler_params=pltpu.CompilerParams(vmem_limit_bytes=LIMIT),
        cost_estimate=BRIEF,
    )(place, *pieces, after)


def more_factor_kernel(first, last, upper_in, inverse_in, _, upper_ref, inverse_ref):
    del upper_in, inverse_in
    factor_steps(upper_ref, inverse_ref, first, last)


def more_factor(upper, inverse, first, last, after, cost):
    order = upper.shape[0]
    return pl.pallas_call(
        functools.partial(more_factor_kernel, first, last),
        out_shape=[square(order)] * 2,
        in_specs=[VMEM] * 2 + [ANY],
        out_specs=[VMEM] * 2,
        input_output_aliases={0: 0, 1: 1},
        compiler_params=pltpu.CompilerParams(vmem_limit_bytes=LIMIT),
        cost_estimate=cost,
    )(upper, inverse, after)


def lower_blocks(order):
    return [(a, b) for a in range(order // BLOCK) for b in range(a + 1)]


def lower_half(order):
    rows = len(lower_blocks(order)) * BLOCK + order // BLOCK
    return -(-rows // 16) * 8


def last_factor_kernel(
    first, place_ref, upper_in, inverse_in, projected, _, upper_ref, inverse, out_ref, half_ref, packed
):
    del upper_in, inverse_in
    order = upper_ref.shape[0]
    factor_steps(upper_ref, inverse, first, order // BLOCK)
    keep_upper(upper_ref)
    solved = solve_twice(inverse, projected)
    out_ref[...] = solved
    blocks = lower_blocks(order)
    for index, (a, b) in enumerate(blocks):
        packed[pl.ds(index * BLOCK, BLOCK), :] = inverse[
            pl.ds(a * BLOCK, BLOCK), pl.ds(b * BLOCK, BLOCK)
        ]
    start = len(blocks) * BLOCK
    packed[start:, :] = jnp.zeros((packed.shape[0] - start, BLOCK), jnp.float32)
    for c in range(order // BLOCK):
        packed[pl.ds(start + c, 1), :] = solved[:, c * BLOCK : (c + 1) * BLOCK]
    size = half_ref.shape[0]
    half_ref[...] = packed[pl.ds(pl.multiple_of(place_ref[1] % 2 * size, 8), size), :]


def last_factor(place, upper, inverse, projected, first, after, cost):
    order = upper.shape[0]
    size = lower_half(order)
    return pl.pallas_call(
        functools.partial(last_factor_kernel, first),
        out_shape=(
            square(order),
            square(order),
            row(order),
            jax.ShapeDtypeStruct((size, BLOCK), jnp.float32),
        ),
        in_specs=[SMEM] + [VMEM] * 3 + [ANY],
        out_specs=[VMEM] * 4,
        input_output_aliases={1: 0, 2: 1},
        scratch_shapes=[pltpu.VMEM((2 * size, BLOCK), jnp.float32)],
        compiler_params=pltpu.CompilerParams(vmem_limit_bytes=LIMIT),
        cost_estimate=cost,
    )(place, upper, inverse, projected, after)


def three_products(left, right):
    def parts(value):
        high = value.astype(jnp.bfloat16)
        return high, (value - high.astype(jnp.float32)).astype(jnp.bfloat16)

    def dot(a, b):
        return lax.dot_general(
            a, b, (((1,), (1,)), ((), ())), preferred_element_type=jnp.float32
        )

    (high, low), (other_high, other_low) = parts(left), parts(right)
    return dot(high, other_high) + (dot(high, other_low) + dot(low, other_high))


def finish_kernel(place_ref, upper_ref, solved_ref, half_ref, other_ref, *refs):
    pieces = refs[:GROUP]
    out_ref, multipliers_ref, cross, packed, inverse = refs[GROUP:]
    order = upper_ref.shape[0]
    part = BLOCK // GROUP

    @pl.when(place_ref[0] == 0)
    def _():
        out_ref[...] = upper_ref[...]
        multipliers_ref[...] = solved_ref[...]

    @pl.when(place_ref[0] != 0)
    def _():
        size = half_ref.shape[0]
        core = place_ref[1] % 2
        packed[pl.ds(pl.multiple_of(core * size, 8), size), :] = half_ref[...]
        packed[pl.ds(pl.multiple_of((1 - core) * size, 8), size), :] = other_ref[...]
        blocks = lower_blocks(order)
        for index, (a, b) in enumerate(blocks):
            inverse[pl.ds(a * BLOCK, BLOCK), pl.ds(b * BLOCK, BLOCK)] = packed[
                pl.ds(index * BLOCK, BLOCK), :
            ]
        for c in range(order // BLOCK):
            multipliers_ref[:, pl.ds(c * BLOCK, BLOCK)] = packed[
                pl.ds(len(blocks) * BLOCK + c, 1), :
            ]
        for mask in range(GROUP):
            quarter = place_ref[1] ^ mask
            for b in range(order // BLOCK):
                start = pl.multiple_of(BLOCK * b + part * quarter, part)
                cross[pl.ds(start, part), :] = pieces[mask][pl.ds(part * b, part), :]
        for a in range(order // BLOCK):
            rows, depth = pl.ds(a * BLOCK, BLOCK), (a + 1) * BLOCK
            out_ref[rows, :] = three_products(
                inverse[rows, pl.ds(0, depth)], cross[:, pl.ds(0, depth)]
            )


def finish(place, upper, solved, half, other, pieces):
    order = upper.shape[0]
    return pl.pallas_call(
        finish_kernel,
        out_shape=(square(order), row(order)),
        in_specs=[SMEM] + [VMEM] * (4 + GROUP),
        out_specs=[VMEM] * 2,
        scratch_shapes=[
            pltpu.VMEM((order, order), jnp.float32),
            pltpu.VMEM((2 * lower_half(order), BLOCK), jnp.float32),
            pltpu.VMEM((order, order), jnp.float32),
        ],
        compiler_params=pltpu.CompilerParams(vmem_limit_bytes=LIMIT),
        cost_estimate=BRIEF,
    )(place, upper, solved, half, other, *pieces)


def shards(sens_base, design_field, gradient, tile_index, type_codes):
    cells, order = sens_base.shape
    rows_here, width = design_field.shape
    side = lax.axis_index("cols")
    quarter = lax.axis_index("rows") % GROUP
    tiles = width // TILE
    first_tile = lax.axis_index("rows") * rows_here // TILE * tiles
    place = jnp.stack([side, quarter, 3 * first_tile]).astype(jnp.int32)
    tile_row, type_row = tile_index[None, :], type_codes[None, :]

    half, split = cells // 2, order - BLOCK
    middle = half // 2
    rows = [
        [(0, middle, 0, split, True)],
        [(middle, half, 0, split, False)],
        [(0, half, split, order, True)],
    ]
    wide = WIDE_LIMIT + 6 * 2**20
    sent = [
        send_parts(place, sens_base, tile_row, type_row, pieces, limit)[0]
        for pieces, limit in zip(rows, (wide, wide, TAIL_LIMIT))
    ]
    lead, rest, tail = [swap(part, "cols", 1) for part in sent]
    received = [[lead, rest], [tail]]

    count = lax.axis_size("rows")
    north = lax.ppermute(design_field[-1:], "rows", [(i, i + 1) for i in range(count - 1)])
    south = lax.ppermute(design_field[:1], "rows", [(i + 1, i) for i in range(count - 1)])
    feature = features(design_field, north, south)
    jac, *packed = own_part(place, sens_base, feature, tile_row, type_row, gradient)
    pieces = rows_gather(groups_sum(group_sum(packed)))

    def stage(index, *after):
        return cross_part(place, received[index], jac, feature, *after)

    upper, inverse, projected = first_factor(place, pieces, order, 1, pieces[0])
    first = stage(0, upper)
    shares = group_swaps(first)
    upper, inverse = more_factor(upper, inverse, 1, 2, first[0], LONG)
    held = add(shares, inverse)
    shares = [held, swap(held, "rows", GROUP)]
    upper, inverse = more_factor(upper, inverse, 2, 3, held, LONG)
    middle = add(shares, inverse)
    far = range(2 * GROUP, count, 2 * GROUP)
    far_shares = [middle] + [swap(middle, "rows", mask) for mask in far]
    last = stage(1, middle)
    shares = group_swaps(last)
    upper, _, solved, half = last_factor(place, upper, inverse, projected, 3, last[0], LONG)
    held_last, half = add_pass(shares, half)
    shares = [held_last] + [swap(held_last, "rows", mask) for mask in range(GROUP, count, GROUP)]
    totals = stacked(far_shares, shares)
    others = lax.ppermute(totals, "cols", [(0, 1)])
    half = lax.ppermute(half, "cols", [(0, 1)])

    cross = joined(totals, others)
    r_panels, multipliers = finish(
        place, upper, solved, half, swap(half, "rows", 1), near_gather(cross)
    )
    return (r_panels, multipliers[0])


def shards_general(sens_base, design_field, gradient, tile_index, type_codes):
    rows_here = design_field.shape[0]
    grid_width = design_field.shape[1]
    cols_here = sens_base.shape[1]
    factored = 2 * PW
    padded = padded_2(design_field, (("rows", 0),), 1)
    padded = jnp.pad(padded, ((0, 0), (1, 1)))
    north_cells = padded[:-2, 1:-1]
    south_cells = padded[2:, 1:-1]
    west_cells = padded[1:-1, :-2]
    east_cells = padded[1:-1, 2:]
    laplace = 4.0 * design_field - (north_cells + south_cells + west_cells + east_cells)
    slope_x = 0.5 * (east_cells - west_cells)
    slope_y = 0.5 * (south_cells - north_cells)
    stencils = jnp.stack([laplace, slope_x, slope_y]).reshape(3, -1)
    row_glob = lax.axis_index("rows") * rows_here + jnp.arange(rows_here, dtype=jnp.int32)
    col_ids = jnp.arange(grid_width, dtype=jnp.int32) // TILE
    cell_tile = ((row_glob // TILE)[:, None] * (grid_width // TILE) + col_ids[None, :]).reshape(-1)
    local_jac = assemble(sens_base, tile_index, type_codes, stencils, cell_tile)
    grad_flat = gradient.reshape(-1)
    row_major = lax.all_to_all(local_jac, "cols", split_axis=0, concat_axis=1, tiled=True)
    row_piece = row_major.shape[0]
    grad_part = lax.dynamic_slice_in_dim(
        grad_flat, lax.axis_index("cols") * row_piece, row_piece, 0
    )
    leading = row_major[:, :factored]
    gram_block = lax.dot_general(
        leading, row_major, (((0,), (0,)), ((), ())), preferred_element_type=jnp.float32
    )
    projected = jnp.dot(grad_part, leading, preferred_element_type=jnp.float32)
    gram_block, projected = lax.psum((gram_block, projected), ("rows", "cols"))
    gram_head = gram_block[:, :factored]
    gram_own = lax.dynamic_slice_in_dim(
        gram_block, lax.axis_index("cols") * cols_here, cols_here, 1
    )
    _, inverse, multipliers = factor(gram_head, projected[None, :])
    r_panels = matmul(inverse, gram_own)
    return (r_panels, multipliers[0])


def solution(mesh):
    placed = (P("rows", "cols"), P("rows", None), P("rows", None), P("cols"), P("cols"))
    pairs = mesh.shape["cols"] == 2 and mesh.shape["rows"] in (8, 16, 32, 64)
    return jax.shard_map(
        shards if pairs else shards_general,
        mesh=mesh,
        in_specs=placed,
        out_specs=(P(None, "cols"), P()),
        check_vma=False,
    )
```

```python
import functools

import jax
import jax.numpy as jnp
from jax import lax
from jax.experimental import pallas as pl
from jax.experimental.pallas import tpu as pltpu
from jax.sharding import PartitionSpec as P

TILE = 128
PW = 256
BLOCK = 128
FEATURES = 80
KEY_ROWS = 16
STEP_ROWS = 1024
COPY_ROWS = 256
OWN_CUTS = 4
GROUP = 4
HIGHEST = lax.Precision.HIGHEST
VMEM = pl.BlockSpec(memory_space=pltpu.VMEM)
SMEM = pl.BlockSpec(memory_space=pltpu.SMEM)
LIMIT = 12 * 2**20
WIDE_LIMIT = 48 * 2**20
TAIL_LIMIT = 36 * 2**20
ANY = pl.BlockSpec(memory_space=pl.ANY)
LONG = pl.CostEstimate(flops=8 * 10**9, bytes_accessed=1000, transcendentals=0)
BRIEF = pl.CostEstimate(flops=1000, bytes_accessed=1000, transcendentals=0)


def padded_2(cells, sides, width):
    for axis, dim in sides:
        count = lax.axis_size(axis)
        ends = count - 1
        head = lax.slice_in_dim(cells, 0, width, axis=dim)
        tail = lax.slice_in_dim(cells, cells.shape[dim] - width, cells.shape[dim], axis=dim)
        cells = jnp.concatenate(
            [
                lax.ppermute(tail, axis, [(i, (i + 1) % count) for i in range(ends)]),
                cells,
                lax.ppermute(head, axis, [((i + 1) % count, i) for i in range(ends)]),
            ],
            axis=dim,
        )
    return cells


def assemble(base_cols, tile_cols, type_cols, stencils, cell_tile):
    kinds_all = jnp.arange(3, dtype=jnp.int32)
    chooser = (type_cols[None, :] == kinds_all[:, None]).astype(jnp.float32)
    picked = lax.dot_general(
        stencils,
        chooser,
        (((0,), (0,)), ((), ())),
        precision=lax.Precision.HIGHEST,
        preferred_element_type=jnp.float32,
    )
    inside = cell_tile[:, None] == tile_cols[None, :]
    total = base_cols.astype(jnp.float32) + jnp.where(inside, picked / TILE, 0.0)
    return total.astype(jnp.bfloat16)


def matmul(left, right):
    return jnp.dot(left, right, precision=HIGHEST, preferred_element_type=jnp.float32)


def tree_sum(terms):
    while len(terms) > 1:
        terms = [a + b for a, b in zip(terms[::2], terms[1::2])] + terms[len(terms) // 2 * 2 :]
    return terms[0]


def lane(part, index):
    return jnp.broadcast_to(part[:, index : index + 1], part.shape)


def sublane(part, index):
    return jnp.broadcast_to(part[index : index + 1, :], part.shape)


def diagonal_inverse(block):
    groups = BLOCK // 8
    shape = (8, BLOCK)
    lanes = lax.broadcasted_iota(jnp.int32, shape, 1)
    subs = lax.broadcasted_iota(jnp.int32, shape, 0)
    parts = [block[8 * g : 8 * g + 8, :] for g in range(groups)]
    whole = []
    for p in range(groups):
        part, first = parts[p], 8 * p
        cols = [lane(part, first + k) for k in range(8)]
        inv = [None] * 8
        low = [jnp.zeros(shape, jnp.float32) for _ in range(8)]
        scale = jnp.ones(shape, jnp.float32)
        for j in range(8):
            here = subs == j
            root = lax.rsqrt(sublane(cols[j], j))
            ratio = root * root
            scale = jnp.where(here, root, scale)
            for k in range(j):
                low[k] = jnp.where(here, inv[k], low[k])
            low[j] = jnp.where(here, 1.0, low[j])
            column = cols[j]
            for part_list, chosen in ((cols, range(j + 1, 8)), (inv, range(j))):
                for k in chosen:
                    row = sublane(part_list[k], j)
                    share = jnp.where(here, -row, column * row)
                    part_list[k] = jnp.where(here, 0.0, part_list[k]) - share * ratio
            inv[j] = jnp.where(here, 1.0, -column) * ratio
        inside = (lanes >= first) & (lanes < first + 8)
        unit = jnp.where(lanes - first == subs, 1.0, 0.0)
        rows = jnp.where(inside, unit, part)
        spread = [sublane(rows, k) for k in range(8)]
        solved = tree_sum([low[k] * spread[k] for k in range(8)]) * scale
        whole.append(jnp.where(lanes < first + 8, solved, 0.0))
        if p + 1 < groups:
            step = tree_sum([inv[k] * spread[k] for k in range(8)])
            step = [sublane(step, k) for k in range(8)]
            for g in range(p + 1, groups):
                taken = tree_sum([lane(parts[g], first + k) * step[k] for k in range(8)])
                parts[g] = jnp.where(inside, 0.0, parts[g]) - taken
    return jnp.concatenate(whole, axis=0)


def factor_steps(upper_ref, inverse_ref, first, last):
    order = upper_ref.shape[0]
    for step in range(first, last):
        mine, done = pl.ds(step * BLOCK, BLOCK), pl.ds(0, (step + 1) * BLOCK)
        ahead = pl.ds(step * BLOCK, order - step * BLOCK)
        small = diagonal_inverse(upper_ref[mine, mine])
        panel = matmul(small, upper_ref[mine, ahead])
        upper_ref[mine, ahead] = panel
        solved = matmul(small, inverse_ref[mine, done])
        inverse_ref[mine, done] = solved
        for later in range(step + 1, order // BLOCK):
            theirs = pl.ds(later * BLOCK, BLOCK)
            left = (later - step) * BLOCK
            factor = panel[:, left : left + BLOCK]

            def product(right):
                return lax.dot_general(
                    factor,
                    right,
                    (((0,), (0,)), ((), ())),
                    precision=HIGHEST,
                    preferred_element_type=jnp.float32,
                )

            upper_ref[theirs, pl.ds(later * BLOCK, order - later * BLOCK)] -= product(
                panel[:, left:]
            )
            inverse_ref[theirs, done] -= product(solved)


def start_inverse(inverse_ref):
    rows = lax.broadcasted_iota(jnp.int32, inverse_ref.shape, 0)
    cols = lax.broadcasted_iota(jnp.int32, inverse_ref.shape, 1)
    inverse_ref[...] = jnp.where(rows == cols, 1.0, 0.0)


def keep_upper(upper_ref):
    rows = lax.broadcasted_iota(jnp.int32, upper_ref.shape, 0)
    cols = lax.broadcasted_iota(jnp.int32, upper_ref.shape, 1)
    upper_ref[...] = jnp.where(rows <= cols, upper_ref[...], 0.0)


def solve_twice(inverse_ref, projected_ref):
    half = jnp.sum(inverse_ref[...] * projected_ref[...], axis=1, keepdims=True)
    return jnp.sum(inverse_ref[...] * half, axis=0, keepdims=True)


def factor_kernel(gram_ref, projected_ref, upper_ref, inverse_ref, multipliers_ref):
    upper_ref[...] = gram_ref[...]
    start_inverse(inverse_ref)
    factor_steps(upper_ref, inverse_ref, 0, upper_ref.shape[0] // BLOCK)
    keep_upper(upper_ref)
    multipliers_ref[...] = solve_twice(inverse_ref, projected_ref)


def factor(gram, projected):
    order = gram.shape[0]
    return pl.pallas_call(
        factor_kernel,
        out_shape=(
            jax.ShapeDtypeStruct((order, order), jnp.float32),
            jax.ShapeDtypeStruct((order, order), jnp.float32),
            jax.ShapeDtypeStruct((1, order), jnp.float32),
        ),
        in_specs=[pl.BlockSpec(memory_space=pltpu.VMEM)] * 2,
        out_specs=[pl.BlockSpec(memory_space=pltpu.VMEM)] * 3,
        compiler_params=pltpu.CompilerParams(vmem_limit_bytes=LIMIT),
        cost_estimate=pl.CostEstimate(
            flops=6 * order**3, bytes_accessed=12 * order**2, transcendentals=0
        ),
    )(gram, projected)


def features_kernel(field_ref, north_ref, south_ref, out_ref):
    field = field_ref[...]
    rows, width = field.shape
    lanes = lax.broadcasted_iota(jnp.int32, field.shape, 1)
    north = jnp.concatenate([north_ref[...], field[:-1]], axis=0)
    south = jnp.concatenate([field[1:], south_ref[...]], axis=0)
    west = jnp.where(lanes == 0, 0.0, pltpu.roll(field, 1, 1))
    east = jnp.where(lanes == width - 1, 0.0, pltpu.roll(field, width - 1, 1))
    laplace = 4.0 * field - (north + south + west + east)
    slope_x = 0.5 * (east - west)
    slope_y = 0.5 * (south - north)
    parts = []
    for stencil in (laplace, slope_x, slope_y):
        rest = stencil / TILE
        for _ in range(3):
            part = rest.astype(jnp.bfloat16).astype(jnp.float32)
            parts.append(part)
            rest = rest - part
    tiles = width // TILE
    shape = (FEATURES, width)
    owner = lax.broadcasted_iota(jnp.int32, shape, 0) // len(parts)
    tile = lax.broadcasted_iota(jnp.int32, shape, 1) // TILE
    blank = jnp.zeros((FEATURES - tiles * len(parts), width), jnp.float32)
    for row in range(rows):
        block = jnp.concatenate([part[row : row + 1] for part in parts], axis=0)
        whole = jnp.concatenate([block] * tiles + [blank], axis=0)
        out_ref[row] = jnp.where(owner == tile, whole, 0.0).astype(jnp.bfloat16)


def features(field, north, south):
    rows, width = field.shape
    return pl.pallas_call(
        features_kernel,
        out_shape=jax.ShapeDtypeStruct((rows, FEATURES, width), jnp.bfloat16),
        in_specs=[VMEM] * 3,
        out_specs=VMEM,
        compiler_params=pltpu.CompilerParams(vmem_limit_bytes=LIMIT),
        cost_estimate=BRIEF,
    )(field, north, south)


def assembled(base, feature, key, first):
    rows = lax.broadcasted_iota(jnp.int32, (FEATURES, key.shape[1]), 0) // 3 + first
    chooser = jnp.where(rows.astype(jnp.float32) == key, 1.0, 0.0).astype(jnp.bfloat16)
    added = lax.dot_general(
        feature, chooser, (((0,), (0,)), ((), ())), preferred_element_type=jnp.float32
    )
    return (base.astype(jnp.float32) + added).astype(jnp.bfloat16)


def transposed_dot(left, right):
    return lax.dot_general(
        left, right, (((0,), (0,)), ((), ())), preferred_element_type=jnp.float32
    )


def strict_blocks(order):
    count = order // BLOCK
    return [(a, b) for a in range(count) for b in range(a + 1, count)]


def packed_rows(order):
    count = order // BLOCK
    used = (len(strict_blocks(order)) + count // 2) * BLOCK + count // 2 + count
    return -(-used // (8 * GROUP)) * 8 * GROUP


def triangles():
    rows = lax.broadcasted_iota(jnp.int32, (BLOCK, BLOCK), 0)
    cols = lax.broadcasted_iota(jnp.int32, (BLOCK, BLOCK), 1)
    return rows < cols, rows == cols


def at(index):
    return pl.ds(index * BLOCK, BLOCK)


def pack_gram(packed, gram, projected):
    order = gram.shape[0]
    packed[...] = jnp.zeros_like(packed)
    blocks = strict_blocks(order)
    for index, (a, b) in enumerate(blocks):
        packed[at(index), :] = gram[at(a), at(b)]
    above, diagonal = triangles()
    pairs = order // BLOCK // 2
    row = (len(blocks) + pairs) * BLOCK
    for p in range(pairs):
        second = gram[at(2 * p + 1), at(2 * p + 1)]
        packed[at(len(blocks) + p), :] = jnp.where(
            above | diagonal, gram[at(2 * p), at(2 * p)], second
        )
        packed[pl.ds(row + p, 1), :] = jnp.sum(
            jnp.where(diagonal, second, 0.0), axis=0, keepdims=True
        )
    for c in range(order // BLOCK):
        packed[pl.ds(row + pairs + c, 1), :] = projected[:, at(c)]


def unpack_gram(packed, upper_ref, projected_ref):
    order = upper_ref.shape[0]
    upper_ref[...] = jnp.zeros_like(upper_ref)
    blocks = strict_blocks(order)
    for index, (a, b) in enumerate(blocks):
        upper_ref[at(a), at(b)] = packed[at(index), :]
    above, diagonal = triangles()
    pairs = order // BLOCK // 2
    row = (len(blocks) + pairs) * BLOCK
    for p in range(pairs):
        both = packed[at(len(blocks) + p), :]
        turned = both.T
        upper_ref[at(2 * p), at(2 * p)] = jnp.where(above | diagonal, both, turned)
        upper_ref[at(2 * p + 1), at(2 * p + 1)] = jnp.where(
            diagonal, packed[pl.ds(row + p, 1), :], jnp.where(above, turned, both)
        )
    for c in range(order // BLOCK):
        projected_ref[:, at(c)] = packed[pl.ds(row + pairs + c, 1), :]


def own_kernel(
    place_ref, *refs
):
    bases = refs[:OWN_CUTS]
    feature_ref, tile_ref, type_ref, grad_ref, jac_ref = refs[OWN_CUTS : OWN_CUTS + 5]
    outs = refs[OWN_CUTS + 5 : OWN_CUTS + 5 + GROUP]
    gram, projected, packed = refs[OWN_CUTS + 5 + GROUP :]
    step = pl.program_id(0)
    half = pl.num_programs(0) // 2
    order = gram.shape[0]
    base = jnp.concatenate([ref[...] for ref in bases], axis=0)
    key = (tile_ref[...] * 3 + type_ref[...]).astype(jnp.float32)
    jac = assembled(base, feature_ref[0], key, place_ref[2])

    @pl.when(step // half == place_ref[0])
    def _():
        jac_ref[...] = jac

    @pl.when(step == 0)
    def _():
        gram[...] = jnp.zeros_like(gram)
        projected[...] = jnp.zeros_like(projected)

    middle = order // 2
    gram[:middle, :] += transposed_dot(jac[:, :middle], jac)
    gram[middle:, middle:] += transposed_dot(jac[:, middle:], jac[:, middle:])
    projected[...] += jnp.dot(grad_ref[0], jac, preferred_element_type=jnp.float32)

    @pl.when(step == pl.num_programs(0) - 1)
    def _():
        pack_gram(packed, gram, projected)
        size = outs[0].shape[0]
        for mask in range(GROUP):
            start = pl.multiple_of((place_ref[1] ^ mask) * size, 8)
            outs[mask][...] = packed[pl.ds(start, size), :]


def cut_index(cut, i, place):
    return (OWN_CUTS * i + cut, 0)


def own_part(place, base, feature, tile_row, type_row, gradient):
    cells, order = base.shape
    rows, width = gradient.shape
    half = rows // 2
    size = packed_rows(order) // GROUP
    return pl.pallas_call(
        own_kernel,
        grid_spec=pltpu.PrefetchScalarGridSpec(
            num_scalar_prefetch=1,
            grid=(rows,),
            in_specs=[
                pl.BlockSpec((width // OWN_CUTS, order), functools.partial(cut_index, k))
                for k in range(OWN_CUTS)
            ]
            + [
                pl.BlockSpec((1, FEATURES, width), lambda i, s: (i, 0, 0)),
                pl.BlockSpec((1, order), lambda i, s: (0, 0)),
                pl.BlockSpec((1, order), lambda i, s: (0, 0)),
                pl.BlockSpec((1, 1, width), lambda i, s: (i, 0, 0)),
            ],
            out_specs=[
                pl.BlockSpec(
                    (width, order), lambda i, s: (jnp.clip(i - s[0] * half, 0, half - 1), 0)
                )
            ]
            + [pl.BlockSpec((size, BLOCK), lambda i, s: (0, 0))] * GROUP,
            scratch_shapes=[
                pltpu.VMEM((order, order), jnp.float32),
                pltpu.VMEM((1, order), jnp.float32),
                pltpu.VMEM((GROUP * size, BLOCK), jnp.float32),
            ],
        ),
        out_shape=[jax.ShapeDtypeStruct((cells // 2, order), jnp.bfloat16)]
        + [jax.ShapeDtypeStruct((size, BLOCK), jnp.float32)] * GROUP,
        compiler_params=pltpu.CompilerParams(vmem_limit_bytes=WIDE_LIMIT),
        cost_estimate=BRIEF,
    )(place, *[base] * OWN_CUTS, feature, tile_row, type_row, gradient.reshape(rows, 1, width))


def send_kernel(pieces, place_ref, base_ref, tile_ref, type_ref, *refs):
    outs, (held, tiles, types, sems) = refs[-4 - len(pieces) : -4], refs[-4:]
    half = base_ref.shape[0] // 2
    low = min(piece[0] for piece in pieces)
    first = (1 - place_ref[0]) * half + low
    chunks = held.shape[0] // COPY_ROWS
    copies = [
        pltpu.make_async_copy(
            base_ref.at[pl.ds(pl.multiple_of(first + k * COPY_ROWS, COPY_ROWS), COPY_ROWS), :],
            held.at[pl.ds(k * COPY_ROWS, COPY_ROWS), :],
            sems.at[k],
        )
        for k in range(chunks)
    ]
    copies.append(pltpu.make_async_copy(tile_ref, tiles, sems.at[chunks]))
    copies.append(pltpu.make_async_copy(type_ref, types, sems.at[chunks + 1]))
    for copy in copies:
        copy.start()
    for k in range(chunks):
        copies[k].wait()
        for (top, end, left, right, _), out in zip(pieces, outs):
            row = low + k * COPY_ROWS
            if top <= row < end:
                out[pl.ds(row - top, COPY_ROWS), :] = held[
                    pl.ds(k * COPY_ROWS, COPY_ROWS), left:right
                ]
    copies[chunks].wait()
    copies[chunks + 1].wait()
    for (top, end, left, right, keyed), out in zip(pieces, outs):
        if keyed:
            key = (tiles[:, left:right] * 3 + types[:, left:right]).astype(jnp.float32)
            key = jnp.broadcast_to(key, (KEY_ROWS, right - left))
            out[pl.ds(end - top, KEY_ROWS), :] = key.astype(jnp.bfloat16)


def send_parts(place, base, tile_row, type_row, pieces, limit):
    order = base.shape[1]
    span = max(piece[1] for piece in pieces) - min(piece[0] for piece in pieces)
    return pl.pallas_call(
        functools.partial(send_kernel, tuple(pieces)),
        in_specs=[SMEM, ANY, ANY, ANY],
        out_specs=[VMEM] * len(pieces),
        out_shape=[
            jax.ShapeDtypeStruct((end - top + KEY_ROWS * keyed, right - left), base.dtype)
            for top, end, left, right, keyed in pieces
        ],
        scratch_shapes=[
            pltpu.VMEM((span, order), base.dtype),
            pltpu.VMEM((1, order), jnp.int32),
            pltpu.VMEM((1, order), jnp.int32),
            pltpu.SemaphoreType.DMA((span // COPY_ROWS + 2,)),
        ],
        compiler_params=pltpu.CompilerParams(vmem_limit_bytes=limit),
        cost_estimate=BRIEF,
    )(place, base, tile_row, type_row)


def cross_kernel(pieces, place_ref, jac_ref, feature_ref, *refs):
    received = refs[:pieces]
    outs = refs[-2 - GROUP : -2]
    total, out_ref = refs[-2:]
    cells, width = jac_ref.shape[0], feature_ref.shape[2]
    cuts = width // STEP_ROWS
    first = place_ref[0] * (cells // width)
    keyed = received[0].shape[0] - KEY_ROWS
    key = received[0][pl.ds(keyed, KEY_ROWS), :][0:1, :].astype(jnp.float32)
    total[...] = jnp.zeros_like(total)
    done = 0
    for piece in received:
        for step in range(piece.shape[0] // STEP_ROWS):
            lanes = pl.ds(done % cuts * STEP_ROWS, STEP_ROWS)
            feature = feature_ref[first + done // cuts, :, lanes]
            other = assembled(piece[pl.ds(step * STEP_ROWS, STEP_ROWS), :], feature, key, place_ref[2])
            total[...] += transposed_dot(other, jac_ref[pl.ds(done * STEP_ROWS, STEP_ROWS), :])
            done += 1

    count = total.shape[1] // BLOCK
    part = BLOCK // GROUP

    blocks = total.shape[0] // BLOCK

    @pl.when(place_ref[0] == 0)
    def _():
        for k in range(blocks):
            for q in range(GROUP):
                for c in range(count):
                    out_ref[q, pl.ds(BLOCK * k + part * c, part), :] = total[
                        pl.ds(BLOCK * k + part * q, part), pl.ds(BLOCK * c, BLOCK)
                    ]

    @pl.when(place_ref[0] != 0)
    def _():
        for k in range(blocks):
            for c in range(count):
                block = total[pl.ds(BLOCK * k, BLOCK), pl.ds(BLOCK * c, BLOCK)].T
                for q in range(GROUP):
                    out_ref[q, pl.ds(BLOCK * k + part * c, part), :] = block[
                        part * q : part * q + part
                    ]

    for mask in range(GROUP):
        outs[mask][...] = out_ref[place_ref[1] ^ mask]


def cross_part(place, received, jac, feature, *after):
    width_recv, order = received[0].shape[1], jac.shape[1]
    return pl.pallas_call(
        functools.partial(cross_kernel, len(received)),
        in_specs=[SMEM] + [VMEM] * (2 + len(received)) + [ANY] * len(after),
        out_specs=[VMEM] * GROUP,
        out_shape=[jax.ShapeDtypeStruct((width_recv, BLOCK), jnp.float32)] * GROUP,
        scratch_shapes=[
            pltpu.VMEM((width_recv, order), jnp.float32),
            pltpu.VMEM((GROUP, width_recv, BLOCK), jnp.float32),
        ],
        compiler_params=pltpu.CompilerParams(vmem_limit_bytes=LIMIT),
        cost_estimate=BRIEF,
    )(place, jac, feature, *received, *after)


def swap(value, axis, mask):
    count = lax.axis_size(axis)
    return lax.ppermute(value, axis, [(i, i ^ mask) for i in range(count)])


def add_kernel(count, *refs):
    refs[-1][...] = sum(ref[...] for ref in refs[1:count]) + refs[0][...]


def add(values, *after):
    return pl.pallas_call(
        functools.partial(add_kernel, len(values)),
        out_shape=jax.ShapeDtypeStruct(values[0].shape, values[0].dtype),
        in_specs=[VMEM] * len(values) + [ANY] * len(after),
        out_specs=VMEM,
        compiler_params=pltpu.CompilerParams(vmem_limit_bytes=LIMIT),
        cost_estimate=BRIEF,
    )(*values, *after)


def add_pass_kernel(*refs):
    *values, passed_ref, _, out_ref, copy_ref = refs
    out_ref[...] = sum(ref[...] for ref in values[1:]) + values[0][...]
    copy_ref[...] = passed_ref[...]


def add_pass(values, passed, after):
    return pl.pallas_call(
        add_pass_kernel,
        out_shape=[jax.ShapeDtypeStruct(v.shape, v.dtype) for v in (values[0], passed)],
        in_specs=[VMEM] * (len(values) + 1) + [ANY],
        out_specs=[VMEM] * 2,
        compiler_params=pltpu.CompilerParams(vmem_limit_bytes=LIMIT),
        cost_estimate=BRIEF,
    )(*values, passed, after)


def stacked_kernel(count, *refs):
    first, second, out_ref = refs[:count], refs[count:-2], refs[-1]
    rows = first[0].shape[0]
    out_ref[:rows, :] = sum(ref[...] for ref in first[1:]) + first[0][...]
    out_ref[rows:, :] = sum(ref[...] for ref in second[1:]) + second[0][...]


def stacked(first, second, after):
    rows = first[0].shape[0] + second[0].shape[0]
    return pl.pallas_call(
        functools.partial(stacked_kernel, len(first)),
        out_shape=jax.ShapeDtypeStruct((rows, BLOCK), jnp.float32),
        in_specs=[VMEM] * (len(first) + len(second)) + [ANY],
        out_specs=VMEM,
        compiler_params=pltpu.CompilerParams(vmem_limit_bytes=LIMIT),
        cost_estimate=BRIEF,
    )(*first, *second, after)


def joined_kernel(own_ref, other_ref, out_ref):
    part = BLOCK // GROUP
    blocks = own_ref.shape[0] // BLOCK
    for a in range(blocks):
        for b in range(blocks):
            out_ref[pl.ds(part * b, part), at(a)] = (
                own_ref[pl.ds(BLOCK * a + part * b, part), :]
                + other_ref[pl.ds(BLOCK * b + part * a, part), :]
            )


def joined(own, other):
    order = own.shape[0]
    return pl.pallas_call(
        joined_kernel,
        out_shape=jax.ShapeDtypeStruct((order // GROUP, order), jnp.float32),
        in_specs=[VMEM] * 2,
        out_specs=VMEM,
        compiler_params=pltpu.CompilerParams(vmem_limit_bytes=LIMIT),
        cost_estimate=BRIEF,
    )(own, other)


def group_swaps(parts):
    return [parts[0]] + [swap(parts[mask], "rows", mask) for mask in range(1, GROUP)]


def group_sum(parts):
    got = group_swaps(parts)
    return got[0] + got[1] + got[2] + got[3]


def groups_sum(held):
    masks = range(GROUP, lax.axis_size("rows"), GROUP)
    return held + sum(swap(held, "rows", mask) for mask in masks)


def doubled(held, masks):
    for mask in masks:
        held = held + swap(held, "rows", mask)
    return held


def rows_gather(own):
    return [own] + [swap(own, "rows", mask) for mask in range(1, GROUP)]


def near_gather(own):
    near, far = swap(own, "rows", 1), swap(own, "rows", 2)
    return [own, near, far, swap(far, "rows", 1)]


def first_factor_kernel(last, place_ref, *refs):
    pieces = refs[:GROUP]
    upper_ref, inverse_ref, projected_ref, whole = refs[GROUP + 1 :]
    size = pieces[0].shape[0]
    for mask in range(GROUP):
        start = pl.multiple_of((place_ref[1] ^ mask) * size, 8)
        whole[pl.ds(start, size), :] = pieces[mask][...]
    unpack_gram(whole, upper_ref, projected_ref)
    start_inverse(inverse_ref)
    factor_steps(upper_ref, inverse_ref, 0, last)


def square(order):
    return jax.ShapeDtypeStruct((order, order), jnp.float32)


def row(order):
    return jax.ShapeDtypeStruct((1, order), jnp.float32)


def first_factor(place, pieces, order, last, after):
    return pl.pallas_call(
        functools.partial(first_factor_kernel, last),
        out_shape=(square(order), square(order), row(order)),
        in_specs=[SMEM] + [VMEM] * GROUP + [ANY],
        out_specs=[VMEM] * 3,
        scratch_shapes=[pltpu.VMEM((packed_rows(order), BLOCK), jnp.float32)],
        compiler_params=pltpu.CompilerParams(vmem_limit_bytes=LIMIT),
        cost_estimate=BRIEF,
    )(place, *pieces, after)


def more_factor_kernel(first, last, upper_in, inverse_in, _, upper_ref, inverse_ref):
    del upper_in, inverse_in
    factor_steps(upper_ref, inverse_ref, first, last)


def more_factor(upper, inverse, first, last, after, cost):
    order = upper.shape[0]
    return pl.pallas_call(
        functools.partial(more_factor_kernel, first, last),
        out_shape=[square(order)] * 2,
        in_specs=[VMEM] * 2 + [ANY],
        out_specs=[VMEM] * 2,
        input_output_aliases={0: 0, 1: 1},
        compiler_params=pltpu.CompilerParams(vmem_limit_bytes=LIMIT),
        cost_estimate=cost,
    )(upper, inverse, after)


def lower_blocks(order):
    return [(a, b) for a in range(order // BLOCK) for b in range(a + 1)]


def lower_half(order):
    rows = len(lower_blocks(order)) * BLOCK + order // BLOCK
    return -(-rows // 16) * 8


def last_factor_kernel(
    first, place_ref, upper_in, inverse_in, projected, _, upper_ref, inverse, out_ref, half_ref, packed
):
    del upper_in, inverse_in
    order = upper_ref.shape[0]
    factor_steps(upper_ref, inverse, first, order // BLOCK)
    solved = solve_twice(inverse, projected)
    out_ref[...] = solved
    blocks = lower_blocks(order)
    for index, (a, b) in enumerate(blocks):
        packed[pl.ds(index * BLOCK, BLOCK), :] = inverse[
            pl.ds(a * BLOCK, BLOCK), pl.ds(b * BLOCK, BLOCK)
        ]
    start = len(blocks) * BLOCK
    packed[start:, :] = jnp.zeros((packed.shape[0] - start, BLOCK), jnp.float32)
    for c in range(order // BLOCK):
        packed[pl.ds(start + c, 1), :] = solved[:, c * BLOCK : (c + 1) * BLOCK]
    size = half_ref.shape[0]
    half_ref[...] = packed[pl.ds(pl.multiple_of(place_ref[1] % 2 * size, 8), size), :]


def last_factor(place, upper, inverse, projected, first, after, cost):
    order = upper.shape[0]
    size = lower_half(order)
    return pl.pallas_call(
        functools.partial(last_factor_kernel, first),
        out_shape=(
            square(order),
            square(order),
            row(order),
            jax.ShapeDtypeStruct((size, BLOCK), jnp.float32),
        ),
        in_specs=[SMEM] + [VMEM] * 3 + [ANY],
        out_specs=[VMEM] * 4,
        input_output_aliases={1: 0, 2: 1},
        scratch_shapes=[pltpu.VMEM((2 * size, BLOCK), jnp.float32)],
        compiler_params=pltpu.CompilerParams(vmem_limit_bytes=LIMIT),
        cost_estimate=cost,
    )(place, upper, inverse, projected, after)


def three_products(left, right):
    def parts(value):
        high = value.astype(jnp.bfloat16)
        return high, (value - high.astype(jnp.float32)).astype(jnp.bfloat16)

    def dot(a, b):
        return lax.dot_general(
            a, b, (((1,), (1,)), ((), ())), preferred_element_type=jnp.float32
        )

    (high, low), (other_high, other_low) = parts(left), parts(right)
    return dot(high, other_high) + (dot(high, other_low) + dot(low, other_high))


def finish_kernel(place_ref, upper_ref, solved_ref, half_ref, other_ref, *refs):
    pieces = refs[:GROUP]
    out_ref, multipliers_ref, cross, packed, inverse = refs[GROUP:]
    order = upper_ref.shape[0]
    part = BLOCK // GROUP

    @pl.when(place_ref[0] == 0)
    def _():
        out_ref[...] = upper_ref[...]
        keep_upper(out_ref)
        multipliers_ref[...] = solved_ref[...]

    @pl.when(place_ref[0] != 0)
    def _():
        size = half_ref.shape[0]
        core = place_ref[1] % 2
        packed[pl.ds(pl.multiple_of(core * size, 8), size), :] = half_ref[...]
        packed[pl.ds(pl.multiple_of((1 - core) * size, 8), size), :] = other_ref[...]
        blocks = lower_blocks(order)
        for index, (a, b) in enumerate(blocks):
            inverse[pl.ds(a * BLOCK, BLOCK), pl.ds(b * BLOCK, BLOCK)] = packed[
                pl.ds(index * BLOCK, BLOCK), :
            ]
        for c in range(order // BLOCK):
            multipliers_ref[:, pl.ds(c * BLOCK, BLOCK)] = packed[
                pl.ds(len(blocks) * BLOCK + c, 1), :
            ]
        for mask in range(GROUP):
            quarter = place_ref[1] ^ mask
            for b in range(order // BLOCK):
                start = pl.multiple_of(BLOCK * b + part * quarter, part)
                cross[pl.ds(start, part), :] = pieces[mask][pl.ds(part * b, part), :]
        for a in range(order // BLOCK):
            rows, depth = pl.ds(a * BLOCK, BLOCK), (a + 1) * BLOCK
            out_ref[rows, :] = three_products(
                inverse[rows, pl.ds(0, depth)], cross[:, pl.ds(0, depth)]
            )


def finish(place, upper, solved, half, other, pieces):
    order = upper.shape[0]
    return pl.pallas_call(
        finish_kernel,
        out_shape=(square(order), row(order)),
        in_specs=[SMEM] + [VMEM] * (4 + GROUP),
        out_specs=[VMEM] * 2,
        scratch_shapes=[
            pltpu.VMEM((order, order), jnp.float32),
            pltpu.VMEM((2 * lower_half(order), BLOCK), jnp.float32),
            pltpu.VMEM((order, order), jnp.float32),
        ],
        compiler_params=pltpu.CompilerParams(vmem_limit_bytes=LIMIT),
        cost_estimate=BRIEF,
    )(place, upper, solved, half, other, *pieces)


def shards(sens_base, design_field, gradient, tile_index, type_codes):
    cells, order = sens_base.shape
    rows_here, width = design_field.shape
    side = lax.axis_index("cols")
    quarter = lax.axis_index("rows") % GROUP
    tiles = width // TILE
    first_tile = lax.axis_index("rows") * rows_here // TILE * tiles
    place = jnp.stack([side, quarter, 3 * first_tile]).astype(jnp.int32)
    tile_row, type_row = tile_index[None, :], type_codes[None, :]

    half, split = cells // 2, order - BLOCK
    middle = half // 2
    rows = [
        [(0, middle, 0, split, True)],
        [(middle, half, 0, split, False)],
        [(0, half, split, order, True)],
    ]
    wide = WIDE_LIMIT + 6 * 2**20
    sent = [
        send_parts(place, sens_base, tile_row, type_row, pieces, limit)[0]
        for pieces, limit in zip(rows, (wide, wide, TAIL_LIMIT))
    ]
    lead, rest, tail = [swap(part, "cols", 1) for part in sent]
    received = [[lead, rest], [tail]]

    count = lax.axis_size("rows")
    north = lax.ppermute(design_field[-1:], "rows", [(i, i + 1) for i in range(count - 1)])
    south = lax.ppermute(design_field[:1], "rows", [(i + 1, i) for i in range(count - 1)])
    feature = features(design_field, north, south)
    jac, *packed = own_part(place, sens_base, feature, tile_row, type_row, gradient)
    pieces = rows_gather(groups_sum(group_sum(packed)))

    def stage(index, *after):
        return cross_part(place, received[index], jac, feature, *after)

    upper, inverse, projected = first_factor(place, pieces, order, 1, pieces[0])
    first = stage(0, upper)
    shares = group_swaps(first)
    upper, inverse = more_factor(upper, inverse, 1, 2, first[0], LONG)
    held = add(shares, inverse)
    shares = [held, swap(held, "rows", GROUP)]
    upper, inverse = more_factor(upper, inverse, 2, 3, held, LONG)
    middle = add(shares, inverse)
    far = range(2 * GROUP, count, 2 * GROUP)
    far_shares = [middle] + [swap(middle, "rows", mask) for mask in far]
    last = stage(1, middle)
    shares = group_swaps(last)
    upper, _, solved, half = last_factor(place, upper, inverse, projected, 3, last[0], LONG)
    held_last, half = add_pass(shares, half, far_shares[-1])
    shares = [held_last] + [swap(held_last, "rows", mask) for mask in range(GROUP, count, GROUP)]
    half = lax.ppermute(half, "cols", [(0, 1)])
    totals = stacked(far_shares, shares, half)
    others = lax.ppermute(totals, "cols", [(0, 1)])

    cross = joined(totals, others)
    r_panels, multipliers = finish(
        place, upper, solved, half, swap(half, "rows", 1), near_gather(cross)
    )
    return (r_panels, multipliers[0])


def shards_general(sens_base, design_field, gradient, tile_index, type_codes):
    rows_here = design_field.shape[0]
    grid_width = design_field.shape[1]
    cols_here = sens_base.shape[1]
    factored = 2 * PW
    padded = padded_2(design_field, (("rows", 0),), 1)
    padded = jnp.pad(padded, ((0, 0), (1, 1)))
    north_cells = padded[:-2, 1:-1]
    south_cells = padded[2:, 1:-1]
    west_cells = padded[1:-1, :-2]
    east_cells = padded[1:-1, 2:]
    laplace = 4.0 * design_field - (north_cells + south_cells + west_cells + east_cells)
    slope_x = 0.5 * (east_cells - west_cells)
    slope_y = 0.5 * (south_cells - north_cells)
    stencils = jnp.stack([laplace, slope_x, slope_y]).reshape(3, -1)
    row_glob = lax.axis_index("rows") * rows_here + jnp.arange(rows_here, dtype=jnp.int32)
    col_ids = jnp.arange(grid_width, dtype=jnp.int32) // TILE
    cell_tile = ((row_glob // TILE)[:, None] * (grid_width // TILE) + col_ids[None, :]).reshape(-1)
    local_jac = assemble(sens_base, tile_index, type_codes, stencils, cell_tile)
    grad_flat = gradient.reshape(-1)
    row_major = lax.all_to_all(local_jac, "cols", split_axis=0, concat_axis=1, tiled=True)
    row_piece = row_major.shape[0]
    grad_part = lax.dynamic_slice_in_dim(
        grad_flat, lax.axis_index("cols") * row_piece, row_piece, 0
    )
    leading = row_major[:, :factored]
    gram_block = lax.dot_general(
        leading, row_major, (((0,), (0,)), ((), ())), preferred_element_type=jnp.float32
    )
    projected = jnp.dot(grad_part, leading, preferred_element_type=jnp.float32)
    gram_block, projected = lax.psum((gram_block, projected), ("rows", "cols"))
    gram_head = gram_block[:, :factored]
    gram_own = lax.dynamic_slice_in_dim(
        gram_block, lax.axis_index("cols") * cols_here, cols_here, 1
    )
    _, inverse, multipliers = factor(gram_head, projected[None, :])
    r_panels = matmul(inverse, gram_own)
    return (r_panels, multipliers[0])


def solution(mesh):
    placed = (P("rows", "cols"), P("rows", None), P("rows", None), P("cols"), P("cols"))
    pairs = mesh.shape["cols"] == 2 and mesh.shape["rows"] in (8, 16, 32, 64)
    return jax.shard_map(
        shards if pairs else shards_general,
        mesh=mesh,
        in_specs=placed,
        out_specs=(P(None, "cols"), P()),
        check_vma=False,
    )
```

```python
import functools

import jax
import jax.numpy as jnp
from jax import lax
from jax.experimental import pallas as pl
from jax.experimental.pallas import tpu as pltpu
from jax.sharding import PartitionSpec as P

TILE = 128
PW = 256
BLOCK = 128
FEATURES = 80
KEY_ROWS = 16
STEP_ROWS = 1024
COPY_ROWS = 256
OWN_CUTS = 4
GROUP = 4
HIGHEST = lax.Precision.HIGHEST
VMEM = pl.BlockSpec(memory_space=pltpu.VMEM)
SMEM = pl.BlockSpec(memory_space=pltpu.SMEM)
LIMIT = 12 * 2**20
WIDE_LIMIT = 48 * 2**20
TAIL_LIMIT = 36 * 2**20
ANY = pl.BlockSpec(memory_space=pl.ANY)
LONG = pl.CostEstimate(flops=8 * 10**9, bytes_accessed=1000, transcendentals=0)
BRIEF = pl.CostEstimate(flops=1000, bytes_accessed=1000, transcendentals=0)


def padded_2(cells, sides, width):
    for axis, dim in sides:
        count = lax.axis_size(axis)
        ends = count - 1
        head = lax.slice_in_dim(cells, 0, width, axis=dim)
        tail = lax.slice_in_dim(cells, cells.shape[dim] - width, cells.shape[dim], axis=dim)
        cells = jnp.concatenate(
            [
                lax.ppermute(tail, axis, [(i, (i + 1) % count) for i in range(ends)]),
                cells,
                lax.ppermute(head, axis, [((i + 1) % count, i) for i in range(ends)]),
            ],
            axis=dim,
        )
    return cells


def assemble(base_cols, tile_cols, type_cols, stencils, cell_tile):
    kinds_all = jnp.arange(3, dtype=jnp.int32)
    chooser = (type_cols[None, :] == kinds_all[:, None]).astype(jnp.float32)
    picked = lax.dot_general(
        stencils,
        chooser,
        (((0,), (0,)), ((), ())),
        precision=lax.Precision.HIGHEST,
        preferred_element_type=jnp.float32,
    )
    inside = cell_tile[:, None] == tile_cols[None, :]
    total = base_cols.astype(jnp.float32) + jnp.where(inside, picked / TILE, 0.0)
    return total.astype(jnp.bfloat16)


def matmul(left, right):
    return jnp.dot(left, right, precision=HIGHEST, preferred_element_type=jnp.float32)


def tree_sum(terms):
    while len(terms) > 1:
        terms = [a + b for a, b in zip(terms[::2], terms[1::2])] + terms[len(terms) // 2 * 2 :]
    return terms[0]


def lane(part, index):
    return jnp.broadcast_to(part[:, index : index + 1], part.shape)


def sublane(part, index):
    return jnp.broadcast_to(part[index : index + 1, :], part.shape)


def diagonal_inverse(block):
    groups = BLOCK // 8
    shape = (8, BLOCK)
    lanes = lax.broadcasted_iota(jnp.int32, shape, 1)
    subs = lax.broadcasted_iota(jnp.int32, shape, 0)
    parts = [block[8 * g : 8 * g + 8, :] for g in range(groups)]
    whole = []
    for p in range(groups):
        part, first = parts[p], 8 * p
        cols = [lane(part, first + k) for k in range(8)]
        inv = [None] * 8
        low = [jnp.zeros(shape, jnp.float32) for _ in range(8)]
        scale = jnp.ones(shape, jnp.float32)
        for j in range(8):
            here = subs == j
            root = lax.rsqrt(sublane(cols[j], j))
            ratio = root * root
            scale = jnp.where(here, root, scale)
            for k in range(j):
                low[k] = jnp.where(here, inv[k], low[k])
            low[j] = jnp.where(here, 1.0, low[j])
            column = cols[j]
            for part_list, chosen in ((cols, range(j + 1, 8)), (inv, range(j))):
                for k in chosen:
                    row = sublane(part_list[k], j)
                    share = jnp.where(here, -row, column * row)
                    part_list[k] = jnp.where(here, 0.0, part_list[k]) - share * ratio
            inv[j] = jnp.where(here, 1.0, -column) * ratio
        inside = (lanes >= first) & (lanes < first + 8)
        unit = jnp.where(lanes - first == subs, 1.0, 0.0)
        rows = jnp.where(inside, unit, part)
        spread = [sublane(rows, k) for k in range(8)]
        solved = tree_sum([low[k] * spread[k] for k in range(8)]) * scale
        whole.append(jnp.where(lanes < first + 8, solved, 0.0))
        if p + 1 < groups:
            step = tree_sum([inv[k] * spread[k] for k in range(8)])
            step = [sublane(step, k) for k in range(8)]
            for g in range(p + 1, groups):
                taken = tree_sum([lane(parts[g], first + k) * step[k] for k in range(8)])
                parts[g] = jnp.where(inside, 0.0, parts[g]) - taken
    return jnp.concatenate(whole, axis=0)


def factor_steps(upper_ref, inverse_ref, first, last):
    order = upper_ref.shape[0]
    for step in range(first, last):
        mine, done = pl.ds(step * BLOCK, BLOCK), pl.ds(0, (step + 1) * BLOCK)
        ahead = pl.ds(step * BLOCK, order - step * BLOCK)
        small = diagonal_inverse(upper_ref[mine, mine])
        panel = matmul(small, upper_ref[mine, ahead])
        upper_ref[mine, ahead] = panel
        solved = matmul(small, inverse_ref[mine, done])
        inverse_ref[mine, done] = solved
        for later in range(step + 1, order // BLOCK):
            theirs = pl.ds(later * BLOCK, BLOCK)
            left = (later - step) * BLOCK
            factor = panel[:, left : left + BLOCK]

            def product(right):
                return lax.dot_general(
                    factor,
                    right,
                    (((0,), (0,)), ((), ())),
                    precision=HIGHEST,
                    preferred_element_type=jnp.float32,
                )

            upper_ref[theirs, pl.ds(later * BLOCK, order - later * BLOCK)] -= product(
                panel[:, left:]
            )
            inverse_ref[theirs, done] -= product(solved)


def start_inverse(inverse_ref):
    rows = lax.broadcasted_iota(jnp.int32, inverse_ref.shape, 0)
    cols = lax.broadcasted_iota(jnp.int32, inverse_ref.shape, 1)
    inverse_ref[...] = jnp.where(rows == cols, 1.0, 0.0)


def keep_upper(upper_ref):
    rows = lax.broadcasted_iota(jnp.int32, upper_ref.shape, 0)
    cols = lax.broadcasted_iota(jnp.int32, upper_ref.shape, 1)
    upper_ref[...] = jnp.where(rows <= cols, upper_ref[...], 0.0)


def solve_twice(inverse_ref, projected_ref):
    half = jnp.sum(inverse_ref[...] * projected_ref[...], axis=1, keepdims=True)
    return jnp.sum(inverse_ref[...] * half, axis=0, keepdims=True)


def factor_kernel(gram_ref, projected_ref, upper_ref, inverse_ref, multipliers_ref):
    upper_ref[...] = gram_ref[...]
    start_inverse(inverse_ref)
    factor_steps(upper_ref, inverse_ref, 0, upper_ref.shape[0] // BLOCK)
    keep_upper(upper_ref)
    multipliers_ref[...] = solve_twice(inverse_ref, projected_ref)


def factor(gram, projected):
    order = gram.shape[0]
    return pl.pallas_call(
        factor_kernel,
        out_shape=(
            jax.ShapeDtypeStruct((order, order), jnp.float32),
            jax.ShapeDtypeStruct((order, order), jnp.float32),
            jax.ShapeDtypeStruct((1, order), jnp.float32),
        ),
        in_specs=[pl.BlockSpec(memory_space=pltpu.VMEM)] * 2,
        out_specs=[pl.BlockSpec(memory_space=pltpu.VMEM)] * 3,
        compiler_params=pltpu.CompilerParams(vmem_limit_bytes=LIMIT),
        cost_estimate=pl.CostEstimate(
            flops=6 * order**3, bytes_accessed=12 * order**2, transcendentals=0
        ),
    )(gram, projected)


def features_kernel(field_ref, north_ref, south_ref, out_ref):
    field = field_ref[...]
    rows, width = field.shape
    lanes = lax.broadcasted_iota(jnp.int32, field.shape, 1)
    north = jnp.concatenate([north_ref[...], field[:-1]], axis=0)
    south = jnp.concatenate([field[1:], south_ref[...]], axis=0)
    west = jnp.where(lanes == 0, 0.0, pltpu.roll(field, 1, 1))
    east = jnp.where(lanes == width - 1, 0.0, pltpu.roll(field, width - 1, 1))
    laplace = 4.0 * field - (north + south + west + east)
    slope_x = 0.5 * (east - west)
    slope_y = 0.5 * (south - north)
    parts = []
    for stencil in (laplace, slope_x, slope_y):
        rest = stencil / TILE
        for _ in range(3):
            part = rest.astype(jnp.bfloat16).astype(jnp.float32)
            parts.append(part)
            rest = rest - part
    tiles = width // TILE
    shape = (FEATURES, width)
    owner = lax.broadcasted_iota(jnp.int32, shape, 0) // len(parts)
    tile = lax.broadcasted_iota(jnp.int32, shape, 1) // TILE
    blank = jnp.zeros((FEATURES - tiles * len(parts), width), jnp.float32)
    for row in range(rows):
        block = jnp.concatenate([part[row : row + 1] for part in parts], axis=0)
        whole = jnp.concatenate([block] * tiles + [blank], axis=0)
        out_ref[row] = jnp.where(owner == tile, whole, 0.0).astype(jnp.bfloat16)


def features(field, north, south):
    rows, width = field.shape
    return pl.pallas_call(
        features_kernel,
        out_shape=jax.ShapeDtypeStruct((rows, FEATURES, width), jnp.bfloat16),
        in_specs=[VMEM] * 3,
        out_specs=VMEM,
        compiler_params=pltpu.CompilerParams(vmem_limit_bytes=LIMIT),
        cost_estimate=BRIEF,
    )(field, north, south)


def assembled(base, feature, key, first):
    rows = lax.broadcasted_iota(jnp.int32, (FEATURES, key.shape[1]), 0) // 3 + first
    chooser = jnp.where(rows.astype(jnp.float32) == key, 1.0, 0.0).astype(jnp.bfloat16)
    added = lax.dot_general(
        feature, chooser, (((0,), (0,)), ((), ())), preferred_element_type=jnp.float32
    )
    return (base.astype(jnp.float32) + added).astype(jnp.bfloat16)


def transposed_dot(left, right):
    return lax.dot_general(
        left, right, (((0,), (0,)), ((), ())), preferred_element_type=jnp.float32
    )


def strict_blocks(order):
    count = order // BLOCK
    return [(a, b) for a in range(count) for b in range(a + 1, count)]


def packed_rows(order):
    count = order // BLOCK
    used = (len(strict_blocks(order)) + count // 2) * BLOCK + count // 2 + count
    return -(-used // (8 * GROUP)) * 8 * GROUP


def triangles():
    rows = lax.broadcasted_iota(jnp.int32, (BLOCK, BLOCK), 0)
    cols = lax.broadcasted_iota(jnp.int32, (BLOCK, BLOCK), 1)
    return rows < cols, rows == cols


def at(index):
    return pl.ds(index * BLOCK, BLOCK)


def pack_gram(packed, gram, projected):
    order = gram.shape[0]
    packed[...] = jnp.zeros_like(packed)
    blocks = strict_blocks(order)
    for index, (a, b) in enumerate(blocks):
        packed[at(index), :] = gram[at(a), at(b)]
    above, diagonal = triangles()
    pairs = order // BLOCK // 2
    row = (len(blocks) + pairs) * BLOCK
    for p in range(pairs):
        second = gram[at(2 * p + 1), at(2 * p + 1)]
        packed[at(len(blocks) + p), :] = jnp.where(
            above | diagonal, gram[at(2 * p), at(2 * p)], second
        )
        packed[pl.ds(row + p, 1), :] = jnp.sum(
            jnp.where(diagonal, second, 0.0), axis=0, keepdims=True
        )
    for c in range(order // BLOCK):
        packed[pl.ds(row + pairs + c, 1), :] = projected[:, at(c)]


def unpack_gram(packed, upper_ref, projected_ref):
    order = upper_ref.shape[0]
    upper_ref[...] = jnp.zeros_like(upper_ref)
    blocks = strict_blocks(order)
    for index, (a, b) in enumerate(blocks):
        upper_ref[at(a), at(b)] = packed[at(index), :]
    above, diagonal = triangles()
    pairs = order // BLOCK // 2
    row = (len(blocks) + pairs) * BLOCK
    for p in range(pairs):
        both = packed[at(len(blocks) + p), :]
        turned = both.T
        upper_ref[at(2 * p), at(2 * p)] = jnp.where(above | diagonal, both, turned)
        upper_ref[at(2 * p + 1), at(2 * p + 1)] = jnp.where(
            diagonal, packed[pl.ds(row + p, 1), :], jnp.where(above, turned, both)
        )
    for c in range(order // BLOCK):
        projected_ref[:, at(c)] = packed[pl.ds(row + pairs + c, 1), :]


def own_kernel(
    place_ref, *refs
):
    bases = refs[:OWN_CUTS]
    feature_ref, tile_ref, type_ref, grad_ref, jac_ref = refs[OWN_CUTS : OWN_CUTS + 5]
    outs = refs[OWN_CUTS + 5 : OWN_CUTS + 5 + GROUP]
    gram, projected, packed = refs[OWN_CUTS + 5 + GROUP :]
    step = pl.program_id(0)
    half = pl.num_programs(0) // 2
    order = gram.shape[0]
    base = jnp.concatenate([ref[...] for ref in bases], axis=0)
    key = (tile_ref[...] * 3 + type_ref[...]).astype(jnp.float32)
    jac = assembled(base, feature_ref[0], key, place_ref[2])

    @pl.when(step // half == place_ref[0])
    def _():
        jac_ref[...] = jac

    @pl.when(step == 0)
    def _():
        gram[...] = jnp.zeros_like(gram)
        projected[...] = jnp.zeros_like(projected)

    middle = order // 2
    gram[:middle, :] += transposed_dot(jac[:, :middle], jac)
    gram[middle:, middle:] += transposed_dot(jac[:, middle:], jac[:, middle:])
    projected[...] += jnp.dot(grad_ref[0], jac, preferred_element_type=jnp.float32)

    @pl.when(step == pl.num_programs(0) - 1)
    def _():
        pack_gram(packed, gram, projected)
        size = outs[0].shape[0]
        for mask in range(GROUP):
            start = pl.multiple_of((place_ref[1] ^ mask) * size, 8)
            outs[mask][...] = packed[pl.ds(start, size), :]


def cut_index(cut, i, place):
    return (OWN_CUTS * i + cut, 0)


def own_part(place, base, feature, tile_row, type_row, gradient):
    cells, order = base.shape
    rows, width = gradient.shape
    half = rows // 2
    size = packed_rows(order) // GROUP
    return pl.pallas_call(
        own_kernel,
        grid_spec=pltpu.PrefetchScalarGridSpec(
            num_scalar_prefetch=1,
            grid=(rows,),
            in_specs=[
                pl.BlockSpec((width // OWN_CUTS, order), functools.partial(cut_index, k))
                for k in range(OWN_CUTS)
            ]
            + [
                pl.BlockSpec((1, FEATURES, width), lambda i, s: (i, 0, 0)),
                pl.BlockSpec((1, order), lambda i, s: (0, 0)),
                pl.BlockSpec((1, order), lambda i, s: (0, 0)),
                pl.BlockSpec((1, 1, width), lambda i, s: (i, 0, 0)),
            ],
            out_specs=[
                pl.BlockSpec(
                    (width, order), lambda i, s: (jnp.clip(i - s[0] * half, 0, half - 1), 0)
                )
            ]
            + [pl.BlockSpec((size, BLOCK), lambda i, s: (0, 0))] * GROUP,
            scratch_shapes=[
                pltpu.VMEM((order, order), jnp.float32),
                pltpu.VMEM((1, order), jnp.float32),
                pltpu.VMEM((GROUP * size, BLOCK), jnp.float32),
            ],
        ),
        out_shape=[jax.ShapeDtypeStruct((cells // 2, order), jnp.bfloat16)]
        + [jax.ShapeDtypeStruct((size, BLOCK), jnp.float32)] * GROUP,
        compiler_params=pltpu.CompilerParams(vmem_limit_bytes=WIDE_LIMIT),
        cost_estimate=BRIEF,
    )(place, *[base] * OWN_CUTS, feature, tile_row, type_row, gradient.reshape(rows, 1, width))


def send_kernel(pieces, place_ref, base_ref, tile_ref, type_ref, *refs):
    outs, (held, tiles, types, sems) = refs[-4 - len(pieces) : -4], refs[-4:]
    half = base_ref.shape[0] // 2
    low = min(piece[0] for piece in pieces)
    first = (1 - place_ref[0]) * half + low
    chunks = held.shape[0] // COPY_ROWS
    copies = [
        pltpu.make_async_copy(
            base_ref.at[pl.ds(pl.multiple_of(first + k * COPY_ROWS, COPY_ROWS), COPY_ROWS), :],
            held.at[pl.ds(k * COPY_ROWS, COPY_ROWS), :],
            sems.at[k],
        )
        for k in range(chunks)
    ]
    copies.append(pltpu.make_async_copy(tile_ref, tiles, sems.at[chunks]))
    copies.append(pltpu.make_async_copy(type_ref, types, sems.at[chunks + 1]))
    for copy in copies:
        copy.start()
    for k in range(chunks):
        copies[k].wait()
        for (top, end, left, right, _), out in zip(pieces, outs):
            row = low + k * COPY_ROWS
            if top <= row < end:
                out[pl.ds(row - top, COPY_ROWS), :] = held[
                    pl.ds(k * COPY_ROWS, COPY_ROWS), left:right
                ]
    copies[chunks].wait()
    copies[chunks + 1].wait()
    for (top, end, left, right, keyed), out in zip(pieces, outs):
        if keyed:
            key = (tiles[:, left:right] * 3 + types[:, left:right]).astype(jnp.float32)
            key = jnp.broadcast_to(key, (KEY_ROWS, right - left))
            out[pl.ds(end - top, KEY_ROWS), :] = key.astype(jnp.bfloat16)


def send_parts(place, base, tile_row, type_row, pieces, limit):
    order = base.shape[1]
    span = max(piece[1] for piece in pieces) - min(piece[0] for piece in pieces)
    return pl.pallas_call(
        functools.partial(send_kernel, tuple(pieces)),
        in_specs=[SMEM, ANY, ANY, ANY],
        out_specs=[VMEM] * len(pieces),
        out_shape=[
            jax.ShapeDtypeStruct((end - top + KEY_ROWS * keyed, right - left), base.dtype)
            for top, end, left, right, keyed in pieces
        ],
        scratch_shapes=[
            pltpu.VMEM((span, order), base.dtype),
            pltpu.VMEM((1, order), jnp.int32),
            pltpu.VMEM((1, order), jnp.int32),
            pltpu.SemaphoreType.DMA((span // COPY_ROWS + 2,)),
        ],
        compiler_params=pltpu.CompilerParams(vmem_limit_bytes=limit),
        cost_estimate=BRIEF,
    )(place, base, tile_row, type_row)


def cross_kernel(pieces, place_ref, jac_ref, feature_ref, *refs):
    received = refs[:pieces]
    outs = refs[-2 - GROUP : -2]
    total, out_ref = refs[-2:]
    cells, width = jac_ref.shape[0], feature_ref.shape[2]
    cuts = width // STEP_ROWS
    first = place_ref[0] * (cells // width)
    keyed = received[0].shape[0] - KEY_ROWS
    key = received[0][pl.ds(keyed, KEY_ROWS), :][0:1, :].astype(jnp.float32)
    total[...] = jnp.zeros_like(total)
    done = 0
    for piece in received:
        for step in range(piece.shape[0] // STEP_ROWS):
            lanes = pl.ds(done % cuts * STEP_ROWS, STEP_ROWS)
            feature = feature_ref[first + done // cuts, :, lanes]
            other = assembled(piece[pl.ds(step * STEP_ROWS, STEP_ROWS), :], feature, key, place_ref[2])
            total[...] += transposed_dot(other, jac_ref[pl.ds(done * STEP_ROWS, STEP_ROWS), :])
            done += 1

    count = total.shape[1] // BLOCK
    part = BLOCK // GROUP

    blocks = total.shape[0] // BLOCK

    @pl.when(place_ref[0] == 0)
    def _():
        for k in range(blocks):
            for q in range(GROUP):
                for c in range(count):
                    out_ref[q, pl.ds(BLOCK * k + part * c, part), :] = total[
                        pl.ds(BLOCK * k + part * q, part), pl.ds(BLOCK * c, BLOCK)
                    ]

    @pl.when(place_ref[0] != 0)
    def _():
        for k in range(blocks):
            for c in range(count):
                block = total[pl.ds(BLOCK * k, BLOCK), pl.ds(BLOCK * c, BLOCK)].T
                for q in range(GROUP):
                    out_ref[q, pl.ds(BLOCK * k + part * c, part), :] = block[
                        part * q : part * q + part
                    ]

    for mask in range(GROUP):
        outs[mask][...] = out_ref[place_ref[1] ^ mask]


def cross_part(place, received, jac, feature, *after):
    width_recv, order = received[0].shape[1], jac.shape[1]
    return pl.pallas_call(
        functools.partial(cross_kernel, len(received)),
        in_specs=[SMEM] + [VMEM] * (2 + len(received)) + [ANY] * len(after),
        out_specs=[VMEM] * GROUP,
        out_shape=[jax.ShapeDtypeStruct((width_recv, BLOCK), jnp.float32)] * GROUP,
        scratch_shapes=[
            pltpu.VMEM((width_recv, order), jnp.float32),
            pltpu.VMEM((GROUP, width_recv, BLOCK), jnp.float32),
        ],
        compiler_params=pltpu.CompilerParams(vmem_limit_bytes=LIMIT),
        cost_estimate=BRIEF,
    )(place, jac, feature, *received, *after)


def swap(value, axis, mask):
    count = lax.axis_size(axis)
    return lax.ppermute(value, axis, [(i, i ^ mask) for i in range(count)])


def add_kernel(count, *refs):
    refs[-1][...] = sum(ref[...] for ref in refs[1:count]) + refs[0][...]


def add(values, *after):
    return pl.pallas_call(
        functools.partial(add_kernel, len(values)),
        out_shape=jax.ShapeDtypeStruct(values[0].shape, values[0].dtype),
        in_specs=[VMEM] * len(values) + [ANY] * len(after),
        out_specs=VMEM,
        compiler_params=pltpu.CompilerParams(vmem_limit_bytes=LIMIT),
        cost_estimate=BRIEF,
    )(*values, *after)


def add_pass_kernel(count, *refs):
    values, far = refs[:count], refs[count:-4]
    passed_ref, out_ref, far_ref, copy_ref = refs[-4:]
    out_ref[...] = sum(ref[...] for ref in values[1:]) + values[0][...]
    far_ref[...] = sum(ref[...] for ref in far[1:]) + far[0][...]
    copy_ref[...] = passed_ref[...]


def add_pass(values, far, passed):
    return pl.pallas_call(
        functools.partial(add_pass_kernel, len(values)),
        out_shape=[jax.ShapeDtypeStruct(v.shape, v.dtype) for v in (values[0], far[0], passed)],
        in_specs=[VMEM] * (len(values) + len(far) + 1),
        out_specs=[VMEM] * 3,
        compiler_params=pltpu.CompilerParams(vmem_limit_bytes=LIMIT),
        cost_estimate=BRIEF,
    )(*values, *far, passed)


def joined_kernel(first, last, other_first, other_last, out_ref):
    part = BLOCK // GROUP
    blocks = out_ref.shape[1] // BLOCK

    def piece(head, end, block, c):
        ref, block = (head, block) if block + 1 < blocks else (end, 0)
        return ref[pl.ds(BLOCK * block + part * c, part), :]

    for a in range(blocks):
        for b in range(blocks):
            out_ref[pl.ds(part * b, part), at(a)] = piece(first, last, a, b) + piece(
                other_first, other_last, b, a
            )


def joined(own, other):
    order = sum(value.shape[0] for value in own)
    return pl.pallas_call(
        joined_kernel,
        out_shape=jax.ShapeDtypeStruct((order // GROUP, order), jnp.float32),
        in_specs=[VMEM] * 4,
        out_specs=VMEM,
        compiler_params=pltpu.CompilerParams(vmem_limit_bytes=LIMIT),
        cost_estimate=BRIEF,
    )(*own, *other)


def group_swaps(parts):
    return [parts[0]] + [swap(parts[mask], "rows", mask) for mask in range(1, GROUP)]


def group_sum(parts):
    got = group_swaps(parts)
    return got[0] + got[1] + got[2] + got[3]


def groups_sum(held):
    masks = range(GROUP, lax.axis_size("rows"), GROUP)
    return held + sum(swap(held, "rows", mask) for mask in masks)


def doubled(held, masks):
    for mask in masks:
        held = held + swap(held, "rows", mask)
    return held


def rows_gather(own):
    return [own] + [swap(own, "rows", mask) for mask in range(1, GROUP)]


def near_gather(own):
    near, far = swap(own, "rows", 1), swap(own, "rows", 2)
    return [own, near, far, swap(far, "rows", 1)]


def first_factor_kernel(last, place_ref, *refs):
    pieces = refs[:GROUP]
    upper_ref, inverse_ref, projected_ref, whole = refs[GROUP + 1 :]
    size = pieces[0].shape[0]
    for mask in range(GROUP):
        start = pl.multiple_of((place_ref[1] ^ mask) * size, 8)
        whole[pl.ds(start, size), :] = pieces[mask][...]
    unpack_gram(whole, upper_ref, projected_ref)
    start_inverse(inverse_ref)
    factor_steps(upper_ref, inverse_ref, 0, last)


def square(order):
    return jax.ShapeDtypeStruct((order, order), jnp.float32)


def row(order):
    return jax.ShapeDtypeStruct((1, order), jnp.float32)


def first_factor(place, pieces, order, last, after):
    return pl.pallas_call(
        functools.partial(first_factor_kernel, last),
        out_shape=(square(order), square(order), row(order)),
        in_specs=[SMEM] + [VMEM] * GROUP + [ANY],
        out_specs=[VMEM] * 3,
        scratch_shapes=[pltpu.VMEM((packed_rows(order), BLOCK), jnp.float32)],
        compiler_params=pltpu.CompilerParams(vmem_limit_bytes=LIMIT),
        cost_estimate=BRIEF,
    )(place, *pieces, after)


def more_factor_kernel(first, last, upper_in, inverse_in, _, upper_ref, inverse_ref):
    del upper_in, inverse_in
    factor_steps(upper_ref, inverse_ref, first, last)


def more_factor(upper, inverse, first, last, after, cost):
    order = upper.shape[0]
    return pl.pallas_call(
        functools.partial(more_factor_kernel, first, last),
        out_shape=[square(order)] * 2,
        in_specs=[VMEM] * 2 + [ANY],
        out_specs=[VMEM] * 2,
        input_output_aliases={0: 0, 1: 1},
        compiler_params=pltpu.CompilerParams(vmem_limit_bytes=LIMIT),
        cost_estimate=cost,
    )(upper, inverse, after)


def lower_blocks(order):
    return [(a, b) for a in range(order // BLOCK) for b in range(a + 1)]


def lower_half(order):
    rows = len(lower_blocks(order)) * BLOCK + order // BLOCK
    return -(-rows // 16) * 8


def last_factor_kernel(
    first, place_ref, upper_in, inverse_in, projected, _, upper_ref, inverse, out_ref, half_ref, packed
):
    del upper_in, inverse_in
    order = upper_ref.shape[0]
    factor_steps(upper_ref, inverse, first, order // BLOCK)
    solved = solve_twice(inverse, projected)
    out_ref[...] = solved
    blocks = lower_blocks(order)
    for index, (a, b) in enumerate(blocks):
        packed[pl.ds(index * BLOCK, BLOCK), :] = inverse[
            pl.ds(a * BLOCK, BLOCK), pl.ds(b * BLOCK, BLOCK)
        ]
    start = len(blocks) * BLOCK
    packed[start:, :] = jnp.zeros((packed.shape[0] - start, BLOCK), jnp.float32)
    for c in range(order // BLOCK):
        packed[pl.ds(start + c, 1), :] = solved[:, c * BLOCK : (c + 1) * BLOCK]
    size = half_ref.shape[0]
    half_ref[...] = packed[pl.ds(pl.multiple_of(place_ref[1] % 2 * size, 8), size), :]


def last_factor(place, upper, inverse, projected, first, after, cost):
    order = upper.shape[0]
    size = lower_half(order)
    return pl.pallas_call(
        functools.partial(last_factor_kernel, first),
        out_shape=(
            square(order),
            square(order),
            row(order),
            jax.ShapeDtypeStruct((size, BLOCK), jnp.float32),
        ),
        in_specs=[SMEM] + [VMEM] * 3 + [ANY],
        out_specs=[VMEM] * 4,
        input_output_aliases={1: 0, 2: 1},
        scratch_shapes=[pltpu.VMEM((2 * size, BLOCK), jnp.float32)],
        compiler_params=pltpu.CompilerParams(vmem_limit_bytes=LIMIT),
        cost_estimate=cost,
    )(place, upper, inverse, projected, after)


def three_products(left, right):
    def parts(value):
        high = value.astype(jnp.bfloat16)
        return high, (value - high.astype(jnp.float32)).astype(jnp.bfloat16)

    def dot(a, b):
        return lax.dot_general(
            a, b, (((1,), (1,)), ((), ())), preferred_element_type=jnp.float32
        )

    (high, low), (other_high, other_low) = parts(left), parts(right)
    return dot(high, other_high) + (dot(high, other_low) + dot(low, other_high))


def finish_kernel(place_ref, upper_ref, solved_ref, half_ref, other_ref, *refs):
    pieces = refs[:GROUP]
    out_ref, multipliers_ref, cross, packed, inverse = refs[GROUP:]
    order = upper_ref.shape[0]
    part = BLOCK // GROUP

    @pl.when(place_ref[0] == 0)
    def _():
        out_ref[...] = upper_ref[...]
        keep_upper(out_ref)
        multipliers_ref[...] = solved_ref[...]

    @pl.when(place_ref[0] != 0)
    def _():
        size = half_ref.shape[0]
        core = place_ref[1] % 2
        packed[pl.ds(pl.multiple_of(core * size, 8), size), :] = half_ref[...]
        packed[pl.ds(pl.multiple_of((1 - core) * size, 8), size), :] = other_ref[...]
        blocks = lower_blocks(order)
        for index, (a, b) in enumerate(blocks):
            inverse[pl.ds(a * BLOCK, BLOCK), pl.ds(b * BLOCK, BLOCK)] = packed[
                pl.ds(index * BLOCK, BLOCK), :
            ]
        for c in range(order // BLOCK):
            multipliers_ref[:, pl.ds(c * BLOCK, BLOCK)] = packed[
                pl.ds(len(blocks) * BLOCK + c, 1), :
            ]
        for mask in range(GROUP):
            quarter = place_ref[1] ^ mask
            for b in range(order // BLOCK):
                start = pl.multiple_of(BLOCK * b + part * quarter, part)
                cross[pl.ds(start, part), :] = pieces[mask][pl.ds(part * b, part), :]
        for a in range(order // BLOCK):
            rows, depth = pl.ds(a * BLOCK, BLOCK), (a + 1) * BLOCK
            out_ref[rows, :] = three_products(
                inverse[rows, pl.ds(0, depth)], cross[:, pl.ds(0, depth)]
            )


def finish(place, upper, solved, half, other, pieces):
    order = upper.shape[0]
    return pl.pallas_call(
        finish_kernel,
        out_shape=(square(order), row(order)),
        in_specs=[SMEM] + [VMEM] * (4 + GROUP),
        out_specs=[VMEM] * 2,
        scratch_shapes=[
            pltpu.VMEM((order, order), jnp.float32),
            pltpu.VMEM((2 * lower_half(order), BLOCK), jnp.float32),
            pltpu.VMEM((order, order), jnp.float32),
        ],
        compiler_params=pltpu.CompilerParams(vmem_limit_bytes=LIMIT),
        cost_estimate=BRIEF,
    )(place, upper, solved, half, other, *pieces)


def shards(sens_base, design_field, gradient, tile_index, type_codes):
    cells, order = sens_base.shape
    rows_here, width = design_field.shape
    side = lax.axis_index("cols")
    quarter = lax.axis_index("rows") % GROUP
    tiles = width // TILE
    first_tile = lax.axis_index("rows") * rows_here // TILE * tiles
    place = jnp.stack([side, quarter, 3 * first_tile]).astype(jnp.int32)
    tile_row, type_row = tile_index[None, :], type_codes[None, :]

    half, split = cells // 2, order - BLOCK
    middle = half // 2
    rows = [
        [(0, middle, 0, split, True)],
        [(middle, half, 0, split, False)],
        [(0, half, split, order, True)],
    ]
    wide = WIDE_LIMIT + 6 * 2**20
    sent = [
        send_parts(place, sens_base, tile_row, type_row, pieces, limit)[0]
        for pieces, limit in zip(rows, (wide, wide, TAIL_LIMIT))
    ]
    lead, rest, tail = [swap(part, "cols", 1) for part in sent]
    received = [[lead, rest], [tail]]

    count = lax.axis_size("rows")
    north = lax.ppermute(design_field[-1:], "rows", [(i, i + 1) for i in range(count - 1)])
    south = lax.ppermute(design_field[:1], "rows", [(i + 1, i) for i in range(count - 1)])
    feature = features(design_field, north, south)
    jac, *packed = own_part(place, sens_base, feature, tile_row, type_row, gradient)
    pieces = rows_gather(groups_sum(group_sum(packed)))

    def stage(index, *after):
        return cross_part(place, received[index], jac, feature, *after)

    upper, inverse, projected = first_factor(place, pieces, order, 1, pieces[0])
    first = stage(0, upper)
    shares = group_swaps(first)
    upper, inverse = more_factor(upper, inverse, 1, 2, first[0], LONG)
    held = add(shares, inverse)
    shares = [held, swap(held, "rows", GROUP)]
    upper, inverse = more_factor(upper, inverse, 2, 3, held, LONG)
    middle = add(shares, inverse)
    far = range(2 * GROUP, count, 2 * GROUP)
    far_shares = [middle] + [swap(middle, "rows", mask) for mask in far]
    last = stage(1, middle)
    shares = group_swaps(last)
    upper, _, solved, half = last_factor(place, upper, inverse, projected, 3, last[0], LONG)
    held_last, far_sum, half = add_pass(shares, far_shares, half)
    shares = [held_last] + [swap(held_last, "rows", mask) for mask in range(GROUP, count, GROUP)]
    half = lax.ppermute(half, "cols", [(0, 1)])
    totals = [far_sum, add(shares)]
    others = [lax.ppermute(value, "cols", [(0, 1)]) for value in totals]

    cross = joined(totals, others)
    r_panels, multipliers = finish(
        place, upper, solved, half, swap(half, "rows", 1), near_gather(cross)
    )
    return (r_panels, multipliers[0])


def shards_general(sens_base, design_field, gradient, tile_index, type_codes):
    rows_here = design_field.shape[0]
    grid_width = design_field.shape[1]
    cols_here = sens_base.shape[1]
    factored = 2 * PW
    padded = padded_2(design_field, (("rows", 0),), 1)
    padded = jnp.pad(padded, ((0, 0), (1, 1)))
    north_cells = padded[:-2, 1:-1]
    south_cells = padded[2:, 1:-1]
    west_cells = padded[1:-1, :-2]
    east_cells = padded[1:-1, 2:]
    laplace = 4.0 * design_field - (north_cells + south_cells + west_cells + east_cells)
    slope_x = 0.5 * (east_cells - west_cells)
    slope_y = 0.5 * (south_cells - north_cells)
    stencils = jnp.stack([laplace, slope_x, slope_y]).reshape(3, -1)
    row_glob = lax.axis_index("rows") * rows_here + jnp.arange(rows_here, dtype=jnp.int32)
    col_ids = jnp.arange(grid_width, dtype=jnp.int32) // TILE
    cell_tile = ((row_glob // TILE)[:, None] * (grid_width // TILE) + col_ids[None, :]).reshape(-1)
    local_jac = assemble(sens_base, tile_index, type_codes, stencils, cell_tile)
    grad_flat = gradient.reshape(-1)
    row_major = lax.all_to_all(local_jac, "cols", split_axis=0, concat_axis=1, tiled=True)
    row_piece = row_major.shape[0]
    grad_part = lax.dynamic_slice_in_dim(
        grad_flat, lax.axis_index("cols") * row_piece, row_piece, 0
    )
    leading = row_major[:, :factored]
    gram_block = lax.dot_general(
        leading, row_major, (((0,), (0,)), ((), ())), preferred_element_type=jnp.float32
    )
    projected = jnp.dot(grad_part, leading, preferred_element_type=jnp.float32)
    gram_block, projected = lax.psum((gram_block, projected), ("rows", "cols"))
    gram_head = gram_block[:, :factored]
    gram_own = lax.dynamic_slice_in_dim(
        gram_block, lax.axis_index("cols") * cols_here, cols_here, 1
    )
    _, inverse, multipliers = factor(gram_head, projected[None, :])
    r_panels = matmul(inverse, gram_own)
    return (r_panels, multipliers[0])


def solution(mesh):
    placed = (P("rows", "cols"), P("rows", None), P("rows", None), P("cols"), P("cols"))
    pairs = mesh.shape["cols"] == 2 and mesh.shape["rows"] in (8, 16, 32, 64)
    return jax.shard_map(
        shards if pairs else shards_general,
        mesh=mesh,
        in_specs=placed,
        out_specs=(P(None, "cols"), P()),
        check_vma=False,
    )
```
